32 devices in a mesh: dp: 8 (over z, y), tensor: 4 (over x, core).
Axes of the slice: x: 2, y: 2, z: 4, core: 2. Of those that a mesh axis runs over, the one named last changes fastest.
Arguments:
- tokens: bfloat16 [7680, 1024], P('dp'), may hold values from -6 to 6
- kept: int32 [24], replicated, may hold values from 192 to 256, as said below
- teacher: bfloat16 [7680, 1024], P('dp'), may hold values from -6 to 6
- out_grad: bfloat16 [7680, 1024], P('dp'), may hold values from -6 to 6
- ln1_gain: bfloat16 [1024], replicated, may hold values from 0.5 to 1.5
- ln1_bias: bfloat16 [1024], replicated, may hold values from -0.3125 to 0.3125
- w_qkv: bfloat16 [1024, 3, 1024], P(None, None, 'tensor'), may hold values from -0.1875 to 0.1875
- bias_qv: bfloat16 [2, 1024], P(None, 'tensor'), may hold values from -0.3125 to 0.3125
- w_proj: bfloat16 [1024, 1024], P('tensor'), may hold values from -1 to 1
- bias_proj: bfloat16 [1024], replicated, may hold values from -0.625 to 0.625
- ln2_gain: bfloat16 [1024], replicated, may hold values from 0.5 to 1.5
- ln2_bias: bfloat16 [1024], replicated, may hold values from -1.75 to 1.75
- w_fc1: bfloat16 [1024, 4096], P(None, 'tensor'), may hold values from -0.1875 to 0.1875
- bias_fc1: bfloat16 [4096], P('tensor'), may hold values from -0.625 to 0.625
- w_fc2: bfloat16 [4096, 1024], P('tensor'), may hold values from -0.09375 to 0.09375
- bias_fc2: bfloat16 [1024], replicated, may hold values from -0.625 to 0.625
Outputs:
- out: bfloat16 [7680, 1024], P('dp')
- loss: float32 [24], P('dp')
- token_grad: float32 [7680, 1024], P('dp')
- grad_ln1_gain: float32 [1024], replicated
- grad_ln1_bias: float32 [1024], replicated
- grad_w_qkv: float32 [1024, 3, 1024], P('dp', None, 'tensor')
- grad_bias_qv: float32 [2, 1024], P(None, 'tensor')
- grad_w_proj: float32 [1024, 1024], P('tensor', 'dp')
- grad_bias_proj: float32 [1024], replicated
- grad_ln2_gain: float32 [1024], replicated
- grad_ln2_bias: float32 [1024], replicated
- grad_w_fc1: float32 [1024, 4096], P('dp', 'tensor')
- grad_bias_fc1: float32 [4096], P('tensor')
- grad_w_fc2: float32 [4096, 1024], P('tensor', 'dp')
- grad_bias_fc2: float32 [1024], replicated
The draws below stay inside these ranges and needn't reach their ends.
Inputs may be any that keep to these rules, and one draw needn't show every extreme that they name: The valid rows of sequence s are its 64 buffer slots and the next kept[s] slots; the remaining slots are padding.
All inputs are finite; a program needn't handle non-finite values.
Results may differ from the reference program's by a relative error of at most 0.014.
The reference program's roundings to bfloat16 on the way count: a program that leaves them out, or rounds other values in their place, can miss the bound.
Values may be sent and summed in bfloat16 or wider, within the bound.
A program may use at most 128 MiB of HBM per device.

```python
import jax
import jax.numpy as jnp
from jax import lax

D = 1024
H = 16
FF = 4096
BUFFER = 64
KEPT_MAX = 256
KEPT_MIN = 192
SLOTS = 320
SEQS = 24
TOTAL_SLOTS = 7680
N_TENSOR = 4


def draw_kept(key, part):
    spread = KEPT_MAX - KEPT_MIN
    reach = max(spread // 8, 1)
    seq_index = jnp.arange(SEQS, dtype=jnp.int32)
    ramp = KEPT_MIN + spread * seq_index // max(SEQS - 1, 1)
    jitter = jax.random.randint(key, (SEQS,), -reach, reach + 1, dtype=jnp.int32)
    kept_rows = jnp.clip(ramp + jitter, KEPT_MIN, KEPT_MAX).astype(jnp.int32)
    kept_rows = kept_rows.at[0].set(KEPT_MIN).at[SEQS - 1].set(KEPT_MAX)
    return kept_rows


def steps_of(key, extent, shards, least, top_value):
    level, own = 1.0, jax.random.fold_in(key, 6)
    for axis_at, parts in shards:
        draws = jnp.exp(jax.random.uniform(jax.random.fold_in(own, axis_at), (parts,), jnp.float32, least / len(shards), top_value / len(shards)))
        level = level * jnp.repeat(draws, extent[axis_at] // parts).reshape([-1 if axis == axis_at else 1 for axis in range(len(extent))])
    return level


def normal_values(key, shape, scale, limit, split=(), held_as=jnp.bfloat16):
    result = scale * jax.random.normal(key, shape, jnp.float32)
    if split:
        result = result * steps_of(key, shape, split, -0.22, 0.18)
    return jnp.clip(result, -limit, limit).astype(held_as)


def setup_inputs(seed: int = 0) -> dict:
    seeds = jax.random.split(jax.random.key(seed), 17)
    return {
        "tokens": normal_values(seeds[0], (TOTAL_SLOTS, D), 1.0, 6.0, ((0, 8),)),
        "kept": draw_kept(jax.random.fold_in(seeds[16], 71), 0),
        "teacher": normal_values(seeds[2], (TOTAL_SLOTS, D), 1.0, 6.0, ((0, 8),)),
        "out_grad": normal_values(seeds[3], (TOTAL_SLOTS, D), 1.0, 6.0, ((0, 8),)),
        "ln1_gain": jnp.clip(1.0 + 0.1 * jax.random.normal(seeds[4], (D,), jnp.float32), 0.5, 1.5).astype(jnp.bfloat16),
        "ln1_bias": normal_values(seeds[5], (D,), 0.05, 0.3125),
        "w_qkv": normal_values(seeds[6], (D, 3, D), D ** -0.5, 0.1875, ((2, 4),)),
        "bias_qv": normal_values(seeds[7], (2, D), 0.05, 0.3125, ((1, 4),)),
        "w_proj": normal_values(seeds[8], (D, D), (D // 32) ** -0.5, 1.0, ((0, 4),)),
        "bias_proj": normal_values(seeds[9], (D,), 0.1, 0.625),
        "ln2_gain": jnp.clip(1.0 + 0.1 * jax.random.normal(seeds[10], (D,), jnp.float32), 0.5, 1.5).astype(jnp.bfloat16),
        "ln2_bias": normal_values(seeds[11], (D,), 0.3, 1.75),
        "w_fc1": normal_values(seeds[12], (D, FF), D ** -0.5, 0.1875, ((1, 4),)),
        "bias_fc1": normal_values(seeds[13], (FF,), 0.1, 0.625, ((0, 4),)),
        "w_fc2": normal_values(seeds[14], (FF, D), FF ** -0.5, 0.09375, ((0, 4),)),
        "bias_fc2": normal_values(seeds[15], (D,), 0.1, 0.625),
    }


@jax.custom_vjp
def low(v):
    return lax.optimization_barrier(v.astype(jnp.bfloat16)).astype(jnp.float32)

@jax.custom_vjp
def low_back(v):
    return v

def low_keep(v):
    return (low(v), None)

def low_pass(kept, grad):
    return (grad,)

def back_keep(v):
    return (v, None)

def back_low(kept, grad):
    return (low(grad),)
low.defvjp(low_keep, low_pass)
low_back.defvjp(back_keep, back_low)
best = lax.Precision.HIGHEST
eps_norm = 1e-06

def norm_apply(hidden, norm_gain, norm_shift):
    center = lax.optimization_barrier(jnp.mean(hidden, axis=-1, keepdims=True))
    offset = hidden - center
    spread = lax.optimization_barrier(jnp.mean(offset * offset, axis=-1, keepdims=True))
    return offset * lax.rsqrt(spread + eps_norm) * norm_gain + norm_shift

def forward_group(inputs, row_mask, params):
    ln1_gain, ln1_bias, w_qkv, bias_qv, w_proj, bias_proj, ln2_gain, ln2_bias, w_fc1, bias_fc1, w_fc2, bias_fc2 = params
    splits = N_TENSOR
    row_count = inputs.shape[0]
    sequences = row_count // SLOTS
    local_width = D // splits
    head_size = D // H
    head_count = H // splits
    feed_width = FF // splits
    masked_in = inputs * row_mask[:, None]
    normed_low = low(norm_apply(masked_in, ln1_gain, ln1_bias))
    normed_many = low_back(jnp.broadcast_to(normed_low, (splits, row_count, D)))
    w_split = w_qkv.reshape(D, 3, splits, local_width).transpose(2, 0, 1, 3)
    qkv_value = jnp.einsum('ntd,ndcf->ntcf', normed_many, w_split, precision=best)
    bias_full = jnp.stack([bias_qv[0], jnp.zeros((D,), jnp.float32), bias_qv[1]])
    bias_full = bias_full.reshape(3, splits, local_width).transpose(1, 0, 2)
    qkv_value = low(low_back(qkv_value + bias_full[:, None]))
    qkv_value = qkv_value.reshape(splits, sequences, SLOTS, 3, head_count, head_size)
    queries = qkv_value[:, :, :, 0]
    key_rows = qkv_value[:, :, :, 1]
    value_rows = qkv_value[:, :, :, 2]
    scores = jnp.einsum('nbshe,nbrhe->nbhsr', queries, key_rows, precision=best) * head_size ** (-0.5)
    scores = low_back(scores)
    key_mask = row_mask.reshape(sequences, SLOTS)
    scores = jnp.where(key_mask[None, :, None, None, :] > 0, scores, -1e+30)
    probs_low = low(jax.nn.softmax(scores, axis=-1))
    head_out = jnp.einsum('nbhsr,nbrhe->nbshe', probs_low, value_rows, precision=best)
    head_out = low(low_back(head_out.reshape(splits, row_count, local_width)))
    proj_split = w_proj.reshape(splits, local_width, D)
    attn_parts = low(low_back(jnp.einsum('ntf,nfe->nte', head_out, proj_split, precision=best)))
    resid_one = masked_in + lax.optimization_barrier(jnp.sum(attn_parts, axis=0)) + bias_proj
    second_low = low(norm_apply(resid_one, ln2_gain, ln2_bias))
    second_many = low_back(jnp.broadcast_to(second_low, (splits, row_count, D)))
    fc1_split = w_fc1.reshape(D, splits, feed_width).transpose(1, 0, 2)
    pre_act = jnp.einsum('ntd,ndf->ntf', second_many, fc1_split, precision=best)
    pre_act = low_back(pre_act + bias_fc1.reshape(splits, 1, feed_width))
    act_low = low(jax.nn.gelu(pre_act, approximate=False))
    fc2_split = w_fc2.reshape(splits, feed_width, D)
    mlp_parts = low(low_back(jnp.einsum('ntf,nfe->nte', act_low, fc2_split, precision=best)))
    return (resid_one + lax.optimization_barrier(jnp.sum(mlp_parts, axis=0)) + bias_fc2) * row_mask[:, None]

def reference(tokens, kept, teacher, out_grad, ln1_gain, ln1_bias, w_qkv, bias_qv, w_proj, bias_proj, ln2_gain, ln2_bias, w_fc1, bias_fc1, w_fc2, bias_fc2):
    params = tuple((weight.astype(jnp.float32) for weight in (ln1_gain, ln1_bias, w_qkv, bias_qv, w_proj, bias_proj, ln2_gain, ln2_bias, w_fc1, bias_fc1, w_fc2, bias_fc2)))
    slot_index = jnp.arange(SLOTS, dtype=jnp.int32)
    lengths = (BUFFER + kept).astype(jnp.int32)
    validity = (slot_index[None, :] < lengths[:, None]).astype(jnp.float32)
    valid_count = jnp.sum(lengths.astype(jnp.float32))
    blocks = SEQS // 8
    block_rows = 8 * SLOTS
    loss_scale = TOTAL_SLOTS / valid_count

    def scan_step(grad_sums, block_data):
        block_in, block_teacher, block_grad, block_mask = block_data

        def apply_block(inputs, weights):
            return forward_group(inputs, block_mask, weights)
        final_out, pull_back = jax.vjp(apply_block, block_in.astype(jnp.float32), params)
        errors = (final_out - block_teacher.astype(jnp.float32)) * block_mask[:, None]
        seed_grad = block_grad.astype(jnp.float32) + errors * loss_scale
        input_grad, weight_grads = pull_back(seed_grad)
        grad_sums = jax.tree.map(jnp.add, grad_sums, weight_grads)
        squared = errors * errors
        per_seq = lax.optimization_barrier(jnp.sum(squared.reshape(8, SLOTS * D), axis=1))
        return (grad_sums, (final_out.astype(jnp.bfloat16), input_grad, per_seq))
    initial = jax.tree.map(jnp.zeros_like, params)
    block_inputs = (tokens.reshape(blocks, block_rows, D), teacher.reshape(blocks, block_rows, D), out_grad.reshape(blocks, block_rows, D), validity.reshape(blocks, block_rows))
    grad_sums, (final_rows, input_rows, seq_sq) = lax.scan(scan_step, initial, block_inputs)
    loss_value = seq_sq.reshape(SEQS) * (SEQS / (2.0 * valid_count * D))
    return (final_rows.reshape(TOTAL_SLOTS, D), loss_value, input_rows.reshape(TOTAL_SLOTS, D), grad_sums[0], grad_sums[1], grad_sums[2], grad_sums[3], grad_sums[4], grad_sums[5], grad_sums[6], grad_sums[7], grad_sums[8], grad_sums[9], grad_sums[10], grad_sums[11])
```

```python
import functools

import jax
import jax.numpy as jnp
from jax import lax
from jax.experimental import pallas as pl
from jax.experimental.pallas import tpu as pltpu
from jax.sharding import PartitionSpec as P

D = 1024
H = 16
HEAD = D // H
BUFFER = 64
SLOTS = 320
HALF = D // 2
RB = 32
EPS = 1e-06
F32 = jnp.float32
BF16 = jnp.bfloat16
MESH = pl.DeviceIdType.MESH
NT = (((1,), (1,)), ((), ()))
TN = (((0,), (0,)), ((), ()))
NN = (((1,), (0,)), ((), ()))
INV_SQRT2 = 0.7071067811865476
INV_SQRT_2PI = 0.3989422804014327


def mm(a, b, dims):
    return lax.dot_general(a, b, dims, preferred_element_type=F32)


def fold8(x):
    return jnp.sum(x.reshape(x.shape[0] // 8, 8, x.shape[1]), axis=0)


def kernel(
    cfg,
    kept_ref, vec_ref, tok_in, tea_in, og_in, wqkv_in, wproj_in, wfc1_in, wfc2_in,
    out_hbm, tg_hbm, loss_ref, vout_ref, gfc2_ref, gfc1_ref, gproj_ref, gqkv_ref,
    wqkv, wproj, wfc1, wfc2, tok, tea, og,
    a_r, qkv_r, heads_r, c_r, h1_r, act_r, gp_r, seed_r, sl_r, dpre_r, dqkv_r,
    core_s, core_r, tot, gs, yr, zr, lacc, vacc, vs, vyr, vzr,
    in_sem, out_sem, ps_s, ps_r, y_s, y_r, z_s, z_r, v_s, v_r,
):
    S, NZ, CH, MB, NBLK, NZB, FW = cfg
    LW = wproj.shape[0]
    R = SLOTS
    rows_all = S * R
    dp = lax.axis_index("dp")
    t = lax.axis_index("tensor")
    y = lax.rem(dp, 2)
    z = dp // 2
    lo = lax.rem(t, 2)
    hi = t // 2
    sib = (dp, hi * 2 + (1 - lo))
    xn = (dp, (1 - hi) * 2 + lo)
    yn = (z * 2 + (1 - y), t)

    def zn(zz):
        return (zz * 2 + y, t)

    def in_copy(i, src, dst):
        return pltpu.make_async_copy(src, dst, in_sem.at[i])

    ins = [
        in_copy(0, tok_in, tok),
        in_copy(1, wqkv_in, wqkv),
        in_copy(2, wproj_in, wproj),
        in_copy(3, wfc1_in, wfc1),
        in_copy(4, wfc2_in, wfc2),
        in_copy(5, tea_in, tea),
        in_copy(6, og_in, og),
    ]
    for c in ins:
        c.start()

    bar = pltpu.get_barrier_semaphore()
    for peer in (sib, xn, yn):
        pl.semaphore_signal(bar, inc=1, device_id=peer, device_id_type=MESH)

    def bar_z(k, _):
        pl.semaphore_signal(bar, inc=1, device_id=zn(lax.rem(z + k, NZ)), device_id_type=MESH)
        return 0

    lax.fori_loop(1, NZ, bar_z, 0)
    pl.semaphore_wait(bar, 3 + NZ - 1)

    vacc[...] = jnp.zeros_like(vacc)
    count = lax.fori_loop(
        0, kept_ref.shape[0], lambda i, acc: acc + (kept_ref[i] + BUFFER).astype(F32), jnp.float32(0.0)
    )

    def length(s):
        return kept_ref[dp * S + s] + BUFFER

    def mask_rows(s, i):
        idx = lax.broadcasted_iota(jnp.int32, (RB, 1), 0) + i * RB
        return (idx < length(s)).astype(F32)

    def seq_rows(s):
        return pl.ds(pl.multiple_of(s * R, 64), R)

    def chunks(fn, init=0):
        return lax.fori_loop(0, R // RB, fn, init)

    def blk(s, i):
        return pl.ds(pl.multiple_of(s * R + i * RB, RB), RB)

    def loc(i):
        return pl.ds(pl.multiple_of(i * RB, RB), RB)

    def norm_stats(x):
        mean = jnp.mean(x, axis=-1, keepdims=True)
        off = x - mean
        var = jnp.mean(off * off, axis=-1, keepdims=True)
        r = lax.rsqrt(var + EPS)
        return off * r, r

    def cp(p, s, kind, src, dst, dev):
        return pltpu.make_async_remote_copy(
            src_ref=src, dst_ref=dst,
            send_sem=ps_s.at[p, s, kind], recv_sem=ps_r.at[p, s, kind],
            device_id=dev, device_id_type=MESH,
        )

    def cp_core(p, s):
        return cp(p, s, 0, core_s.at[s], core_r.at[s], sib)

    def cp_x(p, s):
        ref = tot.at[p, s, lo, hi]
        return cp(p, s, 1, ref, ref, xn)

    def cp_f1(p, s):
        ref = tot.at[p, s, lo, hi]
        return cp(p, s, 2, ref, ref, sib)

    def cp_f2(p, s):
        ref = tot.at[p, s, lo, 1 - hi]
        return cp(p, s, 3, ref, ref, sib)

    def ps_start(p, s, part):
        core_s[s] = part(1 - lo).astype(BF16)
        cp_core(p, s).start()
        own = part(lo).astype(BF16).astype(F32)
        cp_core(p, s).wait_recv()
        tot[p, s, lo, hi] = (own + core_r[s].astype(F32)).astype(BF16)
        cp_x(p, s).start()
        cp_f1(p, s).start()

    def ps_finish(p, s):
        cp_core(p, s).wait_send()
        cp_x(p, s).wait()
        cp_f2(p, s).start()
        cp_f1(p, s).wait()
        cp_f2(p, s).wait()

    def ps_total(p, s, i):
        rr = loc(i)
        parts = [
            tot[p, s, h, 0, rr, :].astype(F32) + tot[p, s, h, 1, rr, :].astype(F32) for h in range(2)
        ]
        return jnp.concatenate(parts, axis=1)

    def half_cols(h):
        return pl.ds(pl.multiple_of(h * HALF, HALF), HALF)

    lane_half = lax.broadcasted_iota(jnp.int32, (1, 2 * HEAD), 1) // HEAD

    def head_mask(hh):
        return (lane_half == hh).astype(F32).astype(BF16)

    def pair_cols(c, hp):
        return pl.ds(pl.multiple_of(c * LW + hp * 2 * HEAD, 2 * HEAD), 2 * HEAD)

    def probs_of(qm, k, s):
        sc = mm(qm, k, NT) * (HEAD ** -0.5)
        col = lax.broadcasted_iota(jnp.int32, (1, R), 1)
        sc = jnp.where(col < length(s), sc, -1e30)
        top = jnp.max(sc, axis=-1, keepdims=True)
        e = jnp.exp(sc - top)
        return e / jnp.sum(e, axis=-1, keepdims=True)

    npair = LW // (2 * HEAD)

    ins[0].wait()
    ins[1].wait()
    ins[2].wait()

    def phase_a(s, _):
        def ln(i, _):
            x = tok[blk(s, i), :].astype(F32) * mask_rows(s, i)
            hat, _r = norm_stats(x)
            a_r[blk(s, i), :] = (hat * vec_ref[0:1, :] + vec_ref[1:2, :]).astype(BF16)
            return 0

        chunks(ln)
        rs = seq_rows(s)
        av = a_r[rs, :]
        for c in range(3):
            cs = slice(c * LW, (c + 1) * LW)
            qkv_r[rs, cs] = (mm(av, wqkv[:, cs], NN) + vec_ref[7:8, cs]).astype(BF16)

        def pair(hp, _):
            q = qkv_r[rs, pair_cols(0, hp)]
            k = qkv_r[rs, pair_cols(1, hp)]
            v = qkv_r[rs, pair_cols(2, hp)]
            o = None
            for hh in range(2):
                pr = probs_of(q * head_mask(hh), k, s).astype(BF16)
                oh = mm(pr, v * head_mask(hh), NN)
                o = oh if o is None else o + oh
            heads_r[rs, pair_cols(0, hp)] = o.astype(BF16)
            return 0

        lax.fori_loop(0, npair, pair, 0)
        hv = heads_r[rs, :]
        ps_start(0, s, lambda h: mm(hv, wproj[:, half_cols(h)], NN))
        return 0

    lax.fori_loop(0, S, phase_a, 0)

    ins[3].wait()
    ins[4].wait()

    def phase_b(s, _):
        ps_finish(0, s)

        def ln(i, _):
            x = tok[blk(s, i), :].astype(F32) * mask_rows(s, i)
            h1 = x + ps_total(0, s, i) + vec_ref[2:3, :]
            h1_r[blk(s, i), :] = h1
            hat, _r = norm_stats(h1)
            c_r[blk(s, i), :] = (hat * vec_ref[3:4, :] + vec_ref[4:5, :]).astype(BF16)
            return 0

        chunks(ln)
        rs = seq_rows(s)
        cv = c_r[rs, :]

        def fc1(j, _):
            cs = pl.ds(pl.multiple_of(j * 256, 256), 256)
            pre = mm(cv, wfc1[:, cs], NN) + vec_ref[5:6, cs]
            phi = 0.5 * (1.0 + lax.erf(pre * INV_SQRT2))
            act_r[rs, cs] = (pre * phi).astype(BF16)
            gp_r[rs, cs] = phi + pre * (INV_SQRT_2PI * jnp.exp(-0.5 * pre * pre))
            return 0

        lax.fori_loop(0, FW // 256, fc1, 0)
        ps_start(1, s, lambda h: mm(act_r[rs, :], wfc2[:, half_cols(h)], NN))
        return 0

    lax.fori_loop(0, S, phase_b, 0)

    ins[5].wait()
    ins[6].wait()
    loss_scale = kept_ref.shape[0] / (2.0 * count * D)
    seed_scale = kept_ref.shape[0] * SLOTS * 1.0 / count

    def out_copy(s):
        return pltpu.make_async_copy(tea.at[seq_rows(s), :], out_hbm.at[seq_rows(s), :], out_sem.at[0, s])

    def tg_copy(s):
        return pltpu.make_async_copy(seed_r.at[seq_rows(s), :], tg_hbm.at[seq_rows(s), :], out_sem.at[1, s])

    def phase_c(s, _):
        ps_finish(1, s)
        lacc[...] = jnp.zeros_like(lacc)

        def fin(i, _):
            m = mask_rows(s, i)
            final = (h1_r[blk(s, i), :] + ps_total(1, s, i) + vec_ref[6:7, :]) * m
            diff = (final - tea[blk(s, i), :].astype(F32)) * m
            seed = (og[blk(s, i), :].astype(F32) + diff * seed_scale) * m
            tea[blk(s, i), :] = final.astype(BF16)
            seed_r[blk(s, i), :] = seed
            sl_r[blk(s, i), :] = seed.astype(BF16)
            lacc[...] += fold8(diff * diff)
            vacc[6] += fold8(seed)
            return 0

        chunks(fin)
        out_copy(s).start()
        loss_ref[s] = jnp.sum(lacc[...]) * loss_scale
        rs = seq_rows(s)
        sv = sl_r[rs, :]

        def dact(j, _):
            cs = pl.ds(pl.multiple_of(j * 256, 256), 256)
            d = mm(sv, wfc2[cs, :], NT) * gp_r[rs, cs]
            dl = d.astype(BF16)
            dpre_r[rs, cs] = dl
            vacc[5, :, cs] += fold8(dl.astype(F32))
            return 0

        lax.fori_loop(0, FW // 256, dact, 0)
        ps_start(0, s, lambda h: mm(dpre_r[rs, :], wfc1[half_cols(h), :], NT))
        return 0

    lax.fori_loop(0, S, phase_c, 0)

    def block_at(k):
        return lax.rem(z // NZB + 1 + k, NBLK)

    def cp_y(tile):
        return pltpu.make_async_remote_copy(
            src_ref=gs.at[tile, :, 1 - y], dst_ref=yr.at[tile],
            send_sem=y_s.at[tile], recv_sem=y_r.at[tile], device_id=yn, device_id_type=MESH,
        )

    def cp_z(g, tile, i, zz):
        slot = lax.rem(zz - z + NZ, NZ) - 1
        return pltpu.make_async_remote_copy(
            src_ref=yr.at[tile, i], dst_ref=zr.at[g, slot],
            send_sem=z_s.at[tile, i], recv_sem=z_r.at[g, slot], device_id=zn(zz), device_id_type=MESH,
        )

    def grad_tiles(g, lhs, parts):
        def one(k, _):
            cols = pl.ds(pl.multiple_of(block_at(k) * MB, MB), MB)
            tile = g * NBLK + k
            off = 0
            for lref, rref in parts:
                n = rref.shape[1]
                val = mm(lref[:, cols], rref[...], TN)
                gs[tile, :, :, :, off:off + n] = val.astype(BF16).reshape(NZB, 2, CH, n)
                off += n
            cp_y(tile).start()
            return 0

        lax.fori_loop(0, NBLK, one, 0)

    def z_stage(g, k):
        tile = g * NBLK + k
        cp_y(tile).wait_recv()

        def one(i, _):
            zz = block_at(k) * NZB + i
            yr[tile, i] = (gs[tile, i, y].astype(F32) + yr[tile, i].astype(F32)).astype(BF16)

            @pl.when(zz != z)
            def _():
                cp_z(g, tile, i, zz).start()

            return 0

        lax.fori_loop(0, NZB, one, 0)

    def z_stages(g):
        def one(k, _):
            z_stage(g, k)
            return 0

        lax.fori_loop(0, NBLK, one, 0)

    def grad_final(g, outs):
        def wait(j, _):
            zz = lax.rem(z + 1 + j, NZ)
            pltpu.make_async_remote_copy(
                src_ref=yr.at[0, 0], dst_ref=zr.at[g, j], send_sem=z_s.at[0, 0],
                recv_sem=z_r.at[g, j], device_id=zn(zz), device_id_type=MESH,
            ).wait_recv()
            return 0

        lax.fori_loop(0, NZ - 1, wait, 0)
        own_tile = g * NBLK + NBLK - 1
        own_i = lax.rem(z, NZB)
        off = 0
        for ref in outs:
            n = ref.shape[1]
            ref[...] = yr[own_tile, own_i, :, off:off + n].astype(F32)

            def add(j, _):
                ref[...] += zr[g, j, :, off:off + n].astype(F32)
                return 0

            lax.fori_loop(0, NZ - 1, add, 0)
            off += n

    grad_tiles(0, sl_r, [(sl_r, act_r)])
    grad_tiles(1, c_r, [(c_r, dpre_r)])

    def phase_d(s, _):
        ps_finish(0, s)

        def lnb(i, _):
            hat, r = norm_stats(h1_r[blk(s, i), :])
            dy = ps_total(0, s, i)
            vacc[3] += fold8(dy * hat)
            vacc[4] += fold8(dy)
            dg = dy * vec_ref[3:4, :]
            m1 = jnp.mean(dg, axis=-1, keepdims=True)
            m2 = jnp.mean(dg * hat, axis=-1, keepdims=True)
            dh1 = seed_r[blk(s, i), :] + r * (dg - m1 - hat * m2)
            seed_r[blk(s, i), :] = dh1
            vacc[2] += fold8(dh1)
            sl_r[blk(s, i), :] = dh1.astype(BF16)
            return 0

        chunks(lnb)
        rs = seq_rows(s)

        def pair(hp, _):
            wc = pl.ds(pl.multiple_of(hp * 2 * HEAD, 2 * HEAD), 2 * HEAD)
            dh = mm(sl_r[rs, :], wproj[wc, :], NT).astype(BF16)
            q = qkv_r[rs, pair_cols(0, hp)]
            k = qkv_r[rs, pair_cols(1, hp)]
            v = qkv_r[rs, pair_cols(2, hp)]
            dq = dk = dv = None
            for hh in range(2):
                hm = head_mask(hh)
                qm, km, dm = q * hm, k * hm, dh * hm
                pr = probs_of(qm, k, s)
                dpr = mm(dm, v, NT)
                ds = (pr * (dpr - jnp.sum(pr * dpr, axis=-1, keepdims=True))).astype(BF16)
                q1, k1, v1 = mm(ds, km, NN), mm(ds, qm, TN), mm(pr.astype(BF16), dm, TN)
                if dq is None:
                    dq, dk, dv = q1, k1, v1
                else:
                    dq, dk, dv = dq + q1, dk + k1, dv + v1
            dql = (dq * (HEAD ** -0.5)).astype(BF16)
            dvl = dv.astype(BF16)
            dqkv_r[rs, pair_cols(0, hp)] = dql
            dqkv_r[rs, pair_cols(1, hp)] = (dk * (HEAD ** -0.5)).astype(BF16)
            dqkv_r[rs, pair_cols(2, hp)] = dvl
            vacc[7, :, pair_cols(0, hp)] += fold8(dql.astype(F32))
            vacc[7, :, pair_cols(1, hp)] += fold8(dvl.astype(F32))
            return 0

        lax.fori_loop(0, npair, pair, 0)
        ps_start(1, s, lambda h: mm(dqkv_r[rs, :], wqkv[half_cols(h), :], NT))
        return 0

    lax.fori_loop(0, S, phase_d, 0)
    grad_tiles(2, None, [(sl_r, heads_r), (a_r, dqkv_r)])
    z_stages(0)

    def phase_e(s, _):
        ps_finish(1, s)

        def lnb(i, _):
            m = mask_rows(s, i)
            hat, r = norm_stats(tok[blk(s, i), :].astype(F32) * m)
            dy = ps_total(1, s, i)
            vacc[0] += fold8(dy * hat)
            vacc[1] += fold8(dy)
            dg = dy * vec_ref[0:1, :]
            m1 = jnp.mean(dg, axis=-1, keepdims=True)
            m2 = jnp.mean(dg * hat, axis=-1, keepdims=True)
            seed_r[blk(s, i), :] = (seed_r[blk(s, i), :] + r * (dg - m1 - hat * m2)) * m
            return 0

        chunks(lnb)
        tg_copy(s).start()
        return 0

    lax.fori_loop(0, S, phase_e, 0)

    for j in range(8):
        vs[j:j + 1, :] = jnp.sum(vacc[j], axis=0, keepdims=True)
    vy = pltpu.make_async_remote_copy(
        src_ref=vs, dst_ref=vyr, send_sem=v_s.at[0], recv_sem=v_r.at[0], device_id=yn, device_id_type=MESH
    )
    vy.start()

    z_stages(1)
    vy.wait()
    vzr[z] = vs[...] + vyr[...]

    def cp_v(k, zz):
        return pltpu.make_async_remote_copy(
            src_ref=vzr.at[z], dst_ref=vzr.at[z], send_sem=v_s.at[k], recv_sem=v_r.at[k],
            device_id=zn(zz), device_id_type=MESH,
        )

    def v_go(k, _):
        cp_v(k, lax.rem(z + k, NZ)).start()
        return 0

    lax.fori_loop(1, NZ, v_go, 0)
    z_stages(2)

    def v_wait(k, _):
        src = lax.rem(z - k + NZ, NZ)
        c = pltpu.make_async_remote_copy(
            src_ref=vzr.at[z], dst_ref=vzr.at[src], send_sem=v_s.at[k], recv_sem=v_r.at[k],
            device_id=zn(lax.rem(z + k, NZ)), device_id_type=MESH,
        )
        c.wait_recv()
        cp_v(k, lax.rem(z + k, NZ)).wait_send()
        return 0

    lax.fori_loop(1, NZ, v_wait, 0)
    vout_ref[...] = jnp.zeros_like(vout_ref)

    def v_add(k, _):
        vout_ref[...] += vzr[k]
        return 0

    lax.fori_loop(0, NZ, v_add, 0)

    grad_final(0, [gfc2_ref])
    grad_final(1, [gfc1_ref])
    grad_final(2, [gproj_ref, gqkv_ref])

    def drain_y(tile, _):
        cp_y(tile).wait_send()
        return 0

    lax.fori_loop(0, 3 * NBLK, drain_y, 0)
    for g in range(3):
        def drain_z(k, _):
            def one(i, _):
                zz = block_at(k) * NZB + i

                @pl.when(zz != z)
                def _():
                    cp_z(g, g * NBLK + k, i, zz).wait_send()

                return 0

            lax.fori_loop(0, NZB, one, 0)
            return 0

        lax.fori_loop(0, NBLK, drain_z, 0)

    def drain_out(s, _):
        out_copy(s).wait()
        tg_copy(s).wait()
        return 0

    lax.fori_loop(0, S, drain_out, 0)


def body(
    n_dp,
    tokens, kept, teacher, out_grad, ln1_gain, ln1_bias, w_qkv, bias_qv, w_proj, bias_proj,
    ln2_gain, ln2_bias, w_fc1, bias_fc1, w_fc2, bias_fc2,
):
    rows = tokens.shape[0]
    S = rows // SLOTS
    LW = w_qkv.shape[2]
    FW = w_fc1.shape[1]
    NZ = n_dp // 2
    CH = D // n_dp
    MB = max(256, 2 * CH)
    NBLK = D // MB
    NZB = MB // (2 * CH)
    T = 3 * NBLK
    cfg = (S, NZ, CH, MB, NBLK, NZB, FW)
    qb = jnp.concatenate([bias_qv[0], jnp.zeros_like(bias_qv[0]), bias_qv[1], jnp.zeros((D - 3 * LW,), BF16)])
    vec = jnp.stack(
        [ln1_gain, ln1_bias, bias_proj, ln2_gain, ln2_bias, bias_fc1, bias_fc2, qb]
    ).astype(F32)
    any_spec = pl.BlockSpec(memory_space=pl.ANY)
    vm = pl.BlockSpec(memory_space=pltpu.VMEM)
    sm = pl.BlockSpec(memory_space=pltpu.SMEM)
    sds = jax.ShapeDtypeStruct
    DMA = pltpu.SemaphoreType.DMA
    V = pltpu.VMEM
    out, token_grad, loss, vout, gfc2, gfc1, gproj, gqkv = pl.pallas_call(
        functools.partial(kernel, cfg),
        out_shape=[
            sds((rows, D), BF16), sds((rows, D), F32), sds((S,), F32), sds((8, D), F32),
            sds((CH, FW), F32), sds((CH, FW), F32), sds((CH, LW), F32), sds((CH, 3 * LW), F32),
        ],
        in_specs=[sm, vm] + [any_spec] * 7,
        out_specs=[any_spec, any_spec, sm] + [vm] * 5,
        scratch_shapes=[
            V((D, 3 * LW), BF16), V((LW, D), BF16), V((D, FW), BF16), V((FW, D), BF16),
            V((rows, D), BF16), V((rows, D), BF16), V((rows, D), BF16),
            V((rows, D), BF16), V((rows, 3 * LW), BF16), V((rows, LW), BF16), V((rows, D), BF16),
            V((rows, D), F32), V((rows, FW), BF16), V((rows, FW), F32), V((rows, D), F32),
            V((rows, D), BF16), V((rows, FW), BF16), V((rows, 3 * LW), BF16),
            V((S, SLOTS, HALF), BF16), V((S, SLOTS, HALF), BF16), V((2, S, 2, 2, SLOTS, HALF), BF16),
            V((T, NZB, 2, CH, 1024), BF16), V((T, NZB, CH, 1024), BF16), V((3, NZ - 1, CH, 1024), BF16),
            V((8, D), F32), V((8, 8, D), F32), V((8, D), F32), V((8, D), F32), V((NZ, 8, D), F32),
            DMA((7,)), DMA((2, S)), DMA((2, S, 4)), DMA((2, S, 4)), DMA((T,)), DMA((T,)),
            DMA((T, NZB)), DMA((3, NZ - 1)), DMA((NZ,)), DMA((NZ,)),
        ],
        compiler_params=pltpu.CompilerParams(
            collective_id=0, has_side_effects=True, vmem_limit_bytes=64 * 2**20 - 2**18
        ),
        name="layer",
    )(
        kept, vec, tokens, teacher, out_grad, w_qkv.reshape(D, 3 * LW), w_proj, w_fc1, w_fc2,
    )
    return (
        out, loss, token_grad, vout[0], vout[1], gqkv.reshape(CH, 3, LW),
        jnp.stack([vout[7, :LW], vout[7, LW:2 * LW]]), gproj.T, vout[2], vout[3], vout[4],
        gfc1, vout[5], gfc2.T, vout[6],
    )


def solution(mesh):
    tp = P("tensor")
    in_specs = (
        P("dp", None), P(), P("dp", None), P("dp", None), P(), P(), P(None, None, "tensor"),
        P(None, "tensor"), P("tensor", None), P(), P(), P(), P(None, "tensor"), tp, P("tensor", None), P(),
    )
    out_specs = (
        P("dp", None), P("dp"), P("dp", None), P(), P(), P("dp", None, "tensor"), P(None, "tensor"),
        P("tensor", "dp"), P(), P(), P(), P("dp", "tensor"), tp, P("tensor", "dp"), P(),
    )
    return jax.shard_map(
        functools.partial(body, mesh.shape["dp"]), mesh=mesh, in_specs=in_specs, out_specs=out_specs,
        check_vma=False,
    )
```

```python
import functools

import jax
import jax.numpy as jnp
from jax import lax
from jax.experimental import pallas as pl
from jax.experimental.pallas import tpu as pltpu
from jax.sharding import PartitionSpec as P

D = 1024
H = 16
HEAD = D // H
BUFFER = 64
SLOTS = 320
HALF = D // 2
RB = 32
EPS = 1e-06
F32 = jnp.float32
BF16 = jnp.bfloat16
MESH = pl.DeviceIdType.MESH
NT = (((1,), (1,)), ((), ()))
TN = (((0,), (0,)), ((), ()))
NN = (((1,), (0,)), ((), ()))
INV_SQRT2 = 0.7071067811865476
INV_SQRT_2PI = 0.3989422804014327


def mm(a, b, dims):
    return lax.dot_general(a, b, dims, preferred_element_type=F32)


def fold8(x):
    return jnp.sum(x.reshape(x.shape[0] // 8, 8, x.shape[1]), axis=0)


def kernel(
    cfg,
    kept_ref, ln1g_in, ln1b_in, bproj_in, ln2g_in, ln2b_in, bfc1_in, bfc2_in, bqv_in,
    tok_in, tea_in, og_in, wqkv_in, wproj_in, wfc1_in, wfc2_in,
    out_hbm, tg_hbm, loss_ref, vout_ref, gfc2_hbm, gfc1_hbm, gproj_hbm, gqkv_hbm,
    wqkv, wproj, wfc1, wfc2, tok, tea, og,
    a_r, qkv_r, heads_r, c_r, h1_r, act_r, gp_r, seed_r, sl_r, dpre_r, dqkv_r,
    core_s, core_r, tot, gs, rb, gfc2_r, gfc1_r, gproj_r, gqkv_r, vec_ref, lacc, vacc, vst, vrc,
    in_sem, out_sem, ps_s, ps_r, g_s, g_r, v_s, v_r,
):
    S, NDP, NBITS, CH, FW = cfg
    LW = wproj.shape[0]
    R = SLOTS
    rows_all = S * R
    dp = lax.axis_index("dp")
    t = lax.axis_index("tensor")
    lo = lax.rem(t, 2)
    hi = t // 2
    sib = (dp, hi * 2 + (1 - lo))
    xn = (dp, (1 - hi) * 2 + lo)
    bits = [lax.rem(dp // (1 << b), 2) for b in range(NBITS)]

    def flip(b):
        return (dp + (1 << b) * (1 - 2 * bits[b]), t)

    bar = pltpu.get_barrier_semaphore()
    for peer in [sib, xn] + [flip(b) for b in range(NBITS)]:
        pl.semaphore_signal(bar, inc=1, device_id=peer, device_id_type=MESH)

    def in_copy(i, src, dst):
        return pltpu.make_async_copy(src, dst, in_sem.at[i])

    def tok_copy(s):
        rows = pl.ds(pl.multiple_of(s * R, 64), R)
        return pltpu.make_async_copy(tok_in.at[rows, :], tok.at[rows, :], in_sem.at[6 + s])

    ins = [
        in_copy(0, wqkv_in, wqkv),
        in_copy(1, wproj_in, wproj),
        in_copy(2, wfc1_in, wfc1),
        in_copy(3, wfc2_in, wfc2),
        in_copy(4, tea_in, tea),
        in_copy(5, og_in, og),
    ]
    tok_copy(0).start()
    ins[0].start()
    ins[1].start()
    for j, ref in enumerate([ln1g_in, ln1b_in, bproj_in, ln2g_in, ln2b_in, bfc1_in, bfc2_in]):
        vec_ref[j:j + 1, :] = ref[...].astype(F32).reshape(1, ref.shape[0])
    vec_ref[7:8, :] = jnp.zeros((1, D), F32)
    bqv = bqv_in[...].astype(F32)
    vec_ref[7:8, 0:LW] = bqv[0:1]
    vec_ref[7:8, 2 * LW:3 * LW] = bqv[1:2]
    vacc[...] = jnp.zeros_like(vacc)
    count = lax.fori_loop(
        0, kept_ref.shape[0], lambda i, acc: acc + (kept_ref[i] + BUFFER).astype(F32), jnp.float32(0.0)
    )

    def length(s):
        return kept_ref[dp * S + s] + BUFFER

    def mask_rows(s, i):
        idx = lax.broadcasted_iota(jnp.int32, (RB, 1), 0) + i * RB
        return (idx < length(s)).astype(F32)

    def seq_rows(s):
        return pl.ds(pl.multiple_of(s * R, 64), R)

    def chunks(fn, init=0):
        return lax.fori_loop(0, R // RB, fn, init, unroll=2)

    def blk(s, i):
        return pl.ds(pl.multiple_of(s * R + i * RB, RB), RB)

    def loc(i):
        return pl.ds(pl.multiple_of(i * RB, RB), RB)

    def norm_stats(x):
        mean = jnp.mean(x, axis=-1, keepdims=True)
        off = x - mean
        var = jnp.mean(off * off, axis=-1, keepdims=True)
        r = lax.rsqrt(var + EPS)
        return off * r, r

    def cp(p, s, kind, src, dst, dev):
        return pltpu.make_async_remote_copy(
            src_ref=src, dst_ref=dst,
            send_sem=ps_s.at[p, s, kind], recv_sem=ps_r.at[p, s, kind],
            device_id=dev, device_id_type=MESH,
        )

    def cp_core(p, s):
        return cp(p, s, 0, core_s.at[s], core_r.at[s], sib)

    def cp_x(p, s):
        ref = tot.at[p, s, lo, hi]
        return cp(p, s, 1, ref, ref, xn)

    def cp_f1(p, s):
        ref = tot.at[p, s, lo, hi]
        return cp(p, s, 2, ref, ref, sib)

    def cp_f2(p, s):
        ref = tot.at[p, s, lo, 1 - hi]
        return cp(p, s, 3, ref, ref, sib)

    def ps_start(p, s, part):
        core_s[s] = part(1 - lo).astype(BF16)
        cp_core(p, s).start()
        own = part(lo).astype(BF16).astype(F32)
        cp_core(p, s).wait_recv()
        tot[p, s, lo, hi] = (own + core_r[s].astype(F32)).astype(BF16)
        cp_x(p, s).start()
        cp_f1(p, s).start()

    def ps_finish(p, s):
        cp_core(p, s).wait_send()
        cp_x(p, s).wait()
        cp_f2(p, s).start()
        cp_f1(p, s).wait()
        cp_f2(p, s).wait()

    def ps_total(p, s, i):
        rr = loc(i)
        parts = [
            tot[p, s, h, 0, rr, :].astype(F32) + tot[p, s, h, 1, rr, :].astype(F32) for h in range(2)
        ]
        return jnp.concatenate(parts, axis=1)

    def half_cols(h):
        return pl.ds(pl.multiple_of(h * HALF, HALF), HALF)

    lane_half = lax.broadcasted_iota(jnp.int32, (1, 2 * HEAD), 1) // HEAD

    def head_mask(hh):
        return (lane_half == hh).astype(F32).astype(BF16)

    def pair_cols(c, hp):
        return pl.ds(pl.multiple_of(c * LW + hp * 2 * HEAD, 2 * HEAD), 2 * HEAD)

    def probs_of(qm, k, s):
        sc = mm(qm, k, NT) * (HEAD ** -0.5)
        col = lax.broadcasted_iota(jnp.int32, (1, R), 1)
        sc = jnp.where(col < length(s), sc, -1e30)
        top = jnp.max(sc, axis=-1, keepdims=True)
        e = jnp.exp(sc - top)
        return e / jnp.sum(e, axis=-1, keepdims=True)

    npair = LW // (2 * HEAD)

    def swapped(tile):
        return (3 - lax.rem(tile + 3, 4)) // 3 if NBITS > 1 else 0

    def mix(f, p, q):
        return p + f * (q - p)

    def place(d, f):
        db = [(d >> b) & 1 for b in range(NBITS)]
        pos = sum(db[b] << (NBITS - 1 - b) for b in range(2, NBITS))
        if NBITS > 1:
            return pos + mix(f, db[0], db[1]) * (NDP // 2) + mix(f, db[1], db[0]) * (NDP // 4)
        return db[0]

    def stage_bit(f, j):
        if NBITS > 1 and j < 2:
            return mix(f, bits[j], bits[1 - j])
        return bits[j]

    def stage_peer(f, j):
        if NBITS > 1 and j < 2:
            step = [(1 << b) * (1 - 2 * bits[b]) for b in range(2)]
            return (dp + mix(f, step[j], step[1 - j]), t)
        return flip(j)

    def base(f, j):
        return sum((stage_bit(f, i) * (NDP >> (i + 1)) for i in range(j)), 0)

    def land(j):
        return NDP - (NDP >> j)

    def cp_g(tile, j):
        f = swapped(tile)
        n = NDP >> (j + 1)
        first = base(f, j) + (1 - stage_bit(f, j)) * n
        return pltpu.make_async_remote_copy(
            src_ref=gs.at[tile, pl.ds(first, n)], dst_ref=rb.at[tile, land(j):land(j) + n],
            send_sem=g_s.at[tile, j], recv_sem=g_r.at[tile, j],
            device_id=stage_peer(f, j), device_id_type=MESH,
        )

    def grad_tile(tile, lhs, rhs):
        f = swapped(tile)
        val = mm(lhs[...], rhs, TN).astype(BF16)
        for d in range(NDP):
            gs[tile, place(d, f)] = val[d * CH:(d + 1) * CH]
        cp_g(tile, 0).start()

    def grad_tiles(first, last, lhs, rhs, skip=0):
        def one(k, _):
            grad_tile(k, lhs, rhs[:, pl.ds(pl.multiple_of((k - skip) * 256, 256), 256)])
            return 0

        lax.fori_loop(first, last, one, 0)

    def advance(tile, j):
        f = swapped(tile)
        cp_g(tile, j).wait_recv()
        n = NDP >> (j + 1)
        mine = base(f, j + 1)

        if j + 1 < NBITS:
            def add(i, _):
                gs[tile, mine + i] = gs[tile, mine + i] + rb[tile, land(j) + i]
                return 0

            lax.fori_loop(0, n, add, 0)
            cp_g(tile, j + 1).start()
            return
        val = gs[tile, mine].astype(F32) + rb[tile, land(j)].astype(F32)

        def cols(k):
            return pl.ds(pl.multiple_of(k * 256, 256), 256)

        @pl.when(tile < NT1)
        def _():
            gfc2_r[cols(tile), :] = val.T

        @pl.when(jnp.logical_and(tile >= NT1, tile < 2 * NT1))
        def _():
            gfc1_r[:, cols(tile - NT1)] = val

        @pl.when(jnp.logical_and(tile >= 2 * NT1, tile < 2 * NT1 + NT2))
        def _():
            gproj_r[cols(tile - 2 * NT1), :] = val.T

        @pl.when(tile >= 2 * NT1 + NT2)
        def _():
            k = tile - 2 * NT1 - NT2
            gqkv_r[k // NT2, :, cols(lax.rem(k, NT2))] = val

    def plain(u):
        return u + (u + 2) // 3

    def pump(u):
        for j in range(NBITS):
            @pl.when(jnp.logical_and(u - j >= 0, u - j < NX))
            def _():
                advance(plain(u - j), j)

    def pumps(first, last):
        def one(u, _):
            pump(u)
            return 0

        lax.fori_loop(first, last, one, 0)

    NT1 = FW // 256
    NT2 = LW // 256
    T = 2 * NT1 + 4 * NT2
    NX = 3 * T // 4

    def phase_a(s, _):
        tok_copy(s).wait()

        def ln(i, _):
            x = tok[blk(s, i), :].astype(F32) * mask_rows(s, i)
            hat, _r = norm_stats(x)
            a_r[blk(s, i), :] = (hat * vec_ref[0:1, :] + vec_ref[1:2, :]).astype(BF16)
            return 0

        chunks(ln)

        @pl.when(s == 0)
        def _():
            ins[0].wait()

            def tok_start(i, _):
                tok_copy(i).start()
                return 0

            lax.fori_loop(1, S, tok_start, 0)
            for c in ins[2:]:
                c.start()

        rs = seq_rows(s)
        av = a_r[rs, :]
        for c in range(3):
            cs = slice(c * LW, (c + 1) * LW)
            qkv_r[rs, cs] = (mm(av, wqkv[c], NN) + vec_ref[7:8, cs]).astype(BF16)

        def pair(hp, _):
            q = qkv_r[rs, pair_cols(0, hp)]
            k = qkv_r[rs, pair_cols(1, hp)]
            v = qkv_r[rs, pair_cols(2, hp)]
            o = None
            for hh in range(2):
                pr = probs_of(q * head_mask(hh), k, s).astype(BF16)
                oh = mm(pr, v * head_mask(hh), NN)
                o = oh if o is None else o + oh
            heads_r[rs, pair_cols(0, hp)] = o.astype(BF16)
            return 0

        lax.fori_loop(0, npair, pair, 0)
        hv = heads_r[rs, :]

        @pl.when(s == 0)
        def _():
            ins[1].wait()
            pl.semaphore_wait(bar, 2 + NBITS)

        ps_start(0, s, lambda h: mm(hv, wproj[:, half_cols(h)], NN))
        return 0

    lax.fori_loop(0, S, phase_a, 0)

    ins[2].wait()
    ins[3].wait()

    def phase_b(s, _):
        ps_finish(0, s)

        def ln(i, _):
            x = tok[blk(s, i), :].astype(F32) * mask_rows(s, i)
            h1 = x + ps_total(0, s, i) + vec_ref[2:3, :]
            h1_r[blk(s, i), :] = h1
            hat, _r = norm_stats(h1)
            c_r[blk(s, i), :] = (hat * vec_ref[3:4, :] + vec_ref[4:5, :]).astype(BF16)
            return 0

        chunks(ln)
        rs = seq_rows(s)
        cv = c_r[rs, :]

        def fc1(j, _):
            cs = pl.ds(pl.multiple_of(j * 256, 256), 256)
            pre = mm(cv, wfc1[:, cs], NN) + vec_ref[5:6, cs]
            phi = 0.5 * (1.0 + lax.erf(pre * INV_SQRT2))
            act_r[rs, cs] = (pre * phi).astype(BF16)
            gp_r[rs, cs] = phi + pre * (INV_SQRT_2PI * jnp.exp(-0.5 * pre * pre))
            return 0

        lax.fori_loop(0, FW // 256, fc1, 0)
        ps_start(1, s, lambda h: mm(act_r[rs, :], wfc2[:, half_cols(h)], NN))
        return 0

    lax.fori_loop(0, S, phase_b, 0)

    ins[4].wait()
    ins[5].wait()
    loss_scale = kept_ref.shape[0] / (2.0 * count * D)
    seed_scale = kept_ref.shape[0] * SLOTS * 1.0 / count

    def out_copy(s):
        return pltpu.make_async_copy(tea.at[seq_rows(s), :], out_hbm.at[seq_rows(s), :], out_sem.at[0, s])

    def tg_copy(s):
        return pltpu.make_async_copy(seed_r.at[seq_rows(s), :], tg_hbm.at[seq_rows(s), :], out_sem.at[1, s])

    def phase_c(s, _):
        ps_finish(1, s)
        lacc[...] = jnp.zeros_like(lacc)

        def fin(i, _):
            m = mask_rows(s, i)
            final = (h1_r[blk(s, i), :] + ps_total(1, s, i) + vec_ref[6:7, :]) * m
            diff = (final - tea[blk(s, i), :].astype(F32)) * m
            seed = (og[blk(s, i), :].astype(F32) + diff * seed_scale) * m
            tea[blk(s, i), :] = final.astype(BF16)
            seed_r[blk(s, i), :] = seed
            sl_r[blk(s, i), :] = seed.astype(BF16)
            lacc[...] += fold8(diff * diff)
            vacc[6] += fold8(seed)
            return 0

        chunks(fin)
        out_copy(s).start()
        loss_ref[s] = jnp.sum(lacc[...]) * loss_scale
        rs = seq_rows(s)
        sv = sl_r[rs, :]

        @pl.when(s == S - 1)
        def _():
            grad_tiles(0, 2, sl_r, act_r)


        def dact(j, _):
            cs = pl.ds(pl.multiple_of(j * 256, 256), 256)
            d = mm(sv, wfc2[cs, :], NT) * gp_r[rs, cs]
            dl = d.astype(BF16)
            dpre_r[rs, cs] = dl
            vacc[5, :, cs] += fold8(dl.astype(F32))
            return 0

        lax.fori_loop(0, FW // 256, dact, 0)
        ps_start(0, s, lambda h: mm(dpre_r[rs, :], wfc1[half_cols(h), :], NT))
        return 0

    lax.fori_loop(0, S, phase_c, 0)

    grad_tiles(2, NT1, sl_r, act_r)
    grad_tiles(NT1, 2 * NT1, c_r, dpre_r, NT1)

    def phase_d(s, _):
        ps_finish(0, s)

        def lnb(i, _):
            hat, r = norm_stats(h1_r[blk(s, i), :])
            dy = ps_total(0, s, i)
            vacc[3] += fold8(dy * hat)
            vacc[4] += fold8(dy)
            dg = dy * vec_ref[3:4, :]
            m1 = jnp.mean(dg, axis=-1, keepdims=True)
            m2 = jnp.mean(dg * hat, axis=-1, keepdims=True)
            dh1 = seed_r[blk(s, i), :] + r * (dg - m1 - hat * m2)
            seed_r[blk(s, i), :] = dh1
            vacc[2] += fold8(dh1)
            sl_r[blk(s, i), :] = dh1.astype(BF16)
            return 0

        chunks(lnb)
        rs = seq_rows(s)

        def pair(hp, _):
            wc = pl.ds(pl.multiple_of(hp * 2 * HEAD, 2 * HEAD), 2 * HEAD)
            dh = mm(sl_r[rs, :], wproj[wc, :], NT).astype(BF16)
            q = qkv_r[rs, pair_cols(0, hp)]
            k = qkv_r[rs, pair_cols(1, hp)]
            v = qkv_r[rs, pair_cols(2, hp)]
            dq = dk = dv = None
            for hh in range(2):
                hm = head_mask(hh)
                qm, km, dm = q * hm, k * hm, dh * hm
                pr = probs_of(qm, k, s)
                dpr = mm(dm, v, NT)
                ds = (pr * (dpr - jnp.sum(pr * dpr, axis=-1, keepdims=True))).astype(BF16)
                q1, k1, v1 = mm(ds, km, NN), mm(ds, qm, TN), mm(pr.astype(BF16), dm, TN)
                if dq is None:
                    dq, dk, dv = q1, k1, v1
                else:
                    dq, dk, dv = dq + q1, dk + k1, dv + v1
            dql = (dq * (HEAD ** -0.5)).astype(BF16)
            dvl = dv.astype(BF16)
            dqkv_r[rs, pair_cols(0, hp)] = dql
            dqkv_r[rs, pair_cols(1, hp)] = (dk * (HEAD ** -0.5)).astype(BF16)
            dqkv_r[rs, pair_cols(2, hp)] = dvl
            vacc[7, :, pair_cols(0, hp)] += fold8(dql.astype(F32))
            vacc[7, :, pair_cols(1, hp)] += fold8(dvl.astype(F32))
            return 0

        lax.fori_loop(0, npair, pair, 0)
        ps_start(1, s, lambda h: sum(
            mm(dqkv_r[rs, c * LW:(c + 1) * LW], wqkv[c, half_cols(h), :], NT) for c in range(3)
        ))
        @pl.when(s < 2)
        def _():
            advance(4 * s + 1, 0)

        pump(s)
        return 0

    lax.fori_loop(0, S, phase_d, 0)
    grad_tiles(2 * NT1, 2 * NT1 + LW // 256, sl_r, heads_r, 2 * NT1)
    grad_tiles(2 * NT1 + LW // 256, T, a_r, dqkv_r, 2 * NT1 + LW // 256)

    pump(S)

    def phase_e(s, _):
        ps_finish(1, s)

        def lnb(i, _):
            m = mask_rows(s, i)
            hat, r = norm_stats(tok[blk(s, i), :].astype(F32) * m)
            dy = ps_total(1, s, i)
            vacc[0] += fold8(dy * hat)
            vacc[1] += fold8(dy)
            dg = dy * vec_ref[0:1, :]
            m1 = jnp.mean(dg, axis=-1, keepdims=True)
            m2 = jnp.mean(dg * hat, axis=-1, keepdims=True)
            seed_r[blk(s, i), :] = (seed_r[blk(s, i), :] + r * (dg - m1 - hat * m2)) * m
            return 0

        chunks(lnb)
        tg_copy(s).start()
        pump(S + 1 + s)
        return 0

    lax.fori_loop(0, S, phase_e, 0)

    for j in range(8):
        vst[0, j:j + 1, :] = jnp.sum(vacc[j], axis=0, keepdims=True)

    def cp_v(j):
        return pltpu.make_async_remote_copy(
            src_ref=vst.at[j], dst_ref=vrc.at[j], send_sem=v_s.at[j], recv_sem=v_r.at[j],
            device_id=flip(j), device_id_type=MESH,
        )

    def step_v(j):
        cp_v(j).wait()
        total = vst[j] + vrc[j]
        if j + 1 < NBITS:
            vst[j + 1] = total
            cp_v(j + 1).start()
        else:
            vout_ref[...] = total

    cp_v(0).start()
    advance(9, 0)
    advance(1, 1)
    advance(5, 1)
    step_v(0)
    pump(2 * S + 1)
    step_v(1)
    for j in range(2, NBITS):
        advance(1, j)
        advance(5, j)
    pump(2 * S + 2)
    for j in range(2, NBITS):
        step_v(j)
    advance(9, 1)
    pumps(2 * S + 3, NX + NBITS - 1)
    for j in range(2, NBITS):
        advance(9, j)
    grad_out = [
        pltpu.make_async_copy(src, dst, out_sem.at[2, i])
        for i, (src, dst) in enumerate(
            ((gfc2_r, gfc2_hbm), (gfc1_r, gfc1_hbm), (gproj_r, gproj_hbm), (gqkv_r, gqkv_hbm))
        )
    ]
    for c in grad_out:
        c.start()

    def drain(tile, _):
        for j in range(NBITS):
            cp_g(tile, j).wait_send()
        return 0

    lax.fori_loop(0, T, drain, 0)

    def drain_out(s, _):
        out_copy(s).wait()
        tg_copy(s).wait()
        return 0

    lax.fori_loop(0, S, drain_out, 0)
    for c in grad_out:
        c.wait()


def finish(loss_in, v_in, *refs):
    ins, refs = refs[:6], refs[6:]
    loss_o, ln1g_o, ln1b_o, bqv_o, bproj_o, ln2g_o, ln2b_o, bfc1_o, bfc2_o = refs[:9]
    outs, mids, sem = refs[9:15], refs[15:21], refs[21]
    moves = []
    for src, mid, dst in zip(ins, mids, outs):
        rows = src.shape[0]
        parts = rows // 240 if rows % 240 == 0 else 1
        for i in range(parts):
            rr = pl.ds(i * (rows // parts), rows // parts)
            k = len(moves)
            moves.append((
                pltpu.make_async_copy(src.at[rr], mid.at[rr], sem.at[0, k]),
                pltpu.make_async_copy(mid.at[rr], dst.at[rr], sem.at[1, k]),
            ))
    for c, _ in moves:
        c.start()
    for i in range(loss_in.shape[0]):
        loss_o[i] = loss_in[i]
    for j, ref in enumerate([ln1g_o, ln1b_o, bproj_o, ln2g_o, ln2b_o, bfc1_o, bfc2_o]):
        ref[...] = v_in[j]
    lw = bqv_o.shape[1]
    bqv_o[0:1, :] = v_in[7:8, 0:lw]
    bqv_o[1:2, :] = v_in[7:8, lw:2 * lw]
    for c, d in moves:
        c.wait()
        d.start()
    for _, d in moves:
        d.wait()


def body(
    n_dp,
    tokens, kept, teacher, out_grad, ln1_gain, ln1_bias, w_qkv, bias_qv, w_proj, bias_proj,
    ln2_gain, ln2_bias, w_fc1, bias_fc1, w_fc2, bias_fc2,
):
    rows = tokens.shape[0]
    S = rows // SLOTS
    LW = w_qkv.shape[2]
    FW = w_fc1.shape[1]
    CH = D // n_dp
    NBITS = n_dp.bit_length() - 1
    T = (2 * FW + 4 * LW) // 256
    cfg = (S, n_dp, NBITS, CH, FW)
    any_spec = pl.BlockSpec(memory_space=pl.ANY)
    vm = pl.BlockSpec(memory_space=pltpu.VMEM)
    sm = pl.BlockSpec(memory_space=pltpu.SMEM)
    sds = jax.ShapeDtypeStruct
    DMA = pltpu.SemaphoreType.DMA
    V = pltpu.VMEM
    big = [
        ((rows, D), BF16), ((rows, D), F32), ((FW, CH), F32), ((CH, FW), F32), ((LW, CH), F32), ((3, CH, LW), F32),
    ]
    out, tg, loss, vout, *grads = pl.pallas_call(
        functools.partial(kernel, cfg),
        out_shape=[sds(*big[0]), sds(*big[1]), sds((S,), F32), sds((8, D), F32)] + [sds(*b) for b in big[2:]],
        in_specs=[sm] + [vm] * 8 + [any_spec] * 7,
        out_specs=[any_spec, any_spec, sm, vm] + [any_spec] * 4,
        scratch_shapes=[
            V((3, D, LW), BF16), V((LW, D), BF16), V((D, FW), BF16), V((FW, D), BF16),
            V((rows, D), BF16), V((rows, D), BF16), V((rows, D), BF16),
            V((rows, D), BF16), V((rows, 3 * LW), BF16), V((rows, LW), BF16), V((rows, D), BF16),
            V((rows, D), F32), V((rows, FW), BF16), V((rows, FW), F32), V((rows, D), F32),
            V((rows, D), BF16), V((rows, FW), BF16), V((rows, 3 * LW), BF16),
            V((S, SLOTS, HALF), BF16), V((S, SLOTS, HALF), BF16), V((2, S, 2, 2, SLOTS, HALF), BF16),
            V((T, n_dp, CH, 256), BF16), V((T, n_dp - 1, CH, 256), BF16),
            V((FW, CH), F32), V((CH, FW), F32), V((LW, CH), F32), V((3, CH, LW), F32),
            V((8, D), F32), V((8, D), F32), V((8, 8, D), F32), V((NBITS, 8, D), F32), V((NBITS, 8, D), F32),
            DMA((6 + S,)), DMA((3, max(S, 4))), DMA((2, S, 4)), DMA((2, S, 4)), DMA((T, NBITS)), DMA((T, NBITS)),
            DMA((NBITS,)), DMA((NBITS,)),
        ],
        compiler_params=pltpu.CompilerParams(
            collective_id=0, has_side_effects=True, vmem_limit_bytes=64 * 2**20 - 2**18
        ),
        name="layer",
    )(
        kept, ln1_gain, ln1_bias, bias_proj, ln2_gain, ln2_bias, bias_fc1, bias_fc2, bias_qv,
        tokens, teacher, out_grad, w_qkv.transpose(1, 0, 2), w_proj, w_fc1, w_fc2,
    )
    vd = sds((D,), F32)
    loss, g_ln1g, g_ln1b, g_bqv, g_bproj, g_ln2g, g_ln2b, g_bfc1, g_bfc2, out, token_grad, g_wfc2, g_wfc1, g_wproj, g_wqkv = (
        pl.pallas_call(
            finish,
            out_shape=[sds((S,), F32), vd, vd, sds((2, LW), F32), vd, vd, vd, sds((FW,), F32), vd]
            + [sds(*b) for b in big],
            in_specs=[sm, vm] + [any_spec] * 6,
            out_specs=[sm] + [vm] * 8 + [any_spec] * 6,
            scratch_shapes=[V(*b) for b in big] + [DMA((2, 16))],
            compiler_params=pltpu.CompilerParams(vmem_limit_bytes=60 * 2**20),
            name="finish",
        )(loss, vout, out, tg, *grads)
    )
    return (
        out, loss, token_grad, g_ln1g, g_ln1b, g_wqkv.transpose(1, 0, 2), g_bqv, g_wproj, g_bproj, g_ln2g, g_ln2b,
        g_wfc1, g_bfc1, g_wfc2, g_bfc2,
    )


def solution(mesh):
    tp = P("tensor")
    in_specs = (
        P("dp", None), P(), P("dp", None), P("dp", None), P(), P(), P(None, None, "tensor"),
        P(None, "tensor"), P("tensor", None), P(), P(), P(), P(None, "tensor"), tp, P("tensor", None), P(),
    )
    out_specs = (
        P("dp", None), P("dp"), P("dp", None), P(), P(), P("dp", None, "tensor"), P(None, "tensor"),
        P("tensor", "dp"), P(), P(), P(), P("dp", "tensor"), tp, P("tensor", "dp"), P(),
    )
    return jax.shard_map(
        functools.partial(body, mesh.shape["dp"]), mesh=mesh, in_specs=in_specs, out_specs=out_specs,
        check_vma=False,
    )
```

```python
import functools

import jax
import jax.numpy as jnp
from jax import lax
from jax.experimental import pallas as pl
from jax.experimental.pallas import tpu as pltpu
from jax.sharding import PartitionSpec as P

D = 1024
H = 16
HEAD = D // H
BUFFER = 64
SLOTS = 320
HALF = D // 2
RB = 32
EPS = 1e-06
F32 = jnp.float32
BF16 = jnp.bfloat16
MESH = pl.DeviceIdType.MESH
NT = (((1,), (1,)), ((), ()))
TN = (((0,), (0,)), ((), ()))
NN = (((1,), (0,)), ((), ()))
INV_SQRT2 = 0.7071067811865476
INV_SQRT_2PI = 0.3989422804014327


def mm(a, b, dims):
    return lax.dot_general(a, b, dims, preferred_element_type=F32)


def fold8(x):
    return jnp.sum(x.reshape(x.shape[0] // 8, 8, x.shape[1]), axis=0)


def kernel(
    cfg,
    kept_ref, ln1g_in, ln1b_in, bproj_in, ln2g_in, ln2b_in, bfc1_in, bfc2_in, bqv_in,
    tok_in, tea_in, og_in, wqkv_in, wproj_in, wfc1_in, wfc2_in,
    tea, seed_r, loss_ref, vout_ref, gfc2_r, gfc1_r, gproj_r, gqkv_r,
    wqkv, wproj, wfc1, wfc2, tok, og,
    a_r, qkv_r, heads_r, c_r, h1_r, act_r, gp_r, sl_r, dpre_r, dqkv_r,
    core_s, core_r, tot, gs, rb, vec_ref, lacc, vacc, vst, vrc,
    in_sem, ps_s, ps_r, g_s, g_r, v_s, v_r,
):
    S, NDP, NBITS, CH, FW = cfg
    LW = wproj.shape[0]
    R = SLOTS
    rows_all = S * R
    dp = lax.axis_index("dp")
    t = lax.axis_index("tensor")
    lo = lax.rem(t, 2)
    hi = t // 2
    sib = (dp, hi * 2 + (1 - lo))
    xn = (dp, (1 - hi) * 2 + lo)
    bits = [lax.rem(dp // (1 << b), 2) for b in range(NBITS)]

    def flip(b):
        return (dp + (1 << b) * (1 - 2 * bits[b]), t)

    bar = pltpu.get_barrier_semaphore()
    for peer in [sib, xn] + [flip(b) for b in range(NBITS)]:
        pl.semaphore_signal(bar, inc=1, device_id=peer, device_id_type=MESH)

    def in_copy(i, src, dst):
        return pltpu.make_async_copy(src, dst, in_sem.at[i])

    def tok_copy(s):
        rows = pl.ds(pl.multiple_of(s * R, 64), R)
        return pltpu.make_async_copy(tok_in.at[rows, :], tok.at[rows, :], in_sem.at[6 + s])

    ins = [
        in_copy(0, wqkv_in, wqkv),
        in_copy(1, wproj_in, wproj),
        in_copy(2, wfc1_in, wfc1),
        in_copy(3, wfc2_in, wfc2),
        in_copy(4, tea_in, tea),
        in_copy(5, og_in, og),
    ]
    tok_copy(0).start()
    ins[0].start()
    ins[1].start()
    for j, ref in enumerate([ln1g_in, ln1b_in, bproj_in, ln2g_in, ln2b_in, bfc1_in, bfc2_in]):
        vec_ref[j:j + 1, :] = ref[...].astype(F32).reshape(1, ref.shape[0])
    vec_ref[7:8, :] = jnp.zeros((1, D), F32)
    bqv = bqv_in[...].astype(F32)
    vec_ref[7:8, 0:LW] = bqv[0:1]
    vec_ref[7:8, 2 * LW:3 * LW] = bqv[1:2]
    vacc[...] = jnp.zeros_like(vacc)
    count = lax.fori_loop(
        0, kept_ref.shape[0], lambda i, acc: acc + (kept_ref[i] + BUFFER).astype(F32), jnp.float32(0.0)
    )

    def length(s):
        return kept_ref[dp * S + s] + BUFFER

    def mask_rows(s, i):
        idx = lax.broadcasted_iota(jnp.int32, (RB, 1), 0) + i * RB
        return (idx < length(s)).astype(F32)

    def seq_rows(s):
        return pl.ds(pl.multiple_of(s * R, 64), R)

    def chunks(fn, init=0):
        return lax.fori_loop(0, R // RB, fn, init, unroll=2)

    def blk(s, i):
        return pl.ds(pl.multiple_of(s * R + i * RB, RB), RB)

    def loc(i):
        return pl.ds(pl.multiple_of(i * RB, RB), RB)

    def norm_stats(x):
        mean = jnp.mean(x, axis=-1, keepdims=True)
        off = x - mean
        var = jnp.mean(off * off, axis=-1, keepdims=True)
        r = lax.rsqrt(var + EPS)
        return off * r, r

    def cp(p, s, kind, src, dst, dev):
        return pltpu.make_async_remote_copy(
            src_ref=src, dst_ref=dst,
            send_sem=ps_s.at[p, s, kind], recv_sem=ps_r.at[p, s, kind],
            device_id=dev, device_id_type=MESH,
        )

    def cp_core(p, s):
        return cp(p, s, 0, core_s.at[s], core_r.at[s], sib)

    def cp_x(p, s):
        ref = tot.at[p, s, lo, hi]
        return cp(p, s, 1, ref, ref, xn)

    def cp_f1(p, s):
        ref = tot.at[p, s, lo, hi]
        return cp(p, s, 2, ref, ref, sib)

    def cp_f2(p, s):
        ref = tot.at[p, s, lo, 1 - hi]
        return cp(p, s, 3, ref, ref, sib)

    def ps_start(p, s, part):
        core_s[s] = part(1 - lo).astype(BF16)
        cp_core(p, s).start()
        own = part(lo).astype(BF16).astype(F32)
        cp_core(p, s).wait_recv()
        tot[p, s, lo, hi] = (own + core_r[s].astype(F32)).astype(BF16)
        cp_x(p, s).start()
        cp_f1(p, s).start()

    def ps_forward(p, s):
        cp_core(p, s).wait_send()
        cp_x(p, s).wait()
        cp_f2(p, s).start()

    def ps_finish(p, s):
        cp_f1(p, s).wait()
        cp_f2(p, s).wait()

    def ps_total(p, s, i):
        rr = loc(i)
        parts = [
            tot[p, s, h, 0, rr, :].astype(F32) + tot[p, s, h, 1, rr, :].astype(F32) for h in range(2)
        ]
        return jnp.concatenate(parts, axis=1)

    def half_cols(h):
        return pl.ds(pl.multiple_of(h * HALF, HALF), HALF)

    lane_half = lax.broadcasted_iota(jnp.int32, (1, 2 * HEAD), 1) // HEAD

    def head_mask(hh):
        return (lane_half == hh).astype(F32).astype(BF16)

    def pair_cols(c, hp):
        return pl.ds(pl.multiple_of(c * LW + hp * 2 * HEAD, 2 * HEAD), 2 * HEAD)

    def probs_of(qm, k, s):
        sc = mm(qm, k, NT) * (HEAD ** -0.5)
        col = lax.broadcasted_iota(jnp.int32, (1, R), 1)
        sc = jnp.where(col < length(s), sc, -1e30)
        top = jnp.max(sc, axis=-1, keepdims=True)
        e = jnp.exp(sc - top)
        return e / jnp.sum(e, axis=-1, keepdims=True)

    npair = LW // (2 * HEAD)

    def swapped(tile):
        return lax.rem(tile, 2) * ((T - tile) // (T - 3)) if NBITS > 1 else 0

    def mix(f, p, q):
        return p + f * (q - p)

    def place(d, f):
        db = [(d >> b) & 1 for b in range(NBITS)]
        pos = sum(db[b] << (NBITS - 1 - b) for b in range(2, NBITS))
        if NBITS > 1:
            return pos + mix(f, db[0], db[1]) * (NDP // 2) + mix(f, db[1], db[0]) * (NDP // 4)
        return db[0]

    def stage_bit(f, j):
        if NBITS > 1 and j < 2:
            return mix(f, bits[j], bits[1 - j])
        return bits[j]

    def stage_peer(f, j):
        if NBITS > 1 and j < 2:
            step = [(1 << b) * (1 - 2 * bits[b]) for b in range(2)]
            return (dp + mix(f, step[j], step[1 - j]), t)
        return flip(j)

    def base(f, j):
        return sum((stage_bit(f, i) * (NDP >> (i + 1)) for i in range(j)), 0)

    def land(j):
        return NDP - (NDP >> j)

    def cp_g(tile, j):
        f = swapped(tile)
        n = NDP >> (j + 1)
        first = base(f, j) + (1 - stage_bit(f, j)) * n
        return pltpu.make_async_remote_copy(
            src_ref=gs.at[tile, pl.ds(first, n)], dst_ref=rb.at[tile, land(j):land(j) + n],
            send_sem=g_s.at[tile, j], recv_sem=g_r.at[tile, j],
            device_id=stage_peer(f, j), device_id_type=MESH,
        )

    def grad_tile(tile, lhs, rhs):
        f = swapped(tile)
        val = mm(lhs[...], rhs, TN).astype(BF16)
        for d in range(NDP):
            gs[tile, place(d, f)] = val[d * CH:(d + 1) * CH]
        cp_g(tile, 0).start()

    def grad_tiles(first, last, lhs, rhs, skip=0):
        def one(k, _):
            grad_tile(k, lhs, rhs[:, pl.ds(pl.multiple_of((k - skip) * 256, 256), 256)])
            return 0

        lax.fori_loop(first, last, one, 0)

    def advance(tile, j):
        f = swapped(tile)
        cp_g(tile, j).wait_recv()
        n = NDP >> (j + 1)
        mine = base(f, j + 1)

        if j + 1 < NBITS:
            def add(i, _):
                gs[tile, mine + i] = gs[tile, mine + i] + rb[tile, land(j) + i]
                return 0

            lax.fori_loop(0, n, add, 0)
            cp_g(tile, j + 1).start()
            return
        val = gs[tile, mine].astype(F32) + rb[tile, land(j)].astype(F32)

        def cols(k):
            return pl.ds(pl.multiple_of(k * 256, 256), 256)

        @pl.when(tile < NT1)
        def _():
            gfc2_r[cols(tile), :] = val.T

        @pl.when(jnp.logical_and(tile >= NT1, tile < 2 * NT1))
        def _():
            gfc1_r[:, cols(tile - NT1)] = val

        @pl.when(jnp.logical_and(tile >= 2 * NT1, tile < 2 * NT1 + NT2))
        def _():
            gproj_r[cols(tile - 2 * NT1), :] = val.T

        @pl.when(tile >= 2 * NT1 + NT2)
        def _():
            k = tile - 2 * NT1 - NT2
            gqkv_r[k // NT2, :, cols(lax.rem(k, NT2))] = val

    def steps(*pairs):
        for tile, j in pairs:
            for i in range(j, NBITS if j == 2 else j + 1):
                advance(tile, i)

    def steps_at(s, *lists):
        for at, pairs in enumerate(lists):
            if pairs:
                @pl.when(s == at)
                def _():
                    steps(*pairs)

    NT1 = FW // 256
    NT2 = LW // 256
    T = 2 * NT1 + 4 * NT2

    def phase_a(s, _):
        tok_copy(s).wait()

        def ln(i, _):
            x = tok[blk(s, i), :].astype(F32) * mask_rows(s, i)
            hat, _r = norm_stats(x)
            a_r[blk(s, i), :] = (hat * vec_ref[0:1, :] + vec_ref[1:2, :]).astype(BF16)
            return 0

        chunks(ln)

        @pl.when(s == 0)
        def _():
            ins[0].wait()

            def tok_start(i, _):
                tok_copy(i).start()
                return 0

            lax.fori_loop(1, S, tok_start, 0)
            for c in ins[2:]:
                c.start()

        rs = seq_rows(s)
        av = a_r[rs, :]
        for c in range(3):
            cs = slice(c * LW, (c + 1) * LW)
            qkv_r[rs, cs] = (mm(av, wqkv[c], NN) + vec_ref[7:8, cs]).astype(BF16)

        def pair(hp, _):
            q = qkv_r[rs, pair_cols(0, hp)]
            k = qkv_r[rs, pair_cols(1, hp)]
            v = qkv_r[rs, pair_cols(2, hp)]
            o = None
            for hh in range(2):
                pr = probs_of(q * head_mask(hh), k, s).astype(BF16)
                oh = mm(pr, v * head_mask(hh), NN)
                o = oh if o is None else o + oh
            heads_r[rs, pair_cols(0, hp)] = o.astype(BF16)
            return 0

        lax.fori_loop(0, npair, pair, 0)
        hv = heads_r[rs, :]

        @pl.when(s == 0)
        def _():
            ins[1].wait()
            pl.semaphore_wait(bar, 2 + NBITS)

        ps_start(0, s, lambda h: mm(hv, wproj[:, half_cols(h)], NN))
        return 0

    lax.fori_loop(0, S, phase_a, 0)

    ins[2].wait()
    ins[3].wait()

    def phase_b(s, _):
        ps_forward(0, s)
        ps_finish(0, s)

        def ln(i, _):
            x = tok[blk(s, i), :].astype(F32) * mask_rows(s, i)
            h1 = x + ps_total(0, s, i) + vec_ref[2:3, :]
            h1_r[blk(s, i), :] = h1
            hat, _r = norm_stats(h1)
            c_r[blk(s, i), :] = (hat * vec_ref[3:4, :] + vec_ref[4:5, :]).astype(BF16)
            return 0

        chunks(ln)
        rs = seq_rows(s)
        cv = c_r[rs, :]

        def fc1(j, _):
            cs = pl.ds(pl.multiple_of(j * 256, 256), 256)
            pre = mm(cv, wfc1[:, cs], NN) + vec_ref[5:6, cs]
            phi = 0.5 * (1.0 + lax.erf(pre * INV_SQRT2))
            act_r[rs, cs] = (pre * phi).astype(BF16)
            gp_r[rs, cs] = phi + pre * (INV_SQRT_2PI * jnp.exp(-0.5 * pre * pre))
            return 0

        lax.fori_loop(0, FW // 256, fc1, 0)
        ps_start(1, s, lambda h: mm(act_r[rs, :], wfc2[:, half_cols(h)], NN))
        return 0

    lax.fori_loop(0, S, phase_b, 0)

    ins[4].wait()
    ins[5].wait()
    loss_scale = kept_ref.shape[0] / (2.0 * count * D)
    seed_scale = kept_ref.shape[0] * SLOTS * 1.0 / count

    def phase_c(s, _):
        ps_forward(1, s)
        ps_finish(1, s)
        lacc[...] = jnp.zeros_like(lacc)

        def fin(i, _):
            m = mask_rows(s, i)
            final = (h1_r[blk(s, i), :] + ps_total(1, s, i) + vec_ref[6:7, :]) * m
            diff = (final - tea[blk(s, i), :].astype(F32)) * m
            seed = (og[blk(s, i), :].astype(F32) + diff * seed_scale) * m
            tea[blk(s, i), :] = final.astype(BF16)
            seed_r[blk(s, i), :] = seed
            sl_r[blk(s, i), :] = seed.astype(BF16)
            lacc[...] += fold8(diff * diff)
            vacc[6] += fold8(seed)
            return 0

        chunks(fin)
        loss_ref[s] = jnp.sum(lacc[...]) * loss_scale
        rs = seq_rows(s)
        sv = sl_r[rs, :]

        @pl.when(s == S - 1)
        def _():
            grad_tiles(0, 2, sl_r, act_r)


        def dact(j, _):
            cs = pl.ds(pl.multiple_of(j * 256, 256), 256)
            d = mm(sv, wfc2[cs, :], NT) * gp_r[rs, cs]
            dl = d.astype(BF16)
            dpre_r[rs, cs] = dl
            vacc[5, :, cs] += fold8(dl.astype(F32))
            return 0

        lax.fori_loop(0, FW // 256, dact, 0)
        ps_start(0, s, lambda h: mm(dpre_r[rs, :], wfc1[half_cols(h), :], NT))
        return 0

    lax.fori_loop(0, S, phase_c, 0)

    grad_tiles(2, 4, sl_r, act_r)
    grad_tiles(4, 5, c_r, dpre_r, 4)

    def phase_d(s, _):
        ps_forward(0, s)

        steps_at(
            s,
            [(0, 0)],
            [(4, 0), (3, 0), (0, 1)],
            [(4, 1), (1, 1), (0, 2)],
        )
        ps_finish(0, s)

        def lnb(i, _):
            hat, r = norm_stats(h1_r[blk(s, i), :])
            dy = ps_total(0, s, i)
            vacc[3] += fold8(dy * hat)
            vacc[4] += fold8(dy)
            dg = dy * vec_ref[3:4, :]
            m1 = jnp.mean(dg, axis=-1, keepdims=True)
            m2 = jnp.mean(dg * hat, axis=-1, keepdims=True)
            dh1 = seed_r[blk(s, i), :] + r * (dg - m1 - hat * m2)
            seed_r[blk(s, i), :] = dh1
            vacc[2] += fold8(dh1)
            sl_r[blk(s, i), :] = dh1.astype(BF16)
            return 0

        chunks(lnb)
        rs = seq_rows(s)

        def pair(hp, _):
            wc = pl.ds(pl.multiple_of(hp * 2 * HEAD, 2 * HEAD), 2 * HEAD)
            dh = mm(sl_r[rs, :], wproj[wc, :], NT).astype(BF16)
            q = qkv_r[rs, pair_cols(0, hp)]
            k = qkv_r[rs, pair_cols(1, hp)]
            v = qkv_r[rs, pair_cols(2, hp)]
            dq = dk = dv = None
            for hh in range(2):
                hm = head_mask(hh)
                qm, km, dm = q * hm, k * hm, dh * hm
                pr = probs_of(qm, k, s)
                dpr = mm(dm, v, NT)
                ds = (pr * (dpr - jnp.sum(pr * dpr, axis=-1, keepdims=True))).astype(BF16)
                q1, k1, v1 = mm(ds, km, NN), mm(ds, qm, TN), mm(pr.astype(BF16), dm, TN)
                if dq is None:
                    dq, dk, dv = q1, k1, v1
                else:
                    dq, dk, dv = dq + q1, dk + k1, dv + v1
            dql = (dq * (HEAD ** -0.5)).astype(BF16)
            dvl = dv.astype(BF16)
            dqkv_r[rs, pair_cols(0, hp)] = dql
            dqkv_r[rs, pair_cols(1, hp)] = (dk * (HEAD ** -0.5)).astype(BF16)
            dqkv_r[rs, pair_cols(2, hp)] = dvl
            vacc[7, :, pair_cols(0, hp)] += fold8(dql.astype(F32))
            vacc[7, :, pair_cols(1, hp)] += fold8(dvl.astype(F32))
            return 0

        steps_at(s, [], [], [(6, 0)])
        lax.fori_loop(0, npair, pair, 0)
        steps_at(
            s,
            [(1, 0), (2, 0)],
            [(5, 0), (2, 1)],
            [(5, 1), (2, 2)],
        )
        ps_start(1, s, lambda h: sum(
            mm(dqkv_r[rs, c * LW:(c + 1) * LW], wqkv[c, half_cols(h), :], NT) for c in range(3)
        ))

        @pl.when(s == 0)
        def _():
            grad_tiles(5, 8, c_r, dpre_r, 4)

        return 0

    lax.fori_loop(0, S, phase_d, 0)
    grad_tiles(8, 9, sl_r, heads_r, 8)
    grad_tiles(9, 10, a_r, dqkv_r, 9)
    steps((7, 0))
    grad_tiles(10, 12, a_r, dqkv_r, 9)
    steps((6, 1), (4, 2))

    def phase_e(s, _):
        ps_forward(1, s)
        steps_at(s, [], [(8, 0), (7, 1), (3, 1)], [])
        ps_finish(1, s)

        def lnb(i, _):
            m = mask_rows(s, i)
            hat, r = norm_stats(tok[blk(s, i), :].astype(F32) * m)
            dy = ps_total(1, s, i)
            vacc[0] += fold8(dy * hat)
            vacc[1] += fold8(dy)
            dg = dy * vec_ref[0:1, :]
            m1 = jnp.mean(dg, axis=-1, keepdims=True)
            m2 = jnp.mean(dg * hat, axis=-1, keepdims=True)
            seed_r[blk(s, i), :] = (seed_r[blk(s, i), :] + r * (dg - m1 - hat * m2)) * m
            return 0

        chunks(lnb)

        steps_at(
            s,
            [(5, 2), (1, 2)],
            [(6, 2)],
            [(9, 0), (3, 2)],
        )
        return 0

    lax.fori_loop(0, S, phase_e, 0)

    for j in range(8):
        vst[0, j:j + 1, :] = jnp.sum(vacc[j], axis=0, keepdims=True)

    def cp_v(j):
        return pltpu.make_async_remote_copy(
            src_ref=vst.at[j], dst_ref=vrc.at[j], send_sem=v_s.at[j], recv_sem=v_r.at[j],
            device_id=flip((j + 1) % NBITS), device_id_type=MESH,
        )

    def step_v(j):
        cp_v(j).wait()
        total = vst[j] + vrc[j]
        if j + 1 < NBITS:
            vst[j + 1] = total
            cp_v(j + 1).start()
        else:
            vout_ref[...] = total

    cp_v(0).start()
    steps((8, 1), (7, 2))
    step_v(0)
    steps((10, 0), (9, 1), (8, 2))
    for j in range(1, NBITS - 1):
        step_v(j)
    steps((11, 0), (10, 1), (9, 2), (11, 1))
    step_v(NBITS - 1)
    steps((10, 2), (11, 2))
    def drain(tile, _):
        for j in range(NBITS):
            cp_g(tile, j).wait_send()
        return 0

    lax.fori_loop(0, T, drain, 0)


def finish(loss_in, v_in, *refs):
    ins, refs = refs[:6], refs[6:]
    loss_o, ln1g_o, ln1b_o, bqv_o, bproj_o, ln2g_o, ln2b_o, bfc1_o, bfc2_o = refs[:9]
    outs, sem = refs[9:15], refs[15]
    moves = [pltpu.make_async_copy(src, dst, sem.at[i]) for i, (src, dst) in enumerate(zip(ins, outs))]
    for c in moves:
        c.start()
    for i in range(loss_in.shape[0]):
        loss_o[i] = loss_in[i]
    for j, ref in enumerate([ln1g_o, ln1b_o, bproj_o, ln2g_o, ln2b_o, bfc1_o, bfc2_o]):
        ref[...] = v_in[j]
    lw = bqv_o.shape[1]
    bqv_o[0:1, :] = v_in[7:8, 0:lw]
    bqv_o[1:2, :] = v_in[7:8, lw:2 * lw]
    for c in moves:
        c.wait()


def body(
    n_dp,
    tokens, kept, teacher, out_grad, ln1_gain, ln1_bias, w_qkv, bias_qv, w_proj, bias_proj,
    ln2_gain, ln2_bias, w_fc1, bias_fc1, w_fc2, bias_fc2,
):
    rows = tokens.shape[0]
    S = rows // SLOTS
    LW = w_qkv.shape[2]
    FW = w_fc1.shape[1]
    CH = D // n_dp
    NBITS = n_dp.bit_length() - 1
    T = (2 * FW + 4 * LW) // 256
    cfg = (S, n_dp, NBITS, CH, FW)
    any_spec = pl.BlockSpec(memory_space=pl.ANY)
    vm = pl.BlockSpec(memory_space=pltpu.VMEM)
    sm = pl.BlockSpec(memory_space=pltpu.SMEM)
    sds = jax.ShapeDtypeStruct
    DMA = pltpu.SemaphoreType.DMA
    V = pltpu.VMEM
    big = [
        ((rows, D), BF16), ((rows, D), F32), ((FW, CH), F32), ((CH, FW), F32), ((LW, CH), F32), ((3, CH, LW), F32),
    ]
    out, tg, loss, vout, *grads = pl.pallas_call(
        functools.partial(kernel, cfg),
        out_shape=[V(*big[0]), V(*big[1]), sds((S,), F32), V((8, D), F32)] + [V(*b) for b in big[2:]],
        in_specs=[sm] + [vm] * 8 + [any_spec] * 7,
        out_specs=[vm, vm, sm, vm] + [vm] * 4,
        scratch_shapes=[
            V((3, D, LW), BF16), V((LW, D), BF16), V((D, FW), BF16), V((FW, D), BF16),
            V((rows, D), BF16), V((rows, D), BF16),
            V((rows, D), BF16), V((rows, 3 * LW), BF16), V((rows, LW), BF16), V((rows, D), BF16),
            V((rows, D), F32), V((rows, FW), BF16), V((rows, FW), F32),
            V((rows, D), BF16), V((rows, FW), BF16), V((rows, 3 * LW), BF16),
            V((S, SLOTS, HALF), BF16), V((S, SLOTS, HALF), BF16), V((2, S, 2, 2, SLOTS, HALF), BF16),
            V((T, n_dp, CH, 256), BF16), V((T, n_dp - 1, CH, 256), BF16),
            V((8, D), F32), V((8, D), F32), V((8, 8, D), F32), V((NBITS, 8, D), F32), V((NBITS, 8, D), F32),
            DMA((6 + S,)), DMA((2, S, 4)), DMA((2, S, 4)), DMA((T, NBITS)), DMA((T, NBITS)),
            DMA((NBITS,)), DMA((NBITS,)),
        ],
        compiler_params=pltpu.CompilerParams(
            collective_id=0, has_side_effects=True, vmem_limit_bytes=56 * 2**20
        ),
        name="layer",
    )(
        kept, ln1_gain, ln1_bias, bias_proj, ln2_gain, ln2_bias, bias_fc1, bias_fc2, bias_qv,
        tokens, teacher, out_grad, w_qkv.transpose(1, 0, 2), w_proj, w_fc1, w_fc2,
    )
    vd = sds((D,), F32)
    loss, g_ln1g, g_ln1b, g_bqv, g_bproj, g_ln2g, g_ln2b, g_bfc1, g_bfc2, out, token_grad, g_wfc2, g_wfc1, g_wproj, g_wqkv = (
        pl.pallas_call(
            finish,
            out_shape=[sds((S,), F32), vd, vd, sds((2, LW), F32), vd, vd, vd, sds((FW,), F32), vd]
            + [sds(*b) for b in big],
            in_specs=[sm, vm] + [vm] * 6,
            out_specs=[sm] + [vm] * 8 + [any_spec] * 6,
            scratch_shapes=[DMA((6,))],
            compiler_params=pltpu.CompilerParams(vmem_limit_bytes=16 * 2**20),
            name="finish",
        )(loss, vout, out, tg, *grads)
    )
    return (
        out, loss, token_grad, g_ln1g, g_ln1b, g_wqkv.transpose(1, 0, 2), g_bqv, g_wproj, g_bproj, g_ln2g, g_ln2b,
        g_wfc1, g_bfc1, g_wfc2, g_bfc2,
    )


def solution(mesh):
    tp = P("tensor")
    in_specs = (
        P("dp", None), P(), P("dp", None), P("dp", None), P(), P(), P(None, None, "tensor"),
        P(None, "tensor"), P("tensor", None), P(), P(), P(), P(None, "tensor"), tp, P("tensor", None), P(),
    )
    out_specs = (
        P("dp", None), P("dp"), P("dp", None), P(), P(), P("dp", None, "tensor"), P(None, "tensor"),
        P("tensor", "dp"), P(), P(), P(), P("dp", "tensor"), tp, P("tensor", "dp"), P(),
    )
    return jax.shard_map(
        functools.partial(body, mesh.shape["dp"]), mesh=mesh, in_specs=in_specs, out_specs=out_specs,
        check_vma=False,
    )
```

```python
import functools

import jax
import jax.numpy as jnp
from jax import lax
from jax.experimental import pallas as pl
from jax.experimental.pallas import tpu as pltpu
from jax.sharding import PartitionSpec as P

D = 1024
H = 16
HEAD = D // H
BUFFER = 64
SLOTS = 320
HALF = D // 2
RB = 32
EPS = 1e-06
F32 = jnp.float32
BF16 = jnp.bfloat16
MESH = pl.DeviceIdType.MESH
NT = (((1,), (1,)), ((), ()))
TN = (((0,), (0,)), ((), ()))
NN = (((1,), (0,)), ((), ()))
INV_SQRT2 = 0.7071067811865476
INV_SQRT_2PI = 0.3989422804014327


def mm(a, b, dims):
    return lax.dot_general(a, b, dims, preferred_element_type=F32)


def fold8(x):
    return jnp.sum(x.reshape(x.shape[0] // 8, 8, x.shape[1]), axis=0)


def kernel(
    cfg,
    kept_ref, ln1g_in, ln1b_in, bproj_in, ln2g_in, ln2b_in, bfc1_in, bfc2_in, bqv_in,
    tok_in, tea_in, og_in, wqkv_in, wproj_in, wfc1_in, wfc2_in,
    tea, seed_r, vout_ref, gfc2_r, gfc1_r, gproj_r, gqkv_r,
    wqkv, wproj, wfc1, wfc2, tok, og,
    a_r, qkv_r, heads_r, c_r, h1_r, act_r, gp_r, sl_r, dpre_r, dqkv_r,
    core_s, core_r, tot, gs, rb, vec_ref, lacc, loss_r, vacc, vst, vrc,
    in_sem, ps_s, ps_r, g_s, g_r, v_s, v_r,
):
    S, NDP, NBITS, CH, FW = cfg
    LW = wproj.shape[0]
    R = SLOTS
    rows_all = S * R
    dp = lax.axis_index("dp")
    t = lax.axis_index("tensor")
    lo = lax.rem(t, 2)
    hi = t // 2
    sib = (dp, hi * 2 + (1 - lo))
    xn = (dp, (1 - hi) * 2 + lo)
    bits = [lax.rem(dp // (1 << b), 2) for b in range(NBITS)]

    def flip(b):
        return (dp + (1 << b) * (1 - 2 * bits[b]), t)

    bar = pltpu.get_barrier_semaphore()
    for peer in [sib, xn] + [flip(b) for b in range(NBITS)]:
        pl.semaphore_signal(bar, inc=1, device_id=peer, device_id_type=MESH)

    def in_copy(i, src, dst):
        return pltpu.make_async_copy(src, dst, in_sem.at[i])

    def tok_copy(s):
        rows = pl.ds(pl.multiple_of(s * R, 64), R)
        return pltpu.make_async_copy(tok_in.at[rows, :], tok.at[rows, :], in_sem.at[6 + s])

    ins = [
        in_copy(0, wqkv_in, wqkv),
        in_copy(1, wproj_in, wproj),
        in_copy(2, wfc1_in, wfc1),
        in_copy(3, wfc2_in, wfc2),
        in_copy(4, tea_in, tea),
        in_copy(5, og_in, og),
    ]
    tok_copy(0).start()
    ins[0].start()
    ins[1].start()
    for j, ref in enumerate([ln1g_in, ln1b_in, bproj_in, ln2g_in, ln2b_in, bfc1_in, bfc2_in]):
        vec_ref[j:j + 1, :] = ref[...].astype(F32).reshape(1, ref.shape[0])
    vec_ref[7:8, :] = jnp.zeros((1, D), F32)
    bqv = bqv_in[...].astype(F32)
    vec_ref[7:8, 0:LW] = bqv[0:1]
    vec_ref[7:8, 2 * LW:3 * LW] = bqv[1:2]
    vacc[...] = jnp.zeros_like(vacc)
    count = lax.fori_loop(
        0, kept_ref.shape[0], lambda i, acc: acc + (kept_ref[i] + BUFFER).astype(F32), jnp.float32(0.0)
    )

    def length(s):
        return kept_ref[dp * S + s] + BUFFER

    def mask_rows(s, i):
        idx = lax.broadcasted_iota(jnp.int32, (RB, 1), 0) + i * RB
        return (idx < length(s)).astype(F32)

    def seq_rows(s):
        return pl.ds(pl.multiple_of(s * R, 64), R)

    def chunks(fn, init=0):
        return lax.fori_loop(0, R // RB, fn, init, unroll=5)

    def blk(s, i):
        return pl.ds(pl.multiple_of(s * R + i * RB, RB), RB)

    def loc(i):
        return pl.ds(pl.multiple_of(i * RB, RB), RB)

    def norm_stats(x):
        mean = jnp.mean(x, axis=-1, keepdims=True)
        off = x - mean
        var = jnp.mean(off * off, axis=-1, keepdims=True)
        r = lax.rsqrt(var + EPS)
        return off * r, r

    def cp(p, s, kind, src, dst, dev):
        return pltpu.make_async_remote_copy(
            src_ref=src, dst_ref=dst,
            send_sem=ps_s.at[p, s, kind], recv_sem=ps_r.at[p, s, kind],
            device_id=dev, device_id_type=MESH,
        )

    def cp_core(p, s):
        return cp(p, s, 0, core_s.at[s], core_r.at[s], sib)

    def cp_x(p, s):
        ref = tot.at[p, s, lo, hi]
        return cp(p, s, 1, ref, ref, xn)

    def cp_f1(p, s):
        ref = tot.at[p, s, lo, hi]
        return cp(p, s, 2, ref, ref, sib)

    def cp_f2(p, s):
        ref = tot.at[p, s, lo, 1 - hi]
        return cp(p, s, 3, ref, ref, sib)

    def ps_start(p, s, part):
        core_s[s] = part(1 - lo).astype(BF16)
        cp_core(p, s).start()
        own = part(lo).astype(BF16).astype(F32)
        cp_core(p, s).wait_recv()
        tot[p, s, lo, hi] = (own + core_r[s].astype(F32)).astype(BF16)
        cp_x(p, s).start()
        cp_f1(p, s).start()

    def ps_forward(p, s):
        cp_core(p, s).wait_send()
        cp_x(p, s).wait()
        cp_f2(p, s).start()

    def ps_finish(p, s):
        cp_f1(p, s).wait()
        cp_f2(p, s).wait()

    def ps_total(p, s, i):
        rr = loc(i)
        parts = [
            tot[p, s, h, 0, rr, :].astype(F32) + tot[p, s, h, 1, rr, :].astype(F32) for h in range(2)
        ]
        return jnp.concatenate(parts, axis=1)

    def half_cols(h):
        return pl.ds(pl.multiple_of(h * HALF, HALF), HALF)

    lane_half = lax.broadcasted_iota(jnp.int32, (1, 2 * HEAD), 1) // HEAD

    def head_mask(hh, scale=1.0):
        return ((lane_half == hh).astype(F32) * scale).astype(BF16)

    SCALE = HEAD ** -0.5

    def pair_cols(c, hp):
        return pl.ds(pl.multiple_of(c * LW + hp * 2 * HEAD, 2 * HEAD), 2 * HEAD)

    def probs_of(qm, k, s):
        sc = mm(qm, k, NT)
        col = lax.broadcasted_iota(jnp.int32, (1, R), 1)
        sc = jnp.where(col < length(s), sc, -1e30)
        top = jnp.max(sc, axis=-1, keepdims=True)
        e = jnp.exp(sc - top)
        return e * (1.0 / jnp.sum(e, axis=-1, keepdims=True))

    npair = LW // (2 * HEAD)

    def swapped(tile):
        if isinstance(tile, int):
            return int(tile in (1, 3))
        return lax.rem(tile, 2) * ((T - tile) // (T - 3))

    def mix(f, p, q):
        return p + f * (q - p)

    def place(d, f):
        db = [(d >> b) & 1 for b in range(NBITS)]
        pos = sum(db[b] << (NBITS - 1 - b) for b in range(2, NBITS))
        if NBITS > 1:
            return pos + mix(f, db[0], db[1]) * (NDP // 2) + mix(f, db[1], db[0]) * (NDP // 4)
        return db[0]

    def stage_bit(f, j):
        if NBITS > 1 and j < 2:
            return mix(f, bits[j], bits[1 - j])
        return bits[j]

    def stage_peer(f, j):
        if NBITS > 1 and j < 2:
            step = [(1 << b) * (1 - 2 * bits[b]) for b in range(2)]
            return (dp + mix(f, step[j], step[1 - j]), t)
        return flip(j)

    def base(f, j):
        return sum((stage_bit(f, i) * (NDP >> (i + 1)) for i in range(j)), 0)

    def land(j):
        return NDP - (NDP >> j)

    def room(tile):
        if isinstance(tile, int) and tile >= T - 1:
            return T - 1, slice((tile - T + 1) * 128, (tile - T + 2) * 128)
        return tile, slice(0, 256)

    def cp_g(tile, j):
        f = swapped(tile)
        at, cols = room(tile)
        n = NDP >> (j + 1)
        first = base(f, j) + (1 - stage_bit(f, j)) * n
        return pltpu.make_async_remote_copy(
            src_ref=gs.at[at, pl.ds(first, n), :, cols], dst_ref=rb.at[at, land(j):land(j) + n, :, cols],
            send_sem=g_s.at[tile, j], recv_sem=g_r.at[tile, j],
            device_id=stage_peer(f, j), device_id_type=MESH,
        )

    def grad_tile(tile, lhs, rhs):
        f = swapped(tile)
        val = mm(lhs[...], rhs, TN).astype(BF16)
        for d in range(NDP):
            gs[tile, place(d, f)] = val[d * CH:(d + 1) * CH]
        cp_g(tile, 0).start()
        if isinstance(tile, int) and tile == T - 1:
            cp_g(T, 0).start()

    def grad_tiles(first, last, lhs, rhs, skip=0):
        def one(k, _):
            grad_tile(k, lhs, rhs[:, pl.ds(pl.multiple_of((k - skip) * 256, 256), 256)])
            return 0

        lax.fori_loop(first, last, one, 0)

    def advance(tile, j):
        f = swapped(tile)
        cp_g(tile, j).wait_recv()
        n = NDP >> (j + 1)
        mine = base(f, j + 1)

        at, cols = room(tile)
        if j + 1 < NBITS:
            def add(i, _):
                gs[at, mine + i, :, cols] = gs[at, mine + i, :, cols] + rb[at, land(j) + i, :, cols]
                return 0

            lax.fori_loop(0, n, add, 0)
            cp_g(tile, j + 1).start()
            return
        val = gs[at, mine, :, cols].astype(F32) + rb[at, land(j), :, cols].astype(F32)
        if at < NT1:
            gfc2_r[at * 256:(at + 1) * 256, :] = val.T
        elif at < 2 * NT1:
            gfc1_r[:, (at - NT1) * 256:(at - NT1 + 1) * 256] = val
        elif at < 2 * NT1 + NT2:
            gproj_r[(at - 2 * NT1) * 256:(at - 2 * NT1 + 1) * 256, :] = val.T
        else:
            k = at - 2 * NT1 - NT2
            first = (k % NT2) * 256 + cols.start
            gqkv_r[k // NT2, :, first:first + cols.stop - cols.start] = val

    def steps(*pairs):
        for tile, j in pairs:
            for i in range(j, NBITS if j == 2 else j + 1):
                advance(tile, i)

    def steps_at(s, *lists):
        for at, pairs in enumerate(lists):
            if pairs:
                @pl.when(s == at)
                def _():
                    steps(*pairs)

    NT1 = FW // 256
    NT2 = LW // 256
    T = 2 * NT1 + 4 * NT2

    def phase_a(s, _):
        tok_copy(s).wait()

        def ln(i, _):
            x = tok[blk(s, i), :].astype(F32) * mask_rows(s, i)
            hat, _r = norm_stats(x)
            a_r[blk(s, i), :] = (hat * vec_ref[0:1, :] + vec_ref[1:2, :]).astype(BF16)
            return 0

        chunks(ln)

        @pl.when(s == 0)
        def _():
            ins[0].wait()

            def tok_start(i, _):
                tok_copy(i).start()
                return 0

            lax.fori_loop(1, S, tok_start, 0)
            for c in ins[2:]:
                c.start()

        rs = seq_rows(s)
        av = a_r[rs, :]
        for c in range(3):
            cs = slice(c * LW, (c + 1) * LW)
            qkv_r[rs, cs] = (mm(av, wqkv[c], NN) + vec_ref[7:8, cs]).astype(BF16)

        def pair(hp, _):
            q = qkv_r[rs, pair_cols(0, hp)]
            k = qkv_r[rs, pair_cols(1, hp)]
            v = qkv_r[rs, pair_cols(2, hp)]
            o = None
            for hh in range(2):
                pr = probs_of(q * head_mask(hh, SCALE), k, s).astype(BF16)
                oh = mm(pr, v * head_mask(hh), NN)
                o = oh if o is None else o + oh
            heads_r[rs, pair_cols(0, hp)] = o.astype(BF16)
            return 0

        lax.fori_loop(0, npair, pair, 0)
        hv = heads_r[rs, :]

        @pl.when(s == 0)
        def _():
            ins[1].wait()
            pl.semaphore_wait(bar, 2 + NBITS)

        ps_start(0, s, lambda h: mm(hv, wproj[:, half_cols(h)], NN))
        return 0

    lax.fori_loop(0, S, phase_a, 0)

    ps_forward(0, 0)

    ins[2].wait()
    ins[3].wait()

    def phase_b(s, _):
        ps_finish(0, s)

        def ln(i, _):
            x = tok[blk(s, i), :].astype(F32) * mask_rows(s, i)
            h1 = x + ps_total(0, s, i) + vec_ref[2:3, :]
            h1_r[blk(s, i), :] = h1
            hat, _r = norm_stats(h1)
            c_r[blk(s, i), :] = (hat * vec_ref[3:4, :] + vec_ref[4:5, :]).astype(BF16)
            return 0

        chunks(ln)
        rs = seq_rows(s)
        cv = c_r[rs, :]

        def fc1(j, _):
            cs = pl.ds(pl.multiple_of(j * 256, 256), 256)
            pre = mm(cv, wfc1[:, cs], NN) + vec_ref[5:6, cs]
            phi = 0.5 * (1.0 + lax.erf(pre * INV_SQRT2))
            act_r[rs, cs] = (pre * phi).astype(BF16)
            gp_r[rs, cs] = phi + pre * (INV_SQRT_2PI * jnp.exp(-0.5 * pre * pre))
            return 0

        lax.fori_loop(0, FW // 256, fc1, 0)
        @pl.when(s + 1 < S)
        def _():
            ps_forward(0, s + 1)

        @pl.when(s + 1 == S)
        def _():
            ps_forward(1, 0)

        ps_start(1, s, lambda h: mm(act_r[rs, :], wfc2[:, half_cols(h)], NN))
        return 0

    lax.fori_loop(0, S, phase_b, 0)

    ins[4].wait()
    ins[5].wait()
    loss_scale = kept_ref.shape[0] / (2.0 * count * D)
    seed_scale = kept_ref.shape[0] * SLOTS * 1.0 / count

    loss_r[...] = jnp.zeros_like(loss_r)

    def phase_c(s, _):
        lacc[...] = jnp.zeros_like(lacc)

        def fin(h):
            hc = half_cols(h)

            def one(i, _):
                m = mask_rows(s, i)
                mlp = tot[1, s, h, 0, loc(i), :].astype(F32) + tot[1, s, h, 1, loc(i), :].astype(F32)
                final = (h1_r[blk(s, i), hc] + mlp + vec_ref[6:7, hc]) * m
                diff = (final - tea[blk(s, i), hc].astype(F32)) * m
                seed = (og[blk(s, i), hc].astype(F32) + diff * seed_scale) * m
                tea[blk(s, i), hc] = final.astype(BF16)
                seed_r[blk(s, i), hc] = seed
                sl_r[blk(s, i), hc] = seed.astype(BF16)
                lacc[...] += fold8(diff * diff)
                vacc[6, :, hc] += fold8(seed)
                return 0

            chunks(one)

        fin(lo)
        ps_finish(1, s)
        fin(1 - lo)
        here = (lax.broadcasted_iota(jnp.int32, (1, D), 1) == s).astype(F32)
        loss_r[...] += here * (jnp.sum(lacc[...]) * loss_scale)
        rs = seq_rows(s)
        sv = sl_r[rs, :]

        @pl.when(s == S - 1)
        def _():
            grad_tiles(0, 2, sl_r, act_r)


        def dact(j, _):
            cs = pl.ds(pl.multiple_of(j * 256, 256), 256)
            d = mm(sv, wfc2[cs, :], NT) * gp_r[rs, cs]
            dl = d.astype(BF16)
            dpre_r[rs, cs] = dl
            vacc[5, :, cs] += fold8(dl.astype(F32))
            return 0

        lax.fori_loop(0, FW // 256, dact, 0)
        ps_start(0, s, lambda h: mm(dpre_r[rs, :], wfc1[half_cols(h), :], NT))

        @pl.when(s + 1 < S)
        def _():
            ps_forward(1, s + 1)

        return 0

    lax.fori_loop(0, S, phase_c, 0)

    grad_tiles(2, 4, sl_r, act_r)
    grad_tiles(4, 5, c_r, dpre_r, 4)
    ps_forward(0, 0)

    def phase_d(s, _):
        ps_finish(0, s)

        def lnb(i, _):
            hat, r = norm_stats(h1_r[blk(s, i), :])
            dy = ps_total(0, s, i)
            vacc[3] += fold8(dy * hat)
            vacc[4] += fold8(dy)
            dg = dy * vec_ref[3:4, :]
            m1 = jnp.mean(dg, axis=-1, keepdims=True)
            m2 = jnp.mean(dg * hat, axis=-1, keepdims=True)
            dh1 = seed_r[blk(s, i), :] + r * (dg - m1 - hat * m2)
            seed_r[blk(s, i), :] = dh1
            vacc[2] += fold8(dh1)
            sl_r[blk(s, i), :] = dh1.astype(BF16)
            return 0

        chunks(lnb)
        rs = seq_rows(s)

        def pair(hp, _):
            wc = pl.ds(pl.multiple_of(hp * 2 * HEAD, 2 * HEAD), 2 * HEAD)
            dh = mm(sl_r[rs, :], wproj[wc, :], NT).astype(BF16)
            q = qkv_r[rs, pair_cols(0, hp)]
            k = qkv_r[rs, pair_cols(1, hp)]
            v = qkv_r[rs, pair_cols(2, hp)]
            dq = dk = dv = None
            for hh in range(2):
                hm = head_mask(hh)
                qm, km, dm = q * head_mask(hh, SCALE), k * hm, dh * hm
                pr = probs_of(qm, k, s)
                dpr = mm(dm, v, NT)
                ds = (pr * (dpr - jnp.sum(pr * dpr, axis=-1, keepdims=True))).astype(BF16)
                q1, k1, v1 = mm(ds, km, NN), mm(ds, qm, TN), mm(pr.astype(BF16), dm, TN)
                if dq is None:
                    dq, dk, dv = q1, k1, v1
                else:
                    dq, dk, dv = dq + q1, dk + k1, dv + v1
            dql = (dq * SCALE).astype(BF16)
            dvl = dv.astype(BF16)
            dqkv_r[rs, pair_cols(0, hp)] = dql
            dqkv_r[rs, pair_cols(1, hp)] = dk.astype(BF16)
            dqkv_r[rs, pair_cols(2, hp)] = dvl
            vacc[7, :, pair_cols(0, hp)] += fold8(dql.astype(F32))
            vacc[7, :, pair_cols(1, hp)] += fold8(dvl.astype(F32))
            return 0

        steps_at(
            s,
            [(0, 0)],
            [(4, 0), (3, 0), (0, 1)],
            [(5, 0), (4, 1), (1, 1), (0, 2)],
        )
        lax.fori_loop(0, npair, pair, 0, unroll=True)
        steps_at(
            s,
            [(1, 0), (2, 0)],
            [(2, 1)],
            [(6, 0), (5, 1), (2, 2)],
        )
        @pl.when(s + 1 < S)
        def _():
            ps_forward(0, s + 1)

        @pl.when(s + 1 == S)
        def _():
            ps_forward(1, 0)

        ps_start(1, s, lambda h: sum(
            mm(dqkv_r[rs, c * LW:(c + 1) * LW], wqkv[c, half_cols(h), :], NT) for c in range(3)
        ))

        @pl.when(s == 0)
        def _():
            grad_tiles(5, 8, c_r, dpre_r, 4)

        return 0

    lax.fori_loop(0, S, phase_d, 0)
    grad_tiles(8, 9, sl_r, heads_r, 8)
    grad_tiles(9, 10, a_r, dqkv_r, 9)
    steps((7, 0))
    grad_tiles(10, 11, a_r, dqkv_r, 9)
    grad_tile(11, a_r, dqkv_r[:, 2 * 256:3 * 256])
    steps((6, 1), (4, 2))

    def phase_e(s, _):
        steps_at(s, [], [(8, 0), (7, 1), (3, 1)], [])
        ps_finish(1, s)

        def lnb(i, _):
            m = mask_rows(s, i)
            hat, r = norm_stats(tok[blk(s, i), :].astype(F32) * m)
            dy = ps_total(1, s, i)
            vacc[0] += fold8(dy * hat)
            vacc[1] += fold8(dy)
            dg = dy * vec_ref[0:1, :]
            m1 = jnp.mean(dg, axis=-1, keepdims=True)
            m2 = jnp.mean(dg * hat, axis=-1, keepdims=True)
            seed_r[blk(s, i), :] = (seed_r[blk(s, i), :] + r * (dg - m1 - hat * m2)) * m
            return 0

        chunks(lnb)

        @pl.when(s + 1 < S)
        def _():
            ps_forward(1, s + 1)

        steps_at(
            s,
            [(5, 2), (1, 2)],
            [(6, 2)],
            [(9, 0), (3, 2)],
        )
        return 0

    lax.fori_loop(0, S, phase_e, 0)

    for j in range(8):
        vst[0, j:j + 1, :] = jnp.sum(vacc[j], axis=0, keepdims=True)

    def cp_v(j):
        return pltpu.make_async_remote_copy(
            src_ref=vst.at[j], dst_ref=vrc.at[j], send_sem=v_s.at[j], recv_sem=v_r.at[j],
            device_id=flip((j + 1) % NBITS), device_id_type=MESH,
        )

    def step_v(j):
        cp_v(j).wait()
        total = vst[j] + vrc[j]
        if j + 1 < NBITS:
            vst[j + 1] = total
            cp_v(j + 1).start()
        else:
            vout_ref[0:8, :] = total
            vout_ref[8:9, :] = loss_r[...]

    cp_v(0).start()
    steps((8, 1), (7, 2), (10, 0), (9, 1))
    step_v(0)
    steps((11, 0), (10, 1), (8, 2))
    for j in range(1, NBITS - 1):
        step_v(j)
    steps((12, 0), (11, 1), (12, 1), (9, 2), (10, 2))
    step_v(NBITS - 1)
    steps((11, 2), (12, 2))

    def drain(tile, _):
        for j in range(NBITS):
            cp_g(tile, j).wait_send()
        return 0

    lax.fori_loop(0, T - 1, drain, 0)
    drain(T - 1, 0)
    drain(T, 0)


def finish(v_in, *refs):
    ins, refs = refs[:6], refs[6:]
    loss_o, ln1g_o, ln1b_o, bqv_o, bproj_o, ln2g_o, ln2b_o, bfc1_o, bfc2_o = refs[:9]
    outs, sem = refs[9:15], refs[15]
    moves = [pltpu.make_async_copy(src, dst, sem.at[i]) for i, (src, dst) in enumerate(zip(ins, outs))]
    for c in moves:
        c.start()
    for i in range(loss_o.shape[0]):
        loss_o[i] = v_in[8, i]
    for j, ref in enumerate([ln1g_o, ln1b_o, bproj_o, ln2g_o, ln2b_o, bfc1_o, bfc2_o]):
        ref[...] = v_in[j]
    lw = bqv_o.shape[1]
    bqv_o[0:1, :] = v_in[7:8, 0:lw]
    bqv_o[1:2, :] = v_in[7:8, lw:2 * lw]
    for c in moves:
        c.wait()


def body(
    n_dp,
    tokens, kept, teacher, out_grad, ln1_gain, ln1_bias, w_qkv, bias_qv, w_proj, bias_proj,
    ln2_gain, ln2_bias, w_fc1, bias_fc1, w_fc2, bias_fc2,
):
    rows = tokens.shape[0]
    S = rows // SLOTS
    LW = w_qkv.shape[2]
    FW = w_fc1.shape[1]
    CH = D // n_dp
    NBITS = n_dp.bit_length() - 1
    T = (2 * FW + 4 * LW) // 256
    cfg = (S, n_dp, NBITS, CH, FW)
    any_spec = pl.BlockSpec(memory_space=pl.ANY)
    vm = pl.BlockSpec(memory_space=pltpu.VMEM)
    sm = pl.BlockSpec(memory_space=pltpu.SMEM)
    sds = jax.ShapeDtypeStruct
    DMA = pltpu.SemaphoreType.DMA
    V = pltpu.VMEM
    big = [
        ((rows, D), BF16), ((rows, D), F32), ((FW, CH), F32), ((CH, FW), F32), ((LW, CH), F32), ((3, CH, LW), F32),
    ]
    out, tg, vout, *grads = pl.pallas_call(
        functools.partial(kernel, cfg),
        out_shape=[V(*big[0]), V(*big[1]), V((16, D), F32)] + [V(*b) for b in big[2:]],
        in_specs=[sm] + [vm] * 8 + [any_spec] * 7,
        out_specs=[vm] * 7,
        scratch_shapes=[
            V((3, D, LW), BF16), V((LW, D), BF16), V((D, FW), BF16), V((FW, D), BF16),
            V((rows, D), BF16), V((rows, D), BF16),
            V((rows, D), BF16), V((rows, 3 * LW), BF16), V((rows, LW), BF16), V((rows, D), BF16),
            V((rows, D), F32), V((rows, FW), BF16), V((rows, FW), F32),
            V((rows, D), BF16), V((rows, FW), BF16), V((rows, 3 * LW), BF16),
            V((S, SLOTS, HALF), BF16), V((S, SLOTS, HALF), BF16), V((2, S, 2, 2, SLOTS, HALF), BF16),
            V((T, n_dp, CH, 256), BF16), V((T, n_dp - 1, CH, 256), BF16),
            V((8, D), F32), V((8, HALF), F32), V((1, D), F32), V((8, 8, D), F32), V((NBITS, 8, D), F32), V((NBITS, 8, D), F32),
            DMA((6 + S,)), DMA((2, S, 4)), DMA((2, S, 4)), DMA((T + 1, NBITS)), DMA((T + 1, NBITS)),
            DMA((NBITS,)), DMA((NBITS,)),
        ],
        compiler_params=pltpu.CompilerParams(
            collective_id=0, has_side_effects=True, vmem_limit_bytes=56 * 2**20
        ),
        name="layer",
    )(
        kept, ln1_gain, ln1_bias, bias_proj, ln2_gain, ln2_bias, bias_fc1, bias_fc2, bias_qv,
        tokens, teacher, out_grad, w_qkv.transpose(1, 0, 2), w_proj, w_fc1, w_fc2,
    )
    vd = sds((D,), F32)
    loss, g_ln1g, g_ln1b, g_bqv, g_bproj, g_ln2g, g_ln2b, g_bfc1, g_bfc2, out, token_grad, g_wfc2, g_wfc1, g_wproj, g_wqkv = (
        pl.pallas_call(
            finish,
            out_shape=[sds((S,), F32), vd, vd, sds((2, LW), F32), vd, vd, vd, sds((FW,), F32), vd]
            + [sds(*b) for b in big],
            in_specs=[vm] * 7,
            out_specs=[sm] + [vm] * 8 + [any_spec] * 6,
            scratch_shapes=[DMA((6,))],
            compiler_params=pltpu.CompilerParams(vmem_limit_bytes=16 * 2**20),
            name="finish",
        )(vout, out, tg, *grads)
    )
    return (
        out, loss, token_grad, g_ln1g, g_ln1b, g_wqkv.transpose(1, 0, 2), g_bqv, g_wproj, g_bproj, g_ln2g, g_ln2b,
        g_wfc1, g_bfc1, g_wfc2, g_bfc2,
    )


def solution(mesh):
    tp = P("tensor")
    in_specs = (
        P("dp", None), P(), P("dp", None), P("dp", None), P(), P(), P(None, None, "tensor"),
        P(None, "tensor"), P("tensor", None), P(), P(), P(), P(None, "tensor"), tp, P("tensor", None), P(),
    )
    out_specs = (
        P("dp", None), P("dp"), P("dp", None), P(), P(), P("dp", None, "tensor"), P(None, "tensor"),
        P("tensor", "dp"), P(), P(), P(), P("dp", "tensor"), tp, P("tensor", "dp"), P(),
    )
    return jax.shard_map(
        functools.partial(body, mesh.shape["dp"]), mesh=mesh, in_specs=in_specs, out_specs=out_specs,
        check_vma=False,
    )
```

```python
import functools

import jax
import jax.numpy as jnp
from jax import lax
from jax.experimental import pallas as pl
from jax.experimental.pallas import tpu as pltpu
from jax.sharding import PartitionSpec as P

D = 1024
H = 16
HEAD = D // H
BUFFER = 64
SLOTS = 320
HALF = D // 2
RB = 32
EPS = 1e-06
F32 = jnp.float32
BF16 = jnp.bfloat16
MESH = pl.DeviceIdType.MESH
NT = (((1,), (1,)), ((), ()))
TN = (((0,), (0,)), ((), ()))
NN = (((1,), (0,)), ((), ()))
INV_SQRT2 = 0.7071067811865476
INV_SQRT_2PI = 0.3989422804014327


def mm(a, b, dims):
    return lax.dot_general(a, b, dims, preferred_element_type=F32)


def fold8(x):
    return jnp.sum(x.reshape(x.shape[0] // 8, 8, x.shape[1]), axis=0)


def kernel(
    cfg,
    kept_ref, ln1g_in, ln1b_in, bproj_in, ln2g_in, ln2b_in, bfc1_in, bfc2_in, bqv_in,
    tok_in, tea_in, og_in, wqkv_in, wproj_in, wfc1_in, wfc2_in,
    tea, seed_r, vout_ref, gfc2_r, gfc1_r, gproj_r, gqkv_r,
    wqkv, wproj, wfc1, wfc2, tok, og,
    a_r, qkv_r, heads_r, c_r, h1_r, act_r, gp_r, sl_r, dpre_r, dqkv_r,
    core_s, core_r, tot, gs, rb, vec_ref, lacc, loss_r, vacc, vst, vrc,
    in_sem, ps_s, ps_r, g_s, g_r, v_s, v_r,
):
    S, NDP, NBITS, CH, FW = cfg
    LW = wproj.shape[0]
    R = SLOTS
    rows_all = S * R
    dp = lax.axis_index("dp")
    t = lax.axis_index("tensor")
    lo = lax.rem(t, 2)
    hi = t // 2
    sib = (dp, hi * 2 + (1 - lo))
    xn = (dp, (1 - hi) * 2 + lo)
    bits = [lax.rem(dp // (1 << b), 2) for b in range(NBITS)]

    def flip(b):
        return (dp + (1 << b) * (1 - 2 * bits[b]), t)

    bar = pltpu.get_barrier_semaphore()
    for peer in [sib, xn] + [flip(b) for b in range(NBITS)]:
        pl.semaphore_signal(bar, inc=1, device_id=peer, device_id_type=MESH)

    def in_copy(i, src, dst):
        return pltpu.make_async_copy(src, dst, in_sem.at[i])

    def tok_copy(s):
        rows = pl.ds(pl.multiple_of(s * R, 64), R)
        return pltpu.make_async_copy(tok_in.at[rows, :], tok.at[rows, :], in_sem.at[6 + s])

    ins = [
        in_copy(0, wqkv_in, wqkv),
        in_copy(1, wproj_in, wproj),
        in_copy(2, wfc1_in, wfc1),
        in_copy(3, wfc2_in, wfc2),
        in_copy(4, tea_in, tea),
        in_copy(5, og_in, og),
    ]
    tok_copy(0).start()
    ins[0].start()
    ins[1].start()
    for j, ref in enumerate([ln1g_in, ln1b_in, bproj_in, ln2g_in, ln2b_in, bfc1_in, bfc2_in]):
        vec_ref[j:j + 1, :] = ref[...].astype(F32).reshape(1, ref.shape[0])
    vec_ref[7:8, :] = jnp.zeros((1, D), F32)
    bqv = bqv_in[...].astype(F32)
    vec_ref[7:8, 0:LW] = bqv[0:1]
    vec_ref[7:8, 2 * LW:3 * LW] = bqv[1:2]
    vacc[...] = jnp.zeros_like(vacc)
    count = lax.fori_loop(
        0, kept_ref.shape[0], lambda i, acc: acc + (kept_ref[i] + BUFFER).astype(F32), jnp.float32(0.0)
    )

    def length(s):
        return kept_ref[dp * S + s] + BUFFER

    def mask_rows(s, i):
        idx = lax.broadcasted_iota(jnp.int32, (RB, 1), 0) + i * RB
        return (idx < length(s)).astype(F32)

    def seq_rows(s):
        return pl.ds(pl.multiple_of(s * R, 64), R)

    def chunks(fn, init=0):
        return lax.fori_loop(0, R // RB, fn, init, unroll=5)

    def blk(s, i):
        return pl.ds(pl.multiple_of(s * R + i * RB, RB), RB)

    def loc(i):
        return pl.ds(pl.multiple_of(i * RB, RB), RB)

    def norm_stats(x):
        mean = jnp.mean(x, axis=-1, keepdims=True)
        off = x - mean
        var = jnp.mean(off * off, axis=-1, keepdims=True)
        r = lax.rsqrt(var + EPS)
        return off * r, r

    def cp(p, s, kind, src, dst, dev):
        return pltpu.make_async_remote_copy(
            src_ref=src, dst_ref=dst,
            send_sem=ps_s.at[p, s, kind], recv_sem=ps_r.at[p, s, kind],
            device_id=dev, device_id_type=MESH,
        )

    def cp_core(p, s):
        return cp(p, s, 0, core_s.at[s], core_r.at[s], sib)

    def cp_x(p, s):
        ref = tot.at[p, s, lo, hi]
        return cp(p, s, 1, ref, ref, xn)

    def cp_f1(p, s):
        ref = tot.at[p, s, lo, hi]
        return cp(p, s, 2, ref, ref, sib)

    def cp_f2(p, s):
        ref = tot.at[p, s, lo, 1 - hi]
        return cp(p, s, 3, ref, ref, sib)

    def ps_start(p, s, part):
        core_s[s] = part(1 - lo).astype(BF16)
        cp_core(p, s).start()
        own = part(lo).astype(BF16).astype(F32)
        cp_core(p, s).wait_recv()
        tot[p, s, lo, hi] = (own + core_r[s].astype(F32)).astype(BF16)
        cp_x(p, s).start()
        cp_f1(p, s).start()

    def ps_forward(p, s):
        cp_core(p, s).wait_send()
        cp_x(p, s).wait()
        cp_f2(p, s).start()

    def ps_finish(p, s):
        cp_f1(p, s).wait()
        cp_f2(p, s).wait()

    def ps_total(p, s, i):
        rr = loc(i)
        parts = [
            tot[p, s, h, 0, rr, :].astype(F32) + tot[p, s, h, 1, rr, :].astype(F32) for h in range(2)
        ]
        return jnp.concatenate(parts, axis=1)

    def half_cols(h):
        return pl.ds(pl.multiple_of(h * HALF, HALF), HALF)

    lane_half = lax.broadcasted_iota(jnp.int32, (1, 2 * HEAD), 1) // HEAD

    def head_mask(hh, scale=1.0):
        return ((lane_half == hh).astype(F32) * scale).astype(BF16)

    SCALE = HEAD ** -0.5

    def pair_cols(c, hp):
        return pl.ds(pl.multiple_of(c * LW + hp * 2 * HEAD, 2 * HEAD), 2 * HEAD)

    def probs_of(qm, k, s):
        sc = mm(qm, k, NT)
        col = lax.broadcasted_iota(jnp.int32, (1, R), 1)
        sc = jnp.where(col < length(s), sc, -1e30)
        top = jnp.max(sc, axis=-1, keepdims=True)
        e = jnp.exp(sc - top)
        return e * (1.0 / jnp.sum(e, axis=-1, keepdims=True))

    npair = LW // (2 * HEAD)

    def swapped(tile):
        if isinstance(tile, int):
            return int(tile in (1, 3))
        return lax.rem(tile, 2) * ((T - tile) // (T - 3))

    def mix(f, p, q):
        return p + f * (q - p)

    def place(d, f):
        db = [(d >> b) & 1 for b in range(NBITS)]
        pos = sum(db[b] << (NBITS - 1 - b) for b in range(2, NBITS))
        if NBITS > 1:
            return pos + mix(f, db[0], db[1]) * (NDP // 2) + mix(f, db[1], db[0]) * (NDP // 4)
        return db[0]

    def stage_bit(f, j):
        if NBITS > 1 and j < 2:
            return mix(f, bits[j], bits[1 - j])
        return bits[j]

    def stage_peer(f, j):
        if NBITS > 1 and j < 2:
            step = [(1 << b) * (1 - 2 * bits[b]) for b in range(2)]
            return (dp + mix(f, step[j], step[1 - j]), t)
        return flip(j)

    def base(f, j):
        return sum((stage_bit(f, i) * (NDP >> (i + 1)) for i in range(j)), 0)

    def land(j):
        return NDP - (NDP >> j)

    def room(tile):
        if isinstance(tile, int) and tile >= T - 1:
            return T - 1, slice((tile - T + 1) * 128, (tile - T + 2) * 128)
        return tile, slice(0, 256)

    def cp_g(tile, j):
        f = swapped(tile)
        at, cols = room(tile)
        n = NDP >> (j + 1)
        first = base(f, j) + (1 - stage_bit(f, j)) * n
        return pltpu.make_async_remote_copy(
            src_ref=gs.at[at, pl.ds(first, n), :, cols], dst_ref=rb.at[at, land(j):land(j) + n, :, cols],
            send_sem=g_s.at[tile, j], recv_sem=g_r.at[tile, j],
            device_id=stage_peer(f, j), device_id_type=MESH,
        )

    def grad_tile(tile, lhs, rhs):
        f = swapped(tile)
        val = mm(lhs[...], rhs, TN).astype(BF16)
        for d in range(NDP):
            gs[tile, place(d, f)] = val[d * CH:(d + 1) * CH]
        if isinstance(tile, int):
            cp_g(tile, 0).start()
            return

        @pl.when(tile < T - 1)
        def _():
            cp_g(tile, 0).start()

        @pl.when(tile == T - 1)
        def _():
            cp_g(T - 1, 0).start()
            cp_g(T, 0).start()

    def grad_tiles(first, last, lhs, rhs, skip=0):
        def one(k, _):
            grad_tile(k, lhs, rhs[:, pl.ds(pl.multiple_of((k - skip) * 256, 256), 256)])
            return 0

        lax.fori_loop(first, last, one, 0)

    def advance(tile, j):
        f = swapped(tile)
        cp_g(tile, j).wait_recv()
        n = NDP >> (j + 1)
        mine = base(f, j + 1)

        at, cols = room(tile)
        if j + 1 < NBITS:
            def add(i, _):
                gs[at, mine + i, :, cols] = gs[at, mine + i, :, cols] + rb[at, land(j) + i, :, cols]
                return 0

            lax.fori_loop(0, n, add, 0)
            cp_g(tile, j + 1).start()
            return
        val = gs[at, mine, :, cols].astype(F32) + rb[at, land(j), :, cols].astype(F32)
        if at < NT1:
            gfc2_r[at * 256:(at + 1) * 256, :] = val.T
        elif at < 2 * NT1:
            gfc1_r[:, (at - NT1) * 256:(at - NT1 + 1) * 256] = val
        elif at < 2 * NT1 + NT2:
            gproj_r[(at - 2 * NT1) * 256:(at - 2 * NT1 + 1) * 256, :] = val.T
        else:
            k = at - 2 * NT1 - NT2
            first = (k % NT2) * 256 + cols.start
            gqkv_r[k // NT2, :, first:first + cols.stop - cols.start] = val

    def steps(*pairs):
        for tile, j in pairs:
            for i in range(j, NBITS if j == 2 else j + 1):
                advance(tile, i)

    def steps_at(s, *lists):
        for at, pairs in enumerate(lists):
            if pairs:
                @pl.when(s == at)
                def _():
                    steps(*pairs)

    NT1 = FW // 256
    NT2 = LW // 256
    T = 2 * NT1 + 4 * NT2

    def phase_a(s, _):
        tok_copy(s).wait()

        def ln(i, _):
            x = tok[blk(s, i), :].astype(F32) * mask_rows(s, i)
            hat, _r = norm_stats(x)
            a_r[blk(s, i), :] = (hat * vec_ref[0:1, :] + vec_ref[1:2, :]).astype(BF16)
            return 0

        chunks(ln)

        @pl.when(s == 0)
        def _():
            ins[0].wait()

            def tok_start(i, _):
                tok_copy(i).start()
                return 0

            lax.fori_loop(1, S, tok_start, 0)
            for c in ins[2:]:
                c.start()

        rs = seq_rows(s)
        av = a_r[rs, :]
        for c in range(3):
            cs = slice(c * LW, (c + 1) * LW)
            qkv_r[rs, cs] = (mm(av, wqkv[c], NN) + vec_ref[7:8, cs]).astype(BF16)

        def pair(hp, _):
            q = qkv_r[rs, pair_cols(0, hp)]
            k = qkv_r[rs, pair_cols(1, hp)]
            v = qkv_r[rs, pair_cols(2, hp)]
            o = None
            for hh in range(2):
                pr = probs_of(q * head_mask(hh, SCALE), k, s).astype(BF16)
                oh = mm(pr, v * head_mask(hh), NN)
                o = oh if o is None else o + oh
            heads_r[rs, pair_cols(0, hp)] = o.astype(BF16)
            return 0

        lax.fori_loop(0, npair, pair, 0)
        hv = heads_r[rs, :]

        @pl.when(s == 0)
        def _():
            ins[1].wait()
            pl.semaphore_wait(bar, 2 + NBITS)

        ps_start(0, s, lambda h: mm(hv, wproj[:, half_cols(h)], NN))
        return 0

    lax.fori_loop(0, S, phase_a, 0)

    ps_forward(0, 0)

    ins[2].wait()
    ins[3].wait()

    def phase_b(s, _):
        ps_finish(0, s)

        def ln(i, _):
            x = tok[blk(s, i), :].astype(F32) * mask_rows(s, i)
            h1 = x + ps_total(0, s, i) + vec_ref[2:3, :]
            h1_r[blk(s, i), :] = h1
            hat, _r = norm_stats(h1)
            c_r[blk(s, i), :] = (hat * vec_ref[3:4, :] + vec_ref[4:5, :]).astype(BF16)
            return 0

        chunks(ln)
        rs = seq_rows(s)
        cv = c_r[rs, :]

        def fc1(j, _):
            cs = pl.ds(pl.multiple_of(j * 256, 256), 256)
            pre = mm(cv, wfc1[:, cs], NN) + vec_ref[5:6, cs]
            phi = 0.5 * (1.0 + lax.erf(pre * INV_SQRT2))
            act_r[rs, cs] = (pre * phi).astype(BF16)
            gp_r[rs, cs] = phi + pre * (INV_SQRT_2PI * jnp.exp(-0.5 * pre * pre))
            return 0

        lax.fori_loop(0, FW // 256, fc1, 0)
        @pl.when(s + 1 < S)
        def _():
            ps_forward(0, s + 1)

        @pl.when(s + 1 == S)
        def _():
            ps_forward(1, 0)

        ps_start(1, s, lambda h: mm(act_r[rs, :], wfc2[:, half_cols(h)], NN))
        return 0

    lax.fori_loop(0, S, phase_b, 0)

    ins[4].wait()
    ins[5].wait()
    loss_scale = kept_ref.shape[0] / (2.0 * count * D)
    seed_scale = kept_ref.shape[0] * SLOTS * 1.0 / count

    loss_r[...] = jnp.zeros_like(loss_r)

    def phase_c(s, _):
        lacc[...] = jnp.zeros_like(lacc)

        def fin(h):
            hc = half_cols(h)

            def one(i, _):
                m = mask_rows(s, i)
                mlp = tot[1, s, h, 0, loc(i), :].astype(F32) + tot[1, s, h, 1, loc(i), :].astype(F32)
                final = (h1_r[blk(s, i), hc] + mlp + vec_ref[6:7, hc]) * m
                diff = (final - tea[blk(s, i), hc].astype(F32)) * m
                seed = (og[blk(s, i), hc].astype(F32) + diff * seed_scale) * m
                tea[blk(s, i), hc] = final.astype(BF16)
                seed_r[blk(s, i), hc] = seed
                sl_r[blk(s, i), hc] = seed.astype(BF16)
                lacc[...] += fold8(diff * diff)
                vacc[6, :, hc] += fold8(seed)
                return 0

            chunks(one)

        fin(lo)
        ps_finish(1, s)
        fin(1 - lo)
        here = (lax.broadcasted_iota(jnp.int32, (1, D), 1) == s).astype(F32)
        loss_r[...] += here * (jnp.sum(lacc[...]) * loss_scale)
        rs = seq_rows(s)
        sv = sl_r[rs, :]

        @pl.when(s == S - 1)
        def _():
            grad_tiles(0, 2, sl_r, act_r)


        def dact(j, _):
            cs = pl.ds(pl.multiple_of(j * 256, 256), 256)
            d = mm(sv, wfc2[cs, :], NT) * gp_r[rs, cs]
            dl = d.astype(BF16)
            dpre_r[rs, cs] = dl
            vacc[5, :, cs] += fold8(dl.astype(F32))
            return 0

        lax.fori_loop(0, FW // 256, dact, 0)
        ps_start(0, s, lambda h: mm(dpre_r[rs, :], wfc1[half_cols(h), :], NT))

        @pl.when(s + 1 < S)
        def _():
            ps_forward(1, s + 1)

        return 0

    lax.fori_loop(0, S, phase_c, 0)

    grad_tiles(2, 4, sl_r, act_r)
    grad_tiles(4, 5, c_r, dpre_r, 4)
    ps_forward(0, 0)

    def phase_d(s, _):
        ps_finish(0, s)

        def lnb(i, _):
            hat, r = norm_stats(h1_r[blk(s, i), :])
            dy = ps_total(0, s, i)
            vacc[3] += fold8(dy * hat)
            vacc[4] += fold8(dy)
            dg = dy * vec_ref[3:4, :]
            m1 = jnp.mean(dg, axis=-1, keepdims=True)
            m2 = jnp.mean(dg * hat, axis=-1, keepdims=True)
            dh1 = seed_r[blk(s, i), :] + r * (dg - m1 - hat * m2)
            seed_r[blk(s, i), :] = dh1
            vacc[2] += fold8(dh1)
            sl_r[blk(s, i), :] = dh1.astype(BF16)
            return 0

        chunks(lnb)
        rs = seq_rows(s)

        def pair(hp, _):
            wc = pl.ds(pl.multiple_of(hp * 2 * HEAD, 2 * HEAD), 2 * HEAD)
            dh = mm(sl_r[rs, :], wproj[wc, :], NT).astype(BF16)
            q = qkv_r[rs, pair_cols(0, hp)]
            k = qkv_r[rs, pair_cols(1, hp)]
            v = qkv_r[rs, pair_cols(2, hp)]
            dq = dk = dv = None
            for hh in range(2):
                hm = head_mask(hh)
                qm, km, dm = q * head_mask(hh, SCALE), k * hm, dh * hm
                pr = probs_of(qm, k, s)
                dpr = mm(dm, v, NT)
                ds = (pr * (dpr - jnp.sum(pr * dpr, axis=-1, keepdims=True))).astype(BF16)
                q1, k1, v1 = mm(ds, km, NN), mm(ds, qm, TN), mm(pr.astype(BF16), dm, TN)
                if dq is None:
                    dq, dk, dv = q1, k1, v1
                else:
                    dq, dk, dv = dq + q1, dk + k1, dv + v1
            dql = (dq * SCALE).astype(BF16)
            dvl = dv.astype(BF16)
            dqkv_r[rs, pair_cols(0, hp)] = dql
            dqkv_r[rs, pair_cols(1, hp)] = dk.astype(BF16)
            dqkv_r[rs, pair_cols(2, hp)] = dvl
            vacc[7, :, pair_cols(0, hp)] += fold8(dql.astype(F32))
            vacc[7, :, pair_cols(1, hp)] += fold8(dvl.astype(F32))
            return 0

        steps_at(
            s,
            [(0, 0)],
            [(0, 1), (4, 0)],
            [(5, 0), (4, 1)],
        )
        lax.fori_loop(0, npair, pair, 0, unroll=True)
        steps_at(
            s,
            [(2, 0)],
            [(3, 0), (2, 1)],
            [(6, 0), (5, 1)],
        )
        @pl.when(s + 1 < S)
        def _():
            ps_forward(0, s + 1)

        @pl.when(s + 1 == S)
        def _():
            ps_forward(1, 0)

        ps_start(1, s, lambda h: sum(
            mm(dqkv_r[rs, c * LW:(c + 1) * LW], wqkv[c, half_cols(h), :], NT) for c in range(3)
        ))

        @pl.when(s == 0)
        def _():
            grad_tiles(5, 8, c_r, dpre_r, 4)

        return 0

    lax.fori_loop(0, S, phase_d, 0)
    grad_tile(8, sl_r, heads_r[...])

    def attn_tile(k, _):
        grad_tile(k, a_r, dqkv_r[:, pl.ds(pl.multiple_of((k - 9) * 256, 256), 256)])

        @pl.when(k == 9)
        def _():
            steps((7, 0))

        return 0

    lax.fori_loop(9, 12, attn_tile, 0)
    steps((1, 0), (6, 1))

    def phase_e(s, _):
        ps_finish(1, s)

        def lnb(i, _):
            m = mask_rows(s, i)
            hat, r = norm_stats(tok[blk(s, i), :].astype(F32) * m)
            dy = ps_total(1, s, i)
            vacc[0] += fold8(dy * hat)
            vacc[1] += fold8(dy)
            dg = dy * vec_ref[0:1, :]
            m1 = jnp.mean(dg, axis=-1, keepdims=True)
            m2 = jnp.mean(dg * hat, axis=-1, keepdims=True)
            seed_r[blk(s, i), :] = (seed_r[blk(s, i), :] + r * (dg - m1 - hat * m2)) * m
            return 0

        chunks(lnb)

        @pl.when(s + 1 < S)
        def _():
            ps_forward(1, s + 1)

        steps_at(
            s,
            [(0, 2), (3, 1)],
            [(2, 2), (7, 1)],
            [],
        )
        return 0

    lax.fori_loop(0, S, phase_e, 0)

    for j in range(8):
        vst[0, j:j + 1, :] = jnp.sum(vacc[j], axis=0, keepdims=True)

    def cp_v(j):
        return pltpu.make_async_remote_copy(
            src_ref=vst.at[j], dst_ref=vrc.at[j], send_sem=v_s.at[j], recv_sem=v_r.at[j],
            device_id=flip((j + 1) % NBITS), device_id_type=MESH,
        )

    def step_v(j):
        cp_v(j).wait()
        total = vst[j] + vrc[j]
        if j + 1 < NBITS:
            vst[j + 1] = total
            cp_v(j + 1).start()
        else:
            vout_ref[0:8, :] = total
            vout_ref[8:9, :] = loss_r[...]

    cp_v(0).start()
    steps((8, 0), (4, 2), (5, 2), (9, 0), (8, 1))
    step_v(0)
    steps((6, 2), (10, 0), (9, 1), (3, 2), (7, 2), (11, 0), (10, 1), (12, 0))
    for j in range(1, NBITS - 1):
        step_v(j)
    steps((11, 1), (8, 2), (1, 1), (12, 1))
    step_v(NBITS - 1)
    steps((9, 2), (10, 2), (11, 2), (1, 2), (12, 2))

    def drain(tile, _):
        for j in range(NBITS):
            cp_g(tile, j).wait_send()
        return 0

    lax.fori_loop(0, T - 1, drain, 0)
    drain(T - 1, 0)
    drain(T, 0)


def finish(v_in, *refs):
    ins, refs = refs[:6], refs[6:]
    loss_o, ln1g_o, ln1b_o, bqv_o, bproj_o, ln2g_o, ln2b_o, bfc1_o, bfc2_o = refs[:9]
    outs, sem, mids = refs[9:15], refs[15], refs[16:]
    moves = [pltpu.make_async_copy(src, dst, sem.at[i]) for i, (src, dst) in enumerate(zip(ins, outs))]
    for c in moves:
        c.start()
    for i in range(loss_o.shape[0]):
        loss_o[i] = v_in[8, i]
    for j, (mid, ref) in enumerate(zip(mids, [ln1g_o, ln1b_o, bproj_o, ln2g_o, ln2b_o, bfc1_o, bfc2_o])):
        mid[...] = v_in[j]
        moves.append(pltpu.make_async_copy(mid, ref, sem.at[6 + j]))
        moves[-1].start()
    lw = bqv_o.shape[1]
    bqv_o[0:1, :] = v_in[7:8, 0:lw]
    bqv_o[1:2, :] = v_in[7:8, lw:2 * lw]
    for c in moves:
        c.wait()


def body(
    n_dp,
    tokens, kept, teacher, out_grad, ln1_gain, ln1_bias, w_qkv, bias_qv, w_proj, bias_proj,
    ln2_gain, ln2_bias, w_fc1, bias_fc1, w_fc2, bias_fc2,
):
    rows = tokens.shape[0]
    S = rows // SLOTS
    LW = w_qkv.shape[2]
    FW = w_fc1.shape[1]
    CH = D // n_dp
    NBITS = n_dp.bit_length() - 1
    T = (2 * FW + 4 * LW) // 256
    cfg = (S, n_dp, NBITS, CH, FW)
    any_spec = pl.BlockSpec(memory_space=pl.ANY)
    vm = pl.BlockSpec(memory_space=pltpu.VMEM)
    sm = pl.BlockSpec(memory_space=pltpu.SMEM)
    sds = jax.ShapeDtypeStruct
    DMA = pltpu.SemaphoreType.DMA
    V = pltpu.VMEM
    big = [
        ((rows, D), BF16), ((rows, D), F32), ((FW, CH), F32), ((CH, FW), F32), ((LW, CH), F32), ((3, CH, LW), F32),
    ]
    out, tg, vout, *grads = pl.pallas_call(
        functools.partial(kernel, cfg),
        out_shape=[V(*big[0]), V(*big[1]), V((16, D), F32)] + [V(*b) for b in big[2:]],
        in_specs=[sm] + [vm] * 8 + [any_spec] * 7,
        out_specs=[vm] * 7,
        scratch_shapes=[
            V((3, D, LW), BF16), V((LW, D), BF16), V((D, FW), BF16), V((FW, D), BF16),
            V((rows, D), BF16), V((rows, D), BF16),
            V((rows, D), BF16), V((rows, 3 * LW), BF16), V((rows, LW), BF16), V((rows, D), BF16),
            V((rows, D), F32), V((rows, FW), BF16), V((rows, FW), F32),
            V((rows, D), BF16), V((rows, FW), BF16), V((rows, 3 * LW), BF16),
            V((S, SLOTS, HALF), BF16), V((S, SLOTS, HALF), BF16), V((2, S, 2, 2, SLOTS, HALF), BF16),
            V((T, n_dp, CH, 256), BF16), V((T, n_dp - 1, CH, 256), BF16),
            V((8, D), F32), V((8, HALF), F32), V((1, D), F32), V((8, 8, D), F32), V((NBITS, 8, D), F32), V((NBITS, 8, D), F32),
            DMA((6 + S,)), DMA((2, S, 4)), DMA((2, S, 4)), DMA((T + 1, NBITS)), DMA((T + 1, NBITS)),
            DMA((NBITS,)), DMA((NBITS,)),
        ],
        compiler_params=pltpu.CompilerParams(
            collective_id=0, has_side_effects=True, vmem_limit_bytes=56 * 2**20
        ),
        name="layer",
    )(
        kept, ln1_gain, ln1_bias, bias_proj, ln2_gain, ln2_bias, bias_fc1, bias_fc2, bias_qv,
        tokens, teacher, out_grad, w_qkv.transpose(1, 0, 2), w_proj, w_fc1, w_fc2,
    )
    vd = sds((D,), F32)
    loss, g_ln1g, g_ln1b, g_bqv, g_bproj, g_ln2g, g_ln2b, g_bfc1, g_bfc2, out, token_grad, g_wfc2, g_wfc1, g_wproj, g_wqkv = (
        pl.pallas_call(
            finish,
            out_shape=[sds((S,), F32), vd, vd, sds((2, LW), F32), vd, vd, vd, sds((FW,), F32), vd]
            + [sds(*b) for b in big],
            in_specs=[vm] * 7,
            out_specs=[sm, any_spec, any_spec, vm] + [any_spec] * 11,
            scratch_shapes=[DMA((13,))] + [V((D,), F32)] * 5 + [V((FW,), F32), V((D,), F32)],
            compiler_params=pltpu.CompilerParams(vmem_limit_bytes=16 * 2**20),
            name="finish",
        )(vout, out, tg, *grads)
    )
    return (
        out, loss, token_grad, g_ln1g, g_ln1b, g_wqkv.transpose(1, 0, 2), g_bqv, g_wproj, g_bproj, g_ln2g, g_ln2b,
        g_wfc1, g_bfc1, g_wfc2, g_bfc2,
    )


def solution(mesh):
    tp = P("tensor")
    in_specs = (
        P("dp", None), P(), P("dp", None), P("dp", None), P(), P(), P(None, None, "tensor"),
        P(None, "tensor"), P("tensor", None), P(), P(), P(), P(None, "tensor"), tp, P("tensor", None), P(),
    )
    out_specs = (
        P("dp", None), P("dp"), P("dp", None), P(), P(), P("dp", None, "tensor"), P(None, "tensor"),
        P("tensor", "dp"), P(), P(), P(), P("dp", "tensor"), tp, P("tensor", "dp"), P(),
    )
    return jax.shard_map(
        functools.partial(body, mesh.shape["dp"]), mesh=mesh, in_specs=in_specs, out_specs=out_specs,
        check_vma=False,
    )
```

```python
import functools

import jax
import jax.numpy as jnp
from jax import lax
from jax.experimental import pallas as pl
from jax.experimental.pallas import tpu as pltpu
from jax.sharding import PartitionSpec as P

D = 1024
H = 16
HEAD = D // H
BUFFER = 64
SLOTS = 320
HALF = D // 2
RB = 32
EPS = 1e-06
F32 = jnp.float32
BF16 = jnp.bfloat16
MESH = pl.DeviceIdType.MESH
NT = (((1,), (1,)), ((), ()))
TN = (((0,), (0,)), ((), ()))
NN = (((1,), (0,)), ((), ()))
INV_SQRT2 = 0.7071067811865476
INV_SQRT_2PI = 0.3989422804014327


def mm(a, b, dims):
    return lax.dot_general(a, b, dims, preferred_element_type=F32)


def fold8(x):
    return jnp.sum(x.reshape(x.shape[0] // 8, 8, x.shape[1]), axis=0)


def kernel(
    cfg,
    kept_in, ln1g_in, ln1b_in, bproj_in, ln2g_in, ln2b_in, bfc1_in, bfc2_in, bqv_in,
    tok_in, tea_in, og_in, wqkv_in, wproj_in, wfc1_in, wfc2_in,
    tea, seed_r, vout_ref, gfc2_r, gfc1_r, gproj_r, gqkv_r,
    wqkv, wproj, wfc1, wfc2, tok, og,
    a_r, qkv_r, heads_r, c_r, h1_r, act_r, gp_r, sl_r, dpre_r, dqkv_r,
    core_s, core_r, tot, gs, rb, vec_ref, lacc, loss_r, vacc, vst, vrc,
    v1_ln1g, v1_ln1b, v1_bproj, v1_ln2g, v1_ln2b, v1_bfc1, v1_bfc2, v1_bqv, kept_ref, in_sem, ps_s, ps_r, px_r, g_s, g_r, v_s, v_r,
):
    S, NDP, NBITS, CH, FW = cfg
    LW = wproj.shape[0]
    R = SLOTS
    rows_all = S * R
    dp = lax.axis_index("dp")
    t = lax.axis_index("tensor")
    lo = lax.rem(t, 2)
    hi = t // 2
    sib = (dp, hi * 2 + (1 - lo))
    xn = (dp, (1 - hi) * 2 + lo)
    bits = [lax.rem(dp // (1 << b), 2) for b in range(NBITS)]

    def flip(b):
        return (dp + (1 << b) * (1 - 2 * bits[b]), t)

    def in_copy(i, src, dst):
        return pltpu.make_async_copy(src, dst, in_sem.at[i])

    def tok_copy(s):
        rows = pl.ds(pl.multiple_of(s * R, 64), R)
        return pltpu.make_async_copy(tok_in.at[rows, :], tok.at[rows, :], in_sem.at[15 + s])

    ins = [
        in_copy(0, wqkv_in, wqkv),
        in_copy(1, wproj_in, wproj),
        in_copy(2, wfc1_in, wfc1),
        in_copy(3, wfc2_in, wfc2),
        in_copy(4, tea_in, tea),
        in_copy(5, og_in, og),
    ]
    v1 = [v1_ln1g, v1_ln1b, v1_bproj, v1_ln2g, v1_ln2b, v1_bfc1, v1_bfc2]
    small = [
        in_copy(6 + i, src, dst)
        for i, (src, dst) in enumerate(zip([ln1g_in, ln1b_in, bproj_in, ln2g_in, ln2b_in, bfc1_in, bfc2_in], v1))
    ]
    bqv_copy, kept_copy = in_copy(13, bqv_in, v1_bqv), in_copy(14, kept_in, kept_ref)
    tok_copy(0).start()
    kept_copy.start()
    small[0].start()
    small[1].start()
    bqv_copy.start()
    ins[0].start()
    ins[1].start()
    for c in small[2:]:
        c.start()

    bar = pltpu.get_barrier_semaphore()
    for peer in [sib, xn] + [flip(b) for b in range(NBITS)]:
        pl.semaphore_signal(bar, inc=1, device_id=peer, device_id_type=MESH)

    vacc[...] = jnp.zeros_like(vacc)
    vec_ref[7:8, :] = jnp.zeros((1, D), F32)

    def vec_rows(first, last):
        for j in range(first, last):
            small[j].wait()
            vec_ref[j:j + 1, :] = v1[j][...].astype(F32).reshape(1, v1[j].shape[0])

    vec_rows(0, 2)
    bqv_copy.wait()
    bqv = v1_bqv[...].astype(F32)
    vec_ref[7:8, 0:LW] = bqv[0:1]
    vec_ref[7:8, 2 * LW:3 * LW] = bqv[1:2]
    kept_copy.wait()

    def length(s):
        return kept_ref[dp * S + s] + BUFFER

    def mask_rows(s, i):
        idx = lax.broadcasted_iota(jnp.int32, (RB, 1), 0) + i * RB
        return (idx < length(s)).astype(F32)

    def seq_rows(s):
        return pl.ds(pl.multiple_of(s * R, 64), R)

    def chunks(fn, init=0):
        return lax.fori_loop(0, R // RB, fn, init, unroll=5)

    def blk(s, i):
        return pl.ds(pl.multiple_of(s * R + i * RB, RB), RB)

    def loc(i):
        return pl.ds(pl.multiple_of(i * RB, RB), RB)

    def norm_stats(x):
        mean = jnp.mean(x, axis=-1, keepdims=True)
        off = x - mean
        var = jnp.mean(off * off, axis=-1, keepdims=True)
        r = lax.rsqrt(var + EPS)
        return off * r, r

    def cp(p, s, kind, src, dst, dev):
        return pltpu.make_async_remote_copy(
            src_ref=src, dst_ref=dst,
            send_sem=ps_s.at[s, kind], recv_sem=px_r.at[p, s] if kind == 1 else ps_r.at[s, kind // 2 + kind // 3],
            device_id=dev, device_id_type=MESH,
        )

    def cp_core(p, s):
        return cp(p, s, 0, core_s.at[s], core_r.at[s], sib)

    def cp_x(p, s):
        ref = tot.at[p, s, lo, hi]
        return cp(p, s, 1, ref, ref, xn)

    def cp_f1(p, s):
        ref = tot.at[p, s, lo, hi]
        return cp(p, s, 2, ref, ref, sib)

    def cp_f2(p, s):
        ref = tot.at[p, s, lo, 1 - hi]
        return cp(p, s, 3, ref, ref, sib)

    def ps_start(p, s, part):
        core_s[s] = part(1 - lo).astype(BF16)
        cp_core(p, s).start()
        own = part(lo).astype(BF16).astype(F32)
        cp_core(p, s).wait_recv()
        tot[p, s, lo, hi] = (own + core_r[s].astype(F32)).astype(BF16)
        cp_x(p, s).start()
        cp_f1(p, s).start()

    def ps_forward(p, s):
        cp_core(p, s).wait_send()
        cp_x(p, s).wait()
        cp_f2(p, s).start()

    def ps_finish(p, s):
        cp_f1(p, s).wait()
        cp_f2(p, s).wait()

    def ps_total(p, s, i):
        rr = loc(i)
        parts = [
            tot[p, s, h, 0, rr, :].astype(F32) + tot[p, s, h, 1, rr, :].astype(F32) for h in range(2)
        ]
        return jnp.concatenate(parts, axis=1)

    def half_cols(h):
        return pl.ds(pl.multiple_of(h * HALF, HALF), HALF)

    lane_half = lax.broadcasted_iota(jnp.int32, (1, 2 * HEAD), 1) // HEAD

    def head_mask(hh, scale=1.0):
        return ((lane_half == hh).astype(F32) * scale).astype(BF16)

    SCALE = HEAD ** -0.5

    def pair_cols(c, hp):
        return pl.ds(pl.multiple_of(c * LW + hp * 2 * HEAD, 2 * HEAD), 2 * HEAD)

    def probs_of(qm, k, s):
        sc = mm(qm, k, NT)
        col = lax.broadcasted_iota(jnp.int32, (1, R), 1)
        sc = jnp.where(col < length(s), sc, -1e30)
        top = jnp.max(sc, axis=-1, keepdims=True)
        e = jnp.exp(sc - top)
        return e * (1.0 / jnp.sum(e, axis=-1, keepdims=True))

    npair = LW // (2 * HEAD)

    def swapped(tile):
        if isinstance(tile, int):
            return int(tile in (1, 3))
        return lax.rem(tile, 2) * ((T - tile) // (T - 3))

    def mix(f, p, q):
        return p + f * (q - p)

    def place(d, f):
        db = [(d >> b) & 1 for b in range(NBITS)]
        pos = sum(db[b] << (NBITS - 1 - b) for b in range(2, NBITS))
        if NBITS > 1:
            return pos + mix(f, db[0], db[1]) * (NDP // 2) + mix(f, db[1], db[0]) * (NDP // 4)
        return db[0]

    def stage_bit(f, j):
        if NBITS > 1 and j < 2:
            return mix(f, bits[j], bits[1 - j])
        return bits[j]

    def stage_peer(f, j):
        if NBITS > 1 and j < 2:
            step = [(1 << b) * (1 - 2 * bits[b]) for b in range(2)]
            return (dp + mix(f, step[j], step[1 - j]), t)
        return flip(j)

    def base(f, j):
        return sum((stage_bit(f, i) * (NDP >> (i + 1)) for i in range(j)), 0)

    def land(j):
        return NDP - (NDP >> j)

    def room(tile):
        if isinstance(tile, int) and tile >= T - 1:
            return T - 1, slice((tile - T + 1) * 128, (tile - T + 2) * 128)
        return tile, slice(0, 256)

    def cp_g(tile, j):
        f = swapped(tile)
        at, cols = room(tile)
        n = NDP >> (j + 1)
        first = base(f, j) + (1 - stage_bit(f, j)) * n
        return pltpu.make_async_remote_copy(
            src_ref=gs.at[at, pl.ds(first, n), :, cols], dst_ref=rb.at[at, land(j):land(j) + n, :, cols],
            send_sem=g_s.at[tile], recv_sem=g_r.at[tile, j],
            device_id=stage_peer(f, j), device_id_type=MESH,
        )

    def grad_tile(tile, lhs, rhs):
        f = swapped(tile)
        val = mm(lhs[...], rhs, TN).astype(BF16)
        for d in range(NDP):
            gs[tile, place(d, f)] = val[d * CH:(d + 1) * CH]
        if isinstance(tile, int):
            cp_g(tile, 0).start()
            return

        @pl.when(tile < T - 1)
        def _():
            cp_g(tile, 0).start()

        @pl.when(tile == T - 1)
        def _():
            cp_g(T - 1, 0).start()
            cp_g(T, 0).start()

    def grad_tiles(first, last, lhs, rhs, skip=0):
        def one(k, _):
            grad_tile(k, lhs, rhs[:, pl.ds(pl.multiple_of((k - skip) * 256, 256), 256)])
            return 0

        lax.fori_loop(first, last, one, 0)

    def advance(tile, j):
        f = swapped(tile)
        cp_g(tile, j).wait_recv()
        n = NDP >> (j + 1)
        mine = base(f, j + 1)

        at, cols = room(tile)
        if j + 1 < NBITS:
            def add(i, _):
                gs[at, mine + i, :, cols] = gs[at, mine + i, :, cols] + rb[at, land(j) + i, :, cols]
                return 0

            lax.fori_loop(0, n, add, 0)
            cp_g(tile, j).wait_send()
            cp_g(tile, j + 1).start()
            return
        val = gs[at, mine, :, cols].astype(F32) + rb[at, land(j), :, cols].astype(F32)
        if at < NT1:
            gfc2_r[at * 256:(at + 1) * 256, :] = val.T
        elif at < 2 * NT1:
            gfc1_r[:, (at - NT1) * 256:(at - NT1 + 1) * 256] = val
        elif at < 2 * NT1 + NT2:
            gproj_r[(at - 2 * NT1) * 256:(at - 2 * NT1 + 1) * 256, :] = val.T
        else:
            k = at - 2 * NT1 - NT2
            first = (k % NT2) * 256 + cols.start
            gqkv_r[k // NT2, :, first:first + cols.stop - cols.start] = val

    def steps(*pairs):
        for tile, j in pairs:
            for i in range(j, NBITS if j == 2 else j + 1):
                advance(tile, i)

    def steps_at(s, *lists):
        for at, pairs in enumerate(lists):
            if pairs:
                @pl.when(s == at)
                def _():
                    steps(*pairs)

    NT1 = FW // 256
    NT2 = LW // 256
    T = 2 * NT1 + 4 * NT2

    def phase_a(s, _):
        tok_copy(s).wait()

        def ln(i, _):
            x = tok[blk(s, i), :].astype(F32) * mask_rows(s, i)
            hat, _r = norm_stats(x)
            a_r[blk(s, i), :] = (hat * vec_ref[0:1, :] + vec_ref[1:2, :]).astype(BF16)
            return 0

        chunks(ln)

        @pl.when(s == 0)
        def _():
            ins[0].wait()

            def tok_start(i, _):
                tok_copy(i).start()
                return 0

            lax.fori_loop(1, S, tok_start, 0)
            for c in ins[2:]:
                c.start()

        rs = seq_rows(s)
        av = a_r[rs, :]
        for c in range(3):
            cs = slice(c * LW, (c + 1) * LW)
            qkv_r[rs, cs] = (mm(av, wqkv[c], NN) + vec_ref[7:8, cs]).astype(BF16)

        def pair(hp, _):
            q = qkv_r[rs, pair_cols(0, hp)]
            k = qkv_r[rs, pair_cols(1, hp)]
            v = qkv_r[rs, pair_cols(2, hp)]
            o = None
            for hh in range(2):
                pr = probs_of(q * head_mask(hh, SCALE), k, s).astype(BF16)
                oh = mm(pr, v * head_mask(hh), NN)
                o = oh if o is None else o + oh
            heads_r[rs, pair_cols(0, hp)] = o.astype(BF16)
            return 0

        lax.fori_loop(0, npair, pair, 0)
        hv = heads_r[rs, :]

        @pl.when(s == 0)
        def _():
            ins[1].wait()
            pl.semaphore_wait(bar, 2 + NBITS)

        ps_start(0, s, lambda h: mm(hv, wproj[:, half_cols(h)], NN))
        return 0

    lax.fori_loop(0, S, phase_a, 0)

    ps_forward(0, 0)

    vec_rows(2, 7)
    count = lax.fori_loop(
        0, kept_ref.shape[0], lambda i, acc: acc + (kept_ref[i] + BUFFER).astype(F32), jnp.float32(0.0)
    )

    ins[2].wait()
    ins[3].wait()

    def phase_b(s, _):
        ps_finish(0, s)

        def ln(i, _):
            x = tok[blk(s, i), :].astype(F32) * mask_rows(s, i)
            h1 = x + ps_total(0, s, i) + vec_ref[2:3, :]
            h1_r[blk(s, i), :] = h1
            hat, _r = norm_stats(h1)
            c_r[blk(s, i), :] = (hat * vec_ref[3:4, :] + vec_ref[4:5, :]).astype(BF16)
            return 0

        chunks(ln)
        rs = seq_rows(s)
        cv = c_r[rs, :]

        def fc1(j, _):
            cs = pl.ds(pl.multiple_of(j * 256, 256), 256)
            pre = mm(cv, wfc1[:, cs], NN) + vec_ref[5:6, cs]
            phi = 0.5 * (1.0 + lax.erf(pre * INV_SQRT2))
            act_r[rs, cs] = (pre * phi).astype(BF16)
            gp_r[rs, cs] = phi + pre * (INV_SQRT_2PI * jnp.exp(-0.5 * pre * pre))
            return 0

        lax.fori_loop(0, FW // 256, fc1, 0)
        @pl.when(s + 1 < S)
        def _():
            ps_forward(0, s + 1)

        @pl.when(s + 1 == S)
        def _():
            ps_forward(1, 0)

        ps_start(1, s, lambda h: mm(act_r[rs, :], wfc2[:, half_cols(h)], NN))
        return 0

    lax.fori_loop(0, S, phase_b, 0)

    ins[4].wait()
    ins[5].wait()
    loss_scale = kept_ref.shape[0] / (2.0 * count * D)
    seed_scale = kept_ref.shape[0] * SLOTS * 1.0 / count

    loss_r[...] = jnp.zeros_like(loss_r)

    def phase_c(s, _):
        lacc[...] = jnp.zeros_like(lacc)

        def fin(h):
            hc = half_cols(h)

            def one(i, _):
                m = mask_rows(s, i)
                mlp = tot[1, s, h, 0, loc(i), :].astype(F32) + tot[1, s, h, 1, loc(i), :].astype(F32)
                final = (h1_r[blk(s, i), hc] + mlp + vec_ref[6:7, hc]) * m
                diff = (final - tea[blk(s, i), hc].astype(F32)) * m
                seed = (og[blk(s, i), hc].astype(F32) + diff * seed_scale) * m
                tea[blk(s, i), hc] = final.astype(BF16)
                seed_r[blk(s, i), hc] = seed
                sl_r[blk(s, i), hc] = seed.astype(BF16)
                lacc[...] += fold8(diff * diff)
                vacc[6, :, hc] += fold8(seed)
                return 0

            chunks(one)

        fin(lo)
        ps_finish(1, s)
        fin(1 - lo)
        here = (lax.broadcasted_iota(jnp.int32, (1, D), 1) == s).astype(F32)
        loss_r[...] += here * (jnp.sum(lacc[...]) * loss_scale)
        rs = seq_rows(s)
        sv = sl_r[rs, :]

        @pl.when(s == S - 1)
        def _():
            grad_tiles(0, 2, sl_r, act_r)


        def dact(j, _):
            cs = pl.ds(pl.multiple_of(j * 256, 256), 256)
            d = mm(sv, wfc2[cs, :], NT) * gp_r[rs, cs]
            dl = d.astype(BF16)
            dpre_r[rs, cs] = dl
            vacc[5, :, cs] += fold8(dl.astype(F32))
            return 0

        lax.fori_loop(0, FW // 256, dact, 0)
        ps_start(0, s, lambda h: mm(dpre_r[rs, :], wfc1[half_cols(h), :], NT))

        @pl.when(s + 1 < S)
        def _():
            ps_forward(1, s + 1)

        return 0

    lax.fori_loop(0, S, phase_c, 0)

    grad_tiles(2, 4, sl_r, act_r)
    grad_tiles(4, 5, c_r, dpre_r, 4)
    ps_forward(0, 0)

    def phase_d(s, _):
        ps_finish(0, s)

        def lnb(i, _):
            hat, r = norm_stats(h1_r[blk(s, i), :])
            dy = ps_total(0, s, i)
            vacc[3] += fold8(dy * hat)
            vacc[4] += fold8(dy)
            dg = dy * vec_ref[3:4, :]
            m1 = jnp.mean(dg, axis=-1, keepdims=True)
            m2 = jnp.mean(dg * hat, axis=-1, keepdims=True)
            dh1 = seed_r[blk(s, i), :] + r * (dg - m1 - hat * m2)
            seed_r[blk(s, i), :] = dh1
            vacc[2] += fold8(dh1)
            sl_r[blk(s, i), :] = dh1.astype(BF16)
            return 0

        chunks(lnb)
        rs = seq_rows(s)

        def pair(hp, _):
            wc = pl.ds(pl.multiple_of(hp * 2 * HEAD, 2 * HEAD), 2 * HEAD)
            dh = mm(sl_r[rs, :], wproj[wc, :], NT).astype(BF16)
            q = qkv_r[rs, pair_cols(0, hp)]
            k = qkv_r[rs, pair_cols(1, hp)]
            v = qkv_r[rs, pair_cols(2, hp)]
            dq = dk = dv = None
            for hh in range(2):
                hm = head_mask(hh)
                qm, km, dm = q * head_mask(hh, SCALE), k * hm, dh * hm
                pr = probs_of(qm, k, s)
                dpr = mm(dm, v, NT)
                ds = (pr * (dpr - jnp.sum(pr * dpr, axis=-1, keepdims=True))).astype(BF16)
                q1, k1, v1 = mm(ds, km, NN), mm(ds, qm, TN), mm(pr.astype(BF16), dm, TN)
                if dq is None:
                    dq, dk, dv = q1, k1, v1
                else:
                    dq, dk, dv = dq + q1, dk + k1, dv + v1
            dql = (dq * SCALE).astype(BF16)
            dvl = dv.astype(BF16)
            dqkv_r[rs, pair_cols(0, hp)] = dql
            dqkv_r[rs, pair_cols(1, hp)] = dk.astype(BF16)
            dqkv_r[rs, pair_cols(2, hp)] = dvl
            vacc[7, :, pair_cols(0, hp)] += fold8(dql.astype(F32))
            vacc[7, :, pair_cols(1, hp)] += fold8(dvl.astype(F32))
            return 0

        steps_at(
            s,
            [(0, 0)],
            [(0, 1), (4, 0)],
            [(5, 0), (4, 1)],
        )
        lax.fori_loop(0, npair, pair, 0, unroll=True)
        steps_at(
            s,
            [(2, 0)],
            [(3, 0), (2, 1)],
            [(6, 0), (5, 1)],
        )
        @pl.when(s + 1 < S)
        def _():
            ps_forward(0, s + 1)

        @pl.when(s + 1 == S)
        def _():
            ps_forward(1, 0)

        ps_start(1, s, lambda h: sum(
            mm(dqkv_r[rs, c * LW:(c + 1) * LW], wqkv[c, half_cols(h), :], NT) for c in range(3)
        ))

        @pl.when(s == 0)
        def _():
            grad_tiles(5, 8, c_r, dpre_r, 4)

        return 0

    lax.fori_loop(0, S, phase_d, 0)
    grad_tile(8, sl_r, heads_r[...])

    def attn_tile(k, _):
        grad_tile(k, a_r, dqkv_r[:, pl.ds(pl.multiple_of((k - 9) * 256, 256), 256)])

        @pl.when(k == 9)
        def _():
            steps((7, 0))

        return 0

    lax.fori_loop(9, 12, attn_tile, 0)
    steps((1, 0), (6, 1))

    def phase_e(s, _):
        ps_finish(1, s)

        def lnb(i, _):
            m = mask_rows(s, i)
            hat, r = norm_stats(tok[blk(s, i), :].astype(F32) * m)
            dy = ps_total(1, s, i)
            vacc[0] += fold8(dy * hat)
            vacc[1] += fold8(dy)
            dg = dy * vec_ref[0:1, :]
            m1 = jnp.mean(dg, axis=-1, keepdims=True)
            m2 = jnp.mean(dg * hat, axis=-1, keepdims=True)
            seed_r[blk(s, i), :] = (seed_r[blk(s, i), :] + r * (dg - m1 - hat * m2)) * m
            return 0

        chunks(lnb)

        @pl.when(s + 1 < S)
        def _():
            ps_forward(1, s + 1)

        steps_at(
            s,
            [(0, 2), (3, 1)],
            [(2, 2), (7, 1)],
            [],
        )
        return 0

    lax.fori_loop(0, S, phase_e, 0)

    for j in range(8):
        vst[0, j:j + 1, :] = jnp.sum(vacc[j], axis=0, keepdims=True)

    def cp_v(j):
        return pltpu.make_async_remote_copy(
            src_ref=vst.at[j], dst_ref=vrc.at[j], send_sem=v_s.at[j], recv_sem=v_r.at[j],
            device_id=flip((j + 1) % NBITS), device_id_type=MESH,
        )

    def step_v(j):
        cp_v(j).wait()
        total = vst[j] + vrc[j]
        if j + 1 < NBITS:
            vst[j + 1] = total
            cp_v(j + 1).start()
        else:
            vout_ref[0:8, :] = total
            vout_ref[8:9, :] = loss_r[...]

    cp_v(0).start()
    steps((8, 0), (4, 2), (5, 2), (9, 0), (8, 1))
    step_v(0)
    steps((6, 2), (10, 0), (9, 1), (3, 2), (7, 2), (11, 0), (10, 1), (12, 0))
    for j in range(1, NBITS - 1):
        step_v(j)
    steps((11, 1), (8, 2), (1, 1), (12, 1))
    step_v(NBITS - 1)
    steps((9, 2), (10, 2), (11, 2), (1, 2), (12, 2))

    def drain(tile, _):
        cp_g(tile, NBITS - 1).wait_send()
        return 0

    lax.fori_loop(0, T - 1, drain, 0)
    drain(T - 1, 0)
    drain(T, 0)


def finish(v_in, *refs):
    ins, refs = refs[:6], refs[6:]
    loss_o, ln1g_o, ln1b_o, bqv_o, bproj_o, ln2g_o, ln2b_o, bfc1_o, bfc2_o = refs[:9]
    outs, sem, mids = refs[9:15], refs[15], refs[16:]
    moves = [pltpu.make_async_copy(src, dst, sem.at[i]) for i, (src, dst) in enumerate(zip(ins, outs))]
    for c in moves:
        c.start()
    loss_s, bqv_s, mids = mids[0], mids[1], mids[2:]
    for i in range(loss_o.shape[0]):
        loss_s[i] = v_in[8, i]
    for j, (mid, ref) in enumerate(zip(mids, [ln1g_o, ln1b_o, bproj_o, ln2g_o, ln2b_o, bfc1_o, bfc2_o])):
        mid[...] = v_in[j]
        moves.append(pltpu.make_async_copy(mid, ref, sem.at[6 + j]))
        moves[-1].start()
    lw = bqv_o.shape[1]
    bqv_s[0:1, :] = v_in[7:8, 0:lw]
    bqv_s[1:2, :] = v_in[7:8, lw:2 * lw]
    for j, (mid, ref) in enumerate(((loss_s, loss_o), (bqv_s, bqv_o))):
        moves.append(pltpu.make_async_copy(mid, ref, sem.at[13 + j]))
        moves[-1].start()
    for c in moves:
        c.wait()


def body(
    n_dp,
    tokens, kept, teacher, out_grad, ln1_gain, ln1_bias, w_qkv, bias_qv, w_proj, bias_proj,
    ln2_gain, ln2_bias, w_fc1, bias_fc1, w_fc2, bias_fc2,
):
    rows = tokens.shape[0]
    S = rows // SLOTS
    LW = w_qkv.shape[2]
    FW = w_fc1.shape[1]
    CH = D // n_dp
    NBITS = n_dp.bit_length() - 1
    T = (2 * FW + 4 * LW) // 256
    cfg = (S, n_dp, NBITS, CH, FW)
    any_spec = pl.BlockSpec(memory_space=pl.ANY)
    vm = pl.BlockSpec(memory_space=pltpu.VMEM)
    sm = pl.BlockSpec(memory_space=pltpu.SMEM)
    sds = jax.ShapeDtypeStruct
    DMA = pltpu.SemaphoreType.DMA
    V = pltpu.VMEM
    big = [
        ((rows, D), BF16), ((rows, D), F32), ((FW, CH), F32), ((CH, FW), F32), ((LW, CH), F32), ((3, CH, LW), F32),
    ]
    out, tg, vout, *grads = pl.pallas_call(
        functools.partial(kernel, cfg),
        out_shape=[V(*big[0]), V(*big[1]), V((16, D), F32)] + [V(*b) for b in big[2:]],
        in_specs=[any_spec] * 16,
        out_specs=[vm] * 7,
        scratch_shapes=[
            V((3, D, LW), BF16), V((LW, D), BF16), V((D, FW), BF16), V((FW, D), BF16),
            V((rows, D), BF16), V((rows, D), BF16),
            V((rows, D), BF16), V((rows, 3 * LW), BF16), V((rows, LW), BF16), V((rows, D), BF16),
            V((rows, D), F32), V((rows, FW), BF16), V((rows, FW), F32),
            V((rows, D), BF16), V((rows, FW), BF16), V((rows, 3 * LW), BF16),
            V((S, SLOTS, HALF), BF16), V((S, SLOTS, HALF), BF16), V((2, S, 2, 2, SLOTS, HALF), BF16),
            V((T, n_dp, CH, 256), BF16), V((T, n_dp - 1, CH, 256), BF16),
            V((8, D), F32), V((8, HALF), F32), V((1, D), F32), V((8, 8, D), F32), V((NBITS, 8, D), F32), V((NBITS, 8, D), F32),
            V((D,), BF16), V((D,), BF16), V((D,), BF16), V((D,), BF16), V((D,), BF16), V((FW,), BF16), V((D,), BF16),
            V((2, LW), BF16), pltpu.SMEM((kept.shape[0],), jnp.int32), DMA((15 + S,)), DMA((S, 4)), DMA((S, 3)), DMA((2, S)), DMA((T + 1,)), DMA((T + 1, NBITS)),
            DMA((NBITS,)), DMA((NBITS,)),
        ],
        compiler_params=pltpu.CompilerParams(
            collective_id=0, has_side_effects=True, vmem_limit_bytes=56 * 2**20
        ),
        name="layer",
    )(
        kept, ln1_gain, ln1_bias, bias_proj, ln2_gain, ln2_bias, bias_fc1, bias_fc2, bias_qv,
        tokens, teacher, out_grad, w_qkv.transpose(1, 0, 2), w_proj, w_fc1, w_fc2,
    )
    vd = sds((D,), F32)
    loss, g_ln1g, g_ln1b, g_bqv, g_bproj, g_ln2g, g_ln2b, g_bfc1, g_bfc2, out, token_grad, g_wfc2, g_wfc1, g_wproj, g_wqkv = (
        pl.pallas_call(
            finish,
            out_shape=[sds((S,), F32), vd, vd, sds((2, LW), F32), vd, vd, vd, sds((FW,), F32), vd]
            + [sds(*b) for b in big],
            in_specs=[vm] * 7,
            out_specs=[any_spec] * 15,
            scratch_shapes=[DMA((15,)), pltpu.SMEM((S,), F32), V((2, LW), F32)] + [V((D,), F32)] * 5 + [V((FW,), F32), V((D,), F32)],
            compiler_params=pltpu.CompilerParams(vmem_limit_bytes=16 * 2**20),
            name="finish",
        )(vout, out, tg, *grads)
    )
    return (
        out, loss, token_grad, g_ln1g, g_ln1b, g_wqkv.transpose(1, 0, 2), g_bqv, g_wproj, g_bproj, g_ln2g, g_ln2b,
        g_wfc1, g_bfc1, g_wfc2, g_bfc2,
    )


def solution(mesh):
    tp = P("tensor")
    in_specs = (
        P("dp", None), P(), P("dp", None), P("dp", None), P(), P(), P(None, None, "tensor"),
        P(None, "tensor"), P("tensor", None), P(), P(), P(), P(None, "tensor"), tp, P("tensor", None), P(),
    )
    out_specs = (
        P("dp", None), P("dp"), P("dp", None), P(), P(), P("dp", None, "tensor"), P(None, "tensor"),
        P("tensor", "dp"), P(), P(), P(), P("dp", "tensor"), tp, P("tensor", "dp"), P(),
    )
    return jax.shard_map(
        functools.partial(body, mesh.shape["dp"]), mesh=mesh, in_specs=in_specs, out_specs=out_specs,
        check_vma=False,
    )
```

```python
import functools

import jax
import jax.numpy as jnp
from jax import lax
from jax.experimental import pallas as pl
from jax.experimental.pallas import tpu as pltpu
from jax.sharding import PartitionSpec as P

D = 1024
H = 16
HEAD = D // H
BUFFER = 64
SLOTS = 320
HALF = D // 2
RB = 32
EPS = 1e-06
F32 = jnp.float32
BF16 = jnp.bfloat16
MESH = pl.DeviceIdType.MESH
NT = (((1,), (1,)), ((), ()))
TN = (((0,), (0,)), ((), ()))
NN = (((1,), (0,)), ((), ()))
INV_SQRT2 = 0.7071067811865476
INV_SQRT_2PI = 0.3989422804014327


def mm(a, b, dims):
    return lax.dot_general(a, b, dims, preferred_element_type=F32)


def fold8(x):
    return jnp.sum(x.reshape(x.shape[0] // 8, 8, x.shape[1]), axis=0)


def kernel(
    cfg,
    kept_in, ln1g_in, ln1b_in, bproj_in, ln2g_in, ln2b_in, bfc1_in, bfc2_in, bqv_in,
    tok_in, tea_in, og_in, wqkv_in, wproj_in, wfc1_in, wfc2_in,
    tea, seed_r, vout_ref, gfc2_r, gfc1_r, gproj_r, gqkv_r,
    wqkv, wproj, wfc1, wfc2, tok, og,
    a_r, qkv_r, heads_r, c_r, h1_r, act_r, gp_r, sl_r, dpre_r, dqkv_r,
    core_s, core_r, tot, gs, rb, vec_ref, lacc, loss_r, vacc, vst, vrc,
    v1_ln1g, v1_ln1b, v1_bproj, v1_ln2g, v1_ln2b, v1_bfc1, v1_bfc2, v1_bqv, kept_ref, in_sem, ps_s, ps_r, px_r, g_s, g_r, v_s, v_r,
):
    S, NDP, NBITS, CH, FW = cfg
    LW = wproj.shape[0]
    R = SLOTS
    rows_all = S * R
    dp = lax.axis_index("dp")
    t = lax.axis_index("tensor")
    lo = lax.rem(t, 2)
    hi = t // 2
    sib = (dp, hi * 2 + (1 - lo))
    xn = (dp, (1 - hi) * 2 + lo)
    bits = [lax.rem(dp // (1 << b), 2) for b in range(NBITS)]

    def flip(b):
        return (dp + (1 << b) * (1 - 2 * bits[b]), t)

    def in_copy(i, src, dst):
        return pltpu.make_async_copy(src, dst, in_sem.at[i])

    def tok_copy(s):
        rows = pl.ds(pl.multiple_of(s * R, 64), R)
        return pltpu.make_async_copy(tok_in.at[rows, :], tok.at[rows, :], in_sem.at[15 + s])

    ins = [
        in_copy(0, wqkv_in, wqkv),
        in_copy(1, wproj_in, wproj),
        in_copy(2, wfc1_in, wfc1),
        in_copy(3, wfc2_in, wfc2),
        in_copy(4, tea_in, tea),
        in_copy(5, og_in, og),
    ]
    v1 = [v1_ln1g, v1_ln1b, v1_bproj, v1_ln2g, v1_ln2b, v1_bfc1, v1_bfc2]
    small = [
        in_copy(6 + i, src, dst)
        for i, (src, dst) in enumerate(zip([ln1g_in, ln1b_in, bproj_in, ln2g_in, ln2b_in, bfc1_in, bfc2_in], v1))
    ]
    bqv_copy, kept_copy = in_copy(13, bqv_in, v1_bqv), in_copy(14, kept_in, kept_ref)
    tok_copy(0).start()
    kept_copy.start()
    small[0].start()
    small[1].start()
    bqv_copy.start()
    ins[0].start()
    ins[1].start()
    for c in small[2:]:
        c.start()

    bar = pltpu.get_barrier_semaphore()
    for peer in [sib, xn] + [flip(b) for b in range(NBITS)]:
        pl.semaphore_signal(bar, inc=1, device_id=peer, device_id_type=MESH)

    vacc[...] = jnp.zeros_like(vacc)
    vec_ref[7:8, :] = jnp.zeros((1, D), F32)

    def vec_rows(first, last):
        for j in range(first, last):
            small[j].wait()
            vec_ref[j:j + 1, :] = v1[j][...].astype(F32).reshape(1, v1[j].shape[0])

    vec_rows(0, 2)
    bqv_copy.wait()
    bqv = v1_bqv[...].astype(F32)
    vec_ref[7:8, 0:LW] = bqv[0:1]
    vec_ref[7:8, 2 * LW:3 * LW] = bqv[1:2]
    kept_copy.wait()

    def length(s):
        return kept_ref[dp * S + s] + BUFFER

    def mask_rows(s, i):
        idx = lax.broadcasted_iota(jnp.int32, (RB, 1), 0) + i * RB
        return (idx < length(s)).astype(F32)

    def seq_rows(s):
        return pl.ds(pl.multiple_of(s * R, 64), R)

    def chunks(fn, init=0):
        return lax.fori_loop(0, R // RB, fn, init, unroll=5)

    def blk(s, i):
        return pl.ds(pl.multiple_of(s * R + i * RB, RB), RB)

    def loc(i):
        return pl.ds(pl.multiple_of(i * RB, RB), RB)

    def norm_stats(x):
        mean = jnp.mean(x, axis=-1, keepdims=True)
        off = x - mean
        var = jnp.mean(off * off, axis=-1, keepdims=True)
        r = lax.rsqrt(var + EPS)
        return off * r, r

    HR = R // 2

    def pieces(p):
        return (0, 1)

    def piece(ref, r):
        return ref if r is None else ref.at[pl.ds(r * HR, HR)]

    def cp(s, send, recv, src, dst, dev):
        return pltpu.make_async_remote_copy(
            src_ref=src, dst_ref=dst, send_sem=ps_s.at[s, send], recv_sem=recv, device_id=dev, device_id_type=MESH
        )

    def cp_core(p, s, r):
        return cp(s, 6 * r, ps_r.at[s, 4 * r], piece(core_s.at[s], r), piece(core_r.at[s], r), sib)

    def cp_x(p, s, r):
        ref = piece(tot.at[p, s, lo, hi], r)
        return cp(s, 4 if r == 1 else 1, px_r.at[2 * r + p, s], ref, ref, xn)

    def cp_f1(p, s):
        ref = tot.at[p, s, lo, hi]
        return cp(s, 2, ps_r.at[s, 1], ref, ref, sib)

    def cp_f2(p, s, r):
        ref = piece(tot.at[p, s, lo, 1 - hi], r)
        return cp(s, 5 if r == 1 else 3, ps_r.at[s, 3 if r == 1 else 2], ref, ref, sib)

    def ps_start(p, s, part):
        core_s[s] = part(1 - lo).astype(BF16)
        for r in pieces(p):
            cp_core(p, s, r).start()
        own = part(lo).astype(BF16).astype(F32)
        for r in pieces(p):
            rr = pl.ds(r * HR, HR)
            cp_core(p, s, r).wait_recv()
            tot[p, s, lo, hi, rr] = (own[r * HR:(r + 1) * HR] + core_r[s, rr].astype(F32)).astype(BF16)
            cp_x(p, s, r).start()
        cp_f1(p, s).start()

    def ps_pass_on(p, s, r):
        cp_x(p, s, r).wait()
        cp_f2(p, s, r).start()

    def ps_forward(p, s):
        for r in pieces(p):
            cp_core(p, s, r).wait_send()
            ps_pass_on(p, s, r)

    def ps_finish(p, s):
        cp_f1(p, s).wait()
        for r in pieces(p):
            cp_f2(p, s, r).wait()

    def ps_total(p, s, i):
        rr = loc(i)
        parts = [
            tot[p, s, h, 0, rr, :].astype(F32) + tot[p, s, h, 1, rr, :].astype(F32) for h in range(2)
        ]
        return jnp.concatenate(parts, axis=1)

    def half_cols(h):
        return pl.ds(pl.multiple_of(h * HALF, HALF), HALF)

    lane_half = lax.broadcasted_iota(jnp.int32, (1, 2 * HEAD), 1) // HEAD

    def head_mask(hh, scale=1.0):
        return ((lane_half == hh).astype(F32) * scale).astype(BF16)

    SCALE = HEAD ** -0.5

    def pair_cols(c, hp):
        return pl.ds(pl.multiple_of(c * LW + hp * 2 * HEAD, 2 * HEAD), 2 * HEAD)

    def probs_of(qm, k, s):
        sc = mm(qm, k, NT)
        col = lax.broadcasted_iota(jnp.int32, (1, R), 1)
        sc = jnp.where(col < length(s), sc, -1e30)
        top = jnp.max(sc, axis=-1, keepdims=True)
        e = jnp.exp(sc - top)
        return e * (1.0 / jnp.sum(e, axis=-1, keepdims=True))

    npair = LW // (2 * HEAD)

    def swapped(tile):
        if isinstance(tile, int):
            return int(tile in (1, 3))
        return lax.rem(tile, 2) * ((T - tile) // (T - 3))

    def mix(f, p, q):
        return p + f * (q - p)

    def place(d, f):
        db = [(d >> b) & 1 for b in range(NBITS)]
        pos = sum(db[b] << (NBITS - 1 - b) for b in range(2, NBITS))
        if NBITS > 1:
            return pos + mix(f, db[0], db[1]) * (NDP // 2) + mix(f, db[1], db[0]) * (NDP // 4)
        return db[0]

    def stage_bit(f, j):
        if NBITS > 1 and j < 2:
            return mix(f, bits[j], bits[1 - j])
        return bits[j]

    def stage_peer(f, j):
        if NBITS > 1 and j < 2:
            step = [(1 << b) * (1 - 2 * bits[b]) for b in range(2)]
            return (dp + mix(f, step[j], step[1 - j]), t)
        return flip(j)

    def base(f, j):
        return sum((stage_bit(f, i) * (NDP >> (i + 1)) for i in range(j)), 0)

    def land(j):
        return NDP - (NDP >> j)

    def room(tile):
        if isinstance(tile, int) and tile >= T - 1:
            return T - 1, slice((tile - T + 1) * 128, (tile - T + 2) * 128)
        return tile, slice(0, 256)

    def cp_g(tile, j):
        f = swapped(tile)
        at, cols = room(tile)
        n = NDP >> (j + 1)
        first = base(f, j) + (1 - stage_bit(f, j)) * n
        return pltpu.make_async_remote_copy(
            src_ref=gs.at[at, pl.ds(first, n), :, cols], dst_ref=rb.at[at, land(j):land(j) + n, :, cols],
            send_sem=g_s.at[tile], recv_sem=g_r.at[tile, j],
            device_id=stage_peer(f, j), device_id_type=MESH,
        )

    def grad_tile(tile, lhs, rhs):
        store_tile(tile, mm(lhs[...], rhs, TN))

    def store_tile(tile, val):
        f = swapped(tile)
        val = val.astype(BF16)
        for d in range(NDP):
            gs[tile, place(d, f)] = val[d * CH:(d + 1) * CH]
        if isinstance(tile, int):
            cp_g(tile, 0).start()
            return

        @pl.when(tile < T - 1)
        def _():
            cp_g(tile, 0).start()

        @pl.when(tile == T - 1)
        def _():
            cp_g(T - 1, 0).start()
            cp_g(T, 0).start()

    def grad_tiles(first, last, lhs, rhs, skip=0):
        def one(k, _):
            grad_tile(k, lhs, rhs[:, pl.ds(pl.multiple_of((k - skip) * 256, 256), 256)])
            return 0

        lax.fori_loop(first, last, one, 0)

    def advance(tile, j):
        f = swapped(tile)
        cp_g(tile, j).wait_recv()
        n = NDP >> (j + 1)
        mine = base(f, j + 1)

        at, cols = room(tile)
        if j + 1 < NBITS:
            def add(i, _):
                gs[at, mine + i, :, cols] = gs[at, mine + i, :, cols] + rb[at, land(j) + i, :, cols]
                return 0

            lax.fori_loop(0, n, add, 0)
            cp_g(tile, j).wait_send()
            cp_g(tile, j + 1).start()
            return
        val = gs[at, mine, :, cols].astype(F32) + rb[at, land(j), :, cols].astype(F32)
        if at < NT1:
            gfc2_r[at * 256:(at + 1) * 256, :] = val.T
        elif at < 2 * NT1:
            gfc1_r[:, (at - NT1) * 256:(at - NT1 + 1) * 256] = val
        elif at < 2 * NT1 + NT2:
            gproj_r[(at - 2 * NT1) * 256:(at - 2 * NT1 + 1) * 256, :] = val.T
        else:
            k = at - 2 * NT1 - NT2
            first = (k % NT2) * 256 + cols.start
            gqkv_r[k // NT2, :, first:first + cols.stop - cols.start] = val

    def steps(*pairs):
        for tile, j in pairs:
            for i in range(j, NBITS if j == 2 else j + 1):
                advance(tile, i)

    def steps_at(s, *lists):
        for at, pairs in enumerate(lists):
            if pairs:
                @pl.when(s == at)
                def _():
                    steps(*pairs)

    NT1 = FW // 256
    NT2 = LW // 256
    T = 2 * NT1 + 4 * NT2

    def phase_a(s, _):
        tok_copy(s).wait()

        def ln(i, _):
            x = tok[blk(s, i), :].astype(F32) * mask_rows(s, i)
            hat, _r = norm_stats(x)
            a_r[blk(s, i), :] = (hat * vec_ref[0:1, :] + vec_ref[1:2, :]).astype(BF16)
            return 0

        chunks(ln)

        @pl.when(s == 0)
        def _():
            ins[0].wait()

            def tok_start(i, _):
                tok_copy(i).start()
                return 0

            lax.fori_loop(1, S, tok_start, 0)
            for c in ins[2:]:
                c.start()

        rs = seq_rows(s)
        av = a_r[rs, :]
        for c in range(3):
            cs = slice(c * LW, (c + 1) * LW)
            qkv_r[rs, cs] = (mm(av, wqkv[c], NN) + vec_ref[7:8, cs]).astype(BF16)

        def pair(hp, _):
            q = qkv_r[rs, pair_cols(0, hp)]
            k = qkv_r[rs, pair_cols(1, hp)]
            v = qkv_r[rs, pair_cols(2, hp)]
            o = None
            for hh in range(2):
                pr = probs_of(q * head_mask(hh, SCALE), k, s).astype(BF16)
                oh = mm(pr, v * head_mask(hh), NN)
                o = oh if o is None else o + oh
            heads_r[rs, pair_cols(0, hp)] = o.astype(BF16)
            return 0

        lax.fori_loop(0, npair, pair, 0)
        hv = heads_r[rs, :]

        @pl.when(s == 0)
        def _():
            ins[1].wait()
            pl.semaphore_wait(bar, 2 + NBITS)

        ps_start(0, s, lambda h: mm(hv, wproj[:, half_cols(h)], NN))
        return 0

    lax.fori_loop(0, S, phase_a, 0)

    ps_forward(0, 0)

    vec_rows(2, 7)
    count = lax.fori_loop(
        0, kept_ref.shape[0], lambda i, acc: acc + (kept_ref[i] + BUFFER).astype(F32), jnp.float32(0.0)
    )

    ins[2].wait()
    ins[3].wait()

    def phase_b(s, _):
        ps_finish(0, s)

        def ln(i, _):
            x = tok[blk(s, i), :].astype(F32) * mask_rows(s, i)
            h1 = x + ps_total(0, s, i) + vec_ref[2:3, :]
            h1_r[blk(s, i), :] = h1
            hat, _r = norm_stats(h1)
            c_r[blk(s, i), :] = (hat * vec_ref[3:4, :] + vec_ref[4:5, :]).astype(BF16)
            return 0

        chunks(ln)
        rs = seq_rows(s)
        cv = c_r[rs, :]

        def fc1(j, _):
            cs = pl.ds(pl.multiple_of(j * 256, 256), 256)
            pre = mm(cv, wfc1[:, cs], NN) + vec_ref[5:6, cs]
            phi = 0.5 * (1.0 + lax.erf(pre * INV_SQRT2))
            act_r[rs, cs] = (pre * phi).astype(BF16)
            gp_r[rs, cs] = phi + pre * (INV_SQRT_2PI * jnp.exp(-0.5 * pre * pre))
            return 0

        lax.fori_loop(0, FW // 256, fc1, 0)
        @pl.when(s + 1 < S)
        def _():
            ps_forward(0, s + 1)

        @pl.when(s + 1 == S)
        def _():
            ps_forward(1, 0)

        ps_start(1, s, lambda h: mm(act_r[rs, :], wfc2[:, half_cols(h)], NN))
        return 0

    lax.fori_loop(0, S, phase_b, 0)

    ins[4].wait()
    ins[5].wait()
    loss_scale = kept_ref.shape[0] / (2.0 * count * D)
    seed_scale = kept_ref.shape[0] * SLOTS * 1.0 / count

    loss_r[...] = jnp.zeros_like(loss_r)

    def phase_c(s, _):
        lacc[...] = jnp.zeros_like(lacc)

        def fin(h, r=None):
            hc = half_cols(h)

            def one(i, _):
                m = mask_rows(s, i)
                mlp = tot[1, s, h, 0, loc(i), :].astype(F32) + tot[1, s, h, 1, loc(i), :].astype(F32)
                final = (h1_r[blk(s, i), hc] + mlp + vec_ref[6:7, hc]) * m
                diff = (final - tea[blk(s, i), hc].astype(F32)) * m
                seed = (og[blk(s, i), hc].astype(F32) + diff * seed_scale) * m
                tea[blk(s, i), hc] = final.astype(BF16)
                seed_r[blk(s, i), hc] = seed
                sl_r[blk(s, i), hc] = seed.astype(BF16)
                lacc[...] += fold8(diff * diff)
                vacc[6, :, hc] += fold8(seed)
                return 0

            n = R // RB
            first, last = (0, n) if r is None else (r * n // 2, (r + 1) * n // 2)
            lax.fori_loop(first, last, one, 0, unroll=5)

        @pl.when(s < S - 1)
        def _():
            fin(lo)
            ps_finish(1, s)
            fin(1 - lo)

        @pl.when(s == S - 1)
        def _():
            last = S - 1
            for r in pieces(1):
                cp_core(1, last, r).wait_send()
            ps_pass_on(1, last, 0)
            fin(lo, 0)
            cp_f1(1, last).wait()
            cp_f2(1, last, 0).wait()
            fin(1 - lo, 0)
            ps_pass_on(1, last, 1)
            fin(lo, 1)
            cp_f2(1, last, 1).wait()
            fin(1 - lo, 1)

        rs = seq_rows(s)
        sv = sl_r[rs, :]

        @pl.when(s == S - 1)
        def _():
            grad_tiles(0, 2, sl_r, act_r)

        def dact(j, _):
            cs = pl.ds(pl.multiple_of(j * 256, 256), 256)
            d = mm(sv, wfc2[cs, :], NT) * gp_r[rs, cs]
            dl = d.astype(BF16)
            dpre_r[rs, cs] = dl
            vacc[5, :, cs] += fold8(dl.astype(F32))
            return 0

        lax.fori_loop(0, FW // 256, dact, 0)
        ps_start(0, s, lambda h: mm(dpre_r[rs, :], wfc1[half_cols(h), :], NT))

        here = (lax.broadcasted_iota(jnp.int32, (1, D), 1) == s).astype(F32)
        loss_r[...] += here * (jnp.sum(lacc[...]) * loss_scale)

        @pl.when(s + 1 < S - 1)
        def _():
            ps_forward(1, s + 1)

        return 0

    lax.fori_loop(0, S, phase_c, 0)

    grad_tiles(2, 4, sl_r, act_r)
    grad_tiles(4, 5, c_r, dpre_r, 4)
    ps_forward(0, 0)

    def phase_d(s, _):
        ps_finish(0, s)

        def lnb(i, _):
            hat, r = norm_stats(h1_r[blk(s, i), :])
            dy = ps_total(0, s, i)
            vacc[3] += fold8(dy * hat)
            vacc[4] += fold8(dy)
            dg = dy * vec_ref[3:4, :]
            m1 = jnp.mean(dg, axis=-1, keepdims=True)
            m2 = jnp.mean(dg * hat, axis=-1, keepdims=True)
            dh1 = seed_r[blk(s, i), :] + r * (dg - m1 - hat * m2)
            seed_r[blk(s, i), :] = dh1
            vacc[2] += fold8(dh1)
            sl_r[blk(s, i), :] = dh1.astype(BF16)
            return 0

        chunks(lnb)
        rs = seq_rows(s)

        def pair(hp, _):
            wc = pl.ds(pl.multiple_of(hp * 2 * HEAD, 2 * HEAD), 2 * HEAD)
            dh = mm(sl_r[rs, :], wproj[wc, :], NT).astype(BF16)
            q = qkv_r[rs, pair_cols(0, hp)]
            k = qkv_r[rs, pair_cols(1, hp)]
            v = qkv_r[rs, pair_cols(2, hp)]
            dq = dk = dv = None
            for hh in range(2):
                hm = head_mask(hh)
                qm, km, dm = q * head_mask(hh, SCALE), k * hm, dh * hm
                pr = probs_of(qm, k, s)
                dpr = mm(dm, v, NT)
                ds = (pr * (dpr - jnp.sum(pr * dpr, axis=-1, keepdims=True))).astype(BF16)
                q1, k1, v1 = mm(ds, km, NN), mm(ds, qm, TN), mm(pr.astype(BF16), dm, TN)
                if dq is None:
                    dq, dk, dv = q1, k1, v1
                else:
                    dq, dk, dv = dq + q1, dk + k1, dv + v1
            dql = (dq * SCALE).astype(BF16)
            dvl = dv.astype(BF16)
            dqkv_r[rs, pair_cols(0, hp)] = dql
            dqkv_r[rs, pair_cols(1, hp)] = dk.astype(BF16)
            dqkv_r[rs, pair_cols(2, hp)] = dvl
            vacc[7, :, pair_cols(0, hp)] += fold8(dql.astype(F32))
            vacc[7, :, pair_cols(1, hp)] += fold8(dvl.astype(F32))
            return 0

        steps_at(
            s,
            [(0, 0)],
            [(0, 1), (4, 0)],
            [(5, 0), (4, 1)],
        )
        lax.fori_loop(0, npair, pair, 0, unroll=True)
        steps_at(
            s,
            [(2, 0)],
            [(3, 0), (2, 1)],
            [(6, 0), (5, 1)],
        )
        @pl.when(s + 1 < S)
        def _():
            ps_forward(0, s + 1)

        @pl.when(s + 1 == S)
        def _():
            ps_forward(1, 0)

        ps_start(1, s, lambda h: sum(
            mm(dqkv_r[rs, c * LW:(c + 1) * LW], wqkv[c, half_cols(h), :], NT) for c in range(3)
        ))

        @pl.when(s == 0)
        def _():
            grad_tiles(5, 8, c_r, dpre_r, 4)

        return 0

    lax.fori_loop(0, S, phase_d, 0)
    grad_tile(8, sl_r, heads_r[...])

    def attn_tile(k, _):
        grad_tile(k, a_r, dqkv_r[:, pl.ds(pl.multiple_of((k - 9) * 256, 256), 256)])

        @pl.when(k == 9)
        def _():
            steps((7, 0))

        return 0

    lax.fori_loop(9, 12, attn_tile, 0)
    steps((1, 0), (6, 1))

    def phase_e(s, _):
        ps_finish(1, s)

        def lnb(i, _):
            m = mask_rows(s, i)
            hat, r = norm_stats(tok[blk(s, i), :].astype(F32) * m)
            dy = ps_total(1, s, i)
            vacc[0] += fold8(dy * hat)
            vacc[1] += fold8(dy)
            dg = dy * vec_ref[0:1, :]
            m1 = jnp.mean(dg, axis=-1, keepdims=True)
            m2 = jnp.mean(dg * hat, axis=-1, keepdims=True)
            seed_r[blk(s, i), :] = (seed_r[blk(s, i), :] + r * (dg - m1 - hat * m2)) * m
            return 0

        chunks(lnb)

        @pl.when(s + 1 < S)
        def _():
            ps_forward(1, s + 1)

        steps_at(
            s,
            [(0, 2), (3, 1)],
            [(2, 2), (7, 1)],
            [],
        )
        return 0

    lax.fori_loop(0, S, phase_e, 0)

    for j in range(8):
        vst[0, j:j + 1, :] = jnp.sum(vacc[j], axis=0, keepdims=True)

    def cp_v(j):
        return pltpu.make_async_remote_copy(
            src_ref=vst.at[j], dst_ref=vrc.at[j], send_sem=v_s.at[j], recv_sem=v_r.at[j],
            device_id=flip((j + 1) % NBITS), device_id_type=MESH,
        )

    def step_v(j):
        cp_v(j).wait()
        total = vst[j] + vrc[j]
        if j + 1 < NBITS:
            vst[j + 1] = total
            cp_v(j + 1).start()
        else:
            vout_ref[0:8, :] = total
            vout_ref[8:9, :] = loss_r[...]

    cp_v(0).start()
    steps((8, 0), (4, 2), (5, 2), (9, 0), (8, 1))
    step_v(0)
    steps((6, 2), (10, 0), (9, 1), (3, 2), (7, 2), (11, 0), (12, 0), (10, 1))
    for j in range(1, NBITS - 1):
        step_v(j)
    steps((11, 1), (8, 2), (1, 1), (12, 1))
    step_v(NBITS - 1)
    steps((9, 2), (10, 2), (11, 2), (1, 2), (12, 2))

    def drain(tile, _):
        cp_g(tile, NBITS - 1).wait_send()
        return 0

    lax.fori_loop(0, T - 1, drain, 0)
    drain(T - 1, 0)
    drain(T, 0)


def finish(v_in, *refs):
    ins, refs = refs[:6], refs[6:]
    loss_o, ln1g_o, ln1b_o, bqv_o, bproj_o, ln2g_o, ln2b_o, bfc1_o, bfc2_o = refs[:9]
    outs, sem, mids = refs[9:15], refs[15], refs[16:]
    moves = [pltpu.make_async_copy(src, dst, sem.at[i]) for i, (src, dst) in enumerate(zip(ins, outs))]
    for c in moves:
        c.start()
    loss_s, bqv_s, mids = mids[0], mids[1], mids[2:]
    for i in range(loss_o.shape[0]):
        loss_s[i] = v_in[8, i]
    for j, (mid, ref) in enumerate(zip(mids, [ln1g_o, ln1b_o, bproj_o, ln2g_o, ln2b_o, bfc1_o, bfc2_o])):
        mid[...] = v_in[j]
        moves.append(pltpu.make_async_copy(mid, ref, sem.at[6 + j]))
        moves[-1].start()
    lw = bqv_o.shape[1]
    bqv_s[0:1, :] = v_in[7:8, 0:lw]
    bqv_s[1:2, :] = v_in[7:8, lw:2 * lw]
    for j, (mid, ref) in enumerate(((loss_s, loss_o), (bqv_s, bqv_o))):
        moves.append(pltpu.make_async_copy(mid, ref, sem.at[13 + j]))
        moves[-1].start()
    for c in moves:
        c.wait()


def body(
    n_dp,
    tokens, kept, teacher, out_grad, ln1_gain, ln1_bias, w_qkv, bias_qv, w_proj, bias_proj,
    ln2_gain, ln2_bias, w_fc1, bias_fc1, w_fc2, bias_fc2,
):
    rows = tokens.shape[0]
    S = rows // SLOTS
    LW = w_qkv.shape[2]
    FW = w_fc1.shape[1]
    CH = D // n_dp
    NBITS = n_dp.bit_length() - 1
    T = (2 * FW + 4 * LW) // 256
    cfg = (S, n_dp, NBITS, CH, FW)
    any_spec = pl.BlockSpec(memory_space=pl.ANY)
    vm = pl.BlockSpec(memory_space=pltpu.VMEM)
    sm = pl.BlockSpec(memory_space=pltpu.SMEM)
    sds = jax.ShapeDtypeStruct
    DMA = pltpu.SemaphoreType.DMA
    V = pltpu.VMEM
    big = [
        ((rows, D), BF16), ((rows, D), F32), ((FW, CH), F32), ((CH, FW), F32), ((LW, CH), F32), ((3, CH, LW), F32),
    ]
    out, tg, vout, *grads = pl.pallas_call(
        functools.partial(kernel, cfg),
        out_shape=[V(*big[0]), V(*big[1]), V((16, D), F32)] + [V(*b) for b in big[2:]],
        in_specs=[any_spec] * 16,
        out_specs=[vm] * 7,
        scratch_shapes=[
            V((3, D, LW), BF16), V((LW, D), BF16), V((D, FW), BF16), V((FW, D), BF16),
            V((rows, D), BF16), V((rows, D), BF16),
            V((rows, D), BF16), V((rows, 3 * LW), BF16), V((rows, LW), BF16), V((rows, D), BF16),
            V((rows, D), F32), V((rows, FW), BF16), V((rows, FW), F32),
            V((rows, D), BF16), V((rows, FW), BF16), V((rows, 3 * LW), BF16),
            V((S, SLOTS, HALF), BF16), V((S, SLOTS, HALF), BF16), V((2, S, 2, 2, SLOTS, HALF), BF16),
            V((T, n_dp, CH, 256), BF16), V((T, n_dp - 1, CH, 256), BF16),
            V((8, D), F32), V((8, HALF), F32), V((1, D), F32), V((8, 8, D), F32), V((NBITS, 8, D), F32), V((NBITS, 8, D), F32),
            V((D,), BF16), V((D,), BF16), V((D,), BF16), V((D,), BF16), V((D,), BF16), V((FW,), BF16), V((D,), BF16),
            V((2, LW), BF16), pltpu.SMEM((kept.shape[0],), jnp.int32), DMA((15 + S,)), DMA((S, 7)), DMA((S, 5)), DMA((4, S)), DMA((T + 1,)), DMA((T + 1, NBITS)),
            DMA((NBITS,)), DMA((NBITS,)),
        ],
        compiler_params=pltpu.CompilerParams(
            collective_id=0, has_side_effects=True, vmem_limit_bytes=56 * 2**20
        ),
        name="layer",
    )(
        kept, ln1_gain, ln1_bias, bias_proj, ln2_gain, ln2_bias, bias_fc1, bias_fc2, bias_qv,
        tokens, teacher, out_grad, w_qkv.transpose(1, 0, 2), w_proj, w_fc1, w_fc2,
    )
    vd = sds((D,), F32)
    loss, g_ln1g, g_ln1b, g_bqv, g_bproj, g_ln2g, g_ln2b, g_bfc1, g_bfc2, out, token_grad, g_wfc2, g_wfc1, g_wproj, g_wqkv = (
        pl.pallas_call(
            finish,
            out_shape=[sds((S,), F32), vd, vd, sds((2, LW), F32), vd, vd, vd, sds((FW,), F32), vd]
            + [sds(*b) for b in big],
            in_specs=[vm] * 7,
            out_specs=[any_spec] * 15,
            scratch_shapes=[DMA((15,)), pltpu.SMEM((S,), F32), V((2, LW), F32)] + [V((D,), F32)] * 5 + [V((FW,), F32), V((D,), F32)],
            compiler_params=pltpu.CompilerParams(vmem_limit_bytes=16 * 2**20),
            name="finish",
        )(vout, out, tg, *grads)
    )
    return (
        out, loss, token_grad, g_ln1g, g_ln1b, g_wqkv.transpose(1, 0, 2), g_bqv, g_wproj, g_bproj, g_ln2g, g_ln2b,
        g_wfc1, g_bfc1, g_wfc2, g_bfc2,
    )


def solution(mesh):
    tp = P("tensor")
    in_specs = (
        P("dp", None), P(), P("dp", None), P("dp", None), P(), P(), P(None, None, "tensor"),
        P(None, "tensor"), P("tensor", None), P(), P(), P(), P(None, "tensor"), tp, P("tensor", None), P(),
    )
    out_specs = (
        P("dp", None), P("dp"), P("dp", None), P(), P(), P("dp", None, "tensor"), P(None, "tensor"),
        P("tensor", "dp"), P(), P(), P(), P("dp", "tensor"), tp, P("tensor", "dp"), P(),
    )
    return jax.shard_map(
        functools.partial(body, mesh.shape["dp"]), mesh=mesh, in_specs=in_specs, out_specs=out_specs,
        check_vma=False,
    )
```

```python
import functools

import jax
import jax.numpy as jnp
from jax import lax
from jax.experimental import pallas as pl
from jax.experimental.pallas import tpu as pltpu
from jax.sharding import PartitionSpec as P

D = 1024
H = 16
HEAD = D // H
BUFFER = 64
SLOTS = 320
HALF = D // 2
RB = 32
EPS = 1e-06
F32 = jnp.float32
BF16 = jnp.bfloat16
MESH = pl.DeviceIdType.MESH
NT = (((1,), (1,)), ((), ()))
TN = (((0,), (0,)), ((), ()))
NN = (((1,), (0,)), ((), ()))
INV_SQRT2 = 0.7071067811865476
INV_SQRT_2PI = 0.3989422804014327


def mm(a, b, dims):
    return lax.dot_general(a, b, dims, preferred_element_type=F32)


def fold8(x):
    return jnp.sum(x.reshape(x.shape[0] // 8, 8, x.shape[1]), axis=0)


def kernel(
    cfg,
    kept_in, ln1g_in, ln1b_in, bproj_in, ln2g_in, ln2b_in, bfc1_in, bfc2_in, bqv_in,
    tok_in, tea_in, og_in, wqkv_in, wproj_in, wfc1_in, wfc2_in,
    tea, seed_r, vout_ref, gfc2_r, gfc1_r, gproj_r, gqkv_r,
    wqkv, wproj, wfc1, wfc2, tok, og,
    a_r, qkv_r, heads_r, c_r, h1_r, act_r, gp_r, sl_r, dpre_r, dqkv_r,
    core_s, core_r, tot, gs, rb, vec_ref, lacc, loss_r, vacc, vst, vrc,
    v1_ln1g, v1_ln1b, v1_bproj, v1_ln2g, v1_ln2b, v1_bfc1, v1_bfc2, v1_bqv, kept_ref, in_sem, ps_s, ps_r, px_r, g_s, g_r, v_s, v_r,
):
    S, NDP, NBITS, CH, FW = cfg
    LW = wproj.shape[0]
    R = SLOTS
    rows_all = S * R
    dp = lax.axis_index("dp")
    t = lax.axis_index("tensor")
    lo = lax.rem(t, 2)
    hi = t // 2
    sib = (dp, hi * 2 + (1 - lo))
    xn = (dp, (1 - hi) * 2 + lo)
    bits = [lax.rem(dp // (1 << b), 2) for b in range(NBITS)]

    def flip(b):
        return (dp + (1 << b) * (1 - 2 * bits[b]), t)

    def in_copy(i, src, dst):
        return pltpu.make_async_copy(src, dst, in_sem.at[i])

    def tok_copy(s):
        rows = pl.ds(pl.multiple_of(s * R, 64), R)
        return pltpu.make_async_copy(tok_in.at[rows, :], tok.at[rows, :], in_sem.at[15 + s])

    ins = [
        in_copy(0, wqkv_in, wqkv),
        in_copy(1, wproj_in, wproj),
        in_copy(2, wfc1_in, wfc1),
        in_copy(3, wfc2_in, wfc2),
        in_copy(4, tea_in, tea),
        in_copy(5, og_in, og),
    ]
    v1 = [v1_ln1g, v1_ln1b, v1_bproj, v1_ln2g, v1_ln2b, v1_bfc1, v1_bfc2]
    small = [
        in_copy(6 + i, src, dst)
        for i, (src, dst) in enumerate(zip([ln1g_in, ln1b_in, bproj_in, ln2g_in, ln2b_in, bfc1_in, bfc2_in], v1))
    ]
    bqv_copy, kept_copy = in_copy(13, bqv_in, v1_bqv), in_copy(14, kept_in, kept_ref)
    tok_copy(0).start()
    kept_copy.start()
    small[0].start()
    small[1].start()
    bqv_copy.start()
    ins[0].start()
    ins[1].start()
    for c in small[2:]:
        c.start()

    bar = pltpu.get_barrier_semaphore()
    for peer in [sib, xn] + [flip(b) for b in range(NBITS)]:
        pl.semaphore_signal(bar, inc=1, device_id=peer, device_id_type=MESH)

    vacc[...] = jnp.zeros_like(vacc)
    vec_ref[7:8, :] = jnp.zeros((1, D), F32)

    def vec_rows(first, last):
        for j in range(first, last):
            small[j].wait()
            vec_ref[j:j + 1, :] = v1[j][...].astype(F32).reshape(1, v1[j].shape[0])

    vec_rows(0, 2)
    bqv_copy.wait()
    bqv = v1_bqv[...].astype(F32)
    vec_ref[7:8, 0:LW] = bqv[0:1]
    vec_ref[7:8, 2 * LW:3 * LW] = bqv[1:2]
    kept_copy.wait()

    def length(s):
        return kept_ref[dp * S + s] + BUFFER

    def mask_rows(s, i):
        idx = lax.broadcasted_iota(jnp.int32, (RB, 1), 0) + i * RB
        return (idx < length(s)).astype(F32)

    def seq_rows(s):
        return pl.ds(pl.multiple_of(s * R, 64), R)

    def chunks(fn, init=0):
        return lax.fori_loop(0, R // RB, fn, init, unroll=10)

    def blk(s, i):
        return pl.ds(pl.multiple_of(s * R + i * RB, RB), RB)

    def loc(i):
        return pl.ds(pl.multiple_of(i * RB, RB), RB)

    def norm_stats(x):
        mean = jnp.mean(x, axis=-1, keepdims=True)
        off = x - mean
        var = jnp.mean(off * off, axis=-1, keepdims=True)
        r = lax.rsqrt(var + EPS)
        return off * r, r

    def cp(p, s, kind, src, dst, dev):
        return pltpu.make_async_remote_copy(
            src_ref=src, dst_ref=dst,
            send_sem=ps_s.at[s, kind], recv_sem=px_r.at[p, s] if kind == 1 else ps_r.at[s, kind // 2 + kind // 3],
            device_id=dev, device_id_type=MESH,
        )

    def cp_core(p, s):
        return cp(p, s, 0, core_s.at[s], core_r.at[s], sib)

    def cp_x(p, s):
        ref = tot.at[p, s, lo, hi]
        return cp(p, s, 1, ref, ref, xn)

    def cp_f1(p, s):
        ref = tot.at[p, s, lo, hi]
        return cp(p, s, 2, ref, ref, sib)

    def cp_f2(p, s):
        ref = tot.at[p, s, lo, 1 - hi]
        return cp(p, s, 3, ref, ref, sib)

    def ps_start(p, s, part):
        core_s[s] = part(1 - lo).astype(BF16)
        cp_core(p, s).start()
        own = part(lo).astype(BF16).astype(F32)
        cp_core(p, s).wait_recv()
        tot[p, s, lo, hi] = (own + core_r[s].astype(F32)).astype(BF16)
        cp_x(p, s).start()
        cp_f1(p, s).start()

    def ps_forward(p, s):
        cp_core(p, s).wait_send()
        cp_x(p, s).wait()
        cp_f2(p, s).start()

    def ps_finish(p, s):
        cp_f1(p, s).wait()
        cp_f2(p, s).wait()

    def ps_total(p, s, i):
        rr = loc(i)
        parts = [
            tot[p, s, h, 0, rr, :].astype(F32) + tot[p, s, h, 1, rr, :].astype(F32) for h in range(2)
        ]
        return jnp.concatenate(parts, axis=1)

    def half_cols(h):
        return pl.ds(pl.multiple_of(h * HALF, HALF), HALF)

    lane_half = lax.broadcasted_iota(jnp.int32, (1, 2 * HEAD), 1) // HEAD

    def head_mask(hh, scale=1.0):
        return ((lane_half == hh).astype(F32) * scale).astype(BF16)

    SCALE = HEAD ** -0.5

    def pair_cols(c, hp):
        return pl.ds(pl.multiple_of(c * LW + hp * 2 * HEAD, 2 * HEAD), 2 * HEAD)

    def probs_of(qm, k, s):
        sc = mm(qm, k, NT)
        col = lax.broadcasted_iota(jnp.int32, (1, R), 1)
        sc = jnp.where(col < length(s), sc, -1e30)
        top = jnp.max(sc, axis=-1, keepdims=True)
        e = jnp.exp(sc - top)
        return e * (1.0 / jnp.sum(e, axis=-1, keepdims=True))

    npair = LW // (2 * HEAD)

    def swapped(tile):
        if isinstance(tile, int):
            return int(tile in (1, 3))
        return lax.rem(tile, 2) * ((T - tile) // (T - 3))

    def mix(f, p, q):
        return p + f * (q - p)

    def place(d, f):
        db = [(d >> b) & 1 for b in range(NBITS)]
        pos = sum(db[b] << (NBITS - 1 - b) for b in range(2, NBITS))
        if NBITS > 1:
            return pos + mix(f, db[0], db[1]) * (NDP // 2) + mix(f, db[1], db[0]) * (NDP // 4)
        return db[0]

    def stage_bit(f, j):
        if NBITS > 1 and j < 2:
            return mix(f, bits[j], bits[1 - j])
        return bits[j]

    def stage_peer(f, j):
        if NBITS > 1 and j < 2:
            step = [(1 << b) * (1 - 2 * bits[b]) for b in range(2)]
            return (dp + mix(f, step[j], step[1 - j]), t)
        return flip(j)

    def base(f, j):
        return sum((stage_bit(f, i) * (NDP >> (i + 1)) for i in range(j)), 0)

    def land(j):
        return NDP - (NDP >> j)

    def room(tile):
        if isinstance(tile, int) and tile >= T - 1:
            return T - 1, slice((tile - T + 1) * 128, (tile - T + 2) * 128)
        return tile, slice(0, 256)

    def cp_g(tile, j):
        f = swapped(tile)
        at, cols = room(tile)
        n = NDP >> (j + 1)
        first = base(f, j) + (1 - stage_bit(f, j)) * n
        return pltpu.make_async_remote_copy(
            src_ref=gs.at[at, pl.ds(first, n), :, cols], dst_ref=rb.at[at, land(j):land(j) + n, :, cols],
            send_sem=g_s.at[tile], recv_sem=g_r.at[tile, j],
            device_id=stage_peer(f, j), device_id_type=MESH,
        )

    def grad_tile(tile, lhs, rhs):
        f = swapped(tile)
        val = mm(lhs[...], rhs, TN).astype(BF16)
        for d in range(NDP):
            gs[tile, place(d, f)] = val[d * CH:(d + 1) * CH]
        if isinstance(tile, int):
            cp_g(tile, 0).start()
            return

        @pl.when(tile < T - 1)
        def _():
            cp_g(tile, 0).start()

        @pl.when(tile == T - 1)
        def _():
            cp_g(T - 1, 0).start()
            cp_g(T, 0).start()

    def grad_tiles(first, last, lhs, rhs, skip=0):
        def one(k, _):
            grad_tile(k, lhs, rhs[:, pl.ds(pl.multiple_of((k - skip) * 256, 256), 256)])
            return 0

        lax.fori_loop(first, last, one, 0)

    def advance(tile, j):
        f = swapped(tile)
        cp_g(tile, j).wait_recv()
        n = NDP >> (j + 1)
        mine = base(f, j + 1)

        at, cols = room(tile)
        if j + 1 < NBITS:
            def add(i, _):
                gs[at, mine + i, :, cols] = gs[at, mine + i, :, cols] + rb[at, land(j) + i, :, cols]
                return 0

            lax.fori_loop(0, n, add, 0)
            cp_g(tile, j).wait_send()
            cp_g(tile, j + 1).start()
            return
        val = gs[at, mine, :, cols].astype(F32) + rb[at, land(j), :, cols].astype(F32)
        if at < NT1:
            gfc2_r[at * 256:(at + 1) * 256, :] = val.T
        elif at < 2 * NT1:
            gfc1_r[:, (at - NT1) * 256:(at - NT1 + 1) * 256] = val
        elif at < 2 * NT1 + NT2:
            gproj_r[(at - 2 * NT1) * 256:(at - 2 * NT1 + 1) * 256, :] = val.T
        else:
            k = at - 2 * NT1 - NT2
            first = (k % NT2) * 256 + cols.start
            gqkv_r[k // NT2, :, first:first + cols.stop - cols.start] = val

    def steps(*pairs):
        for tile, j in pairs:
            for i in range(j, NBITS if j == 2 else j + 1):
                advance(tile, i)

    def steps_at(s, *lists):
        for at, pairs in enumerate(lists):
            if pairs:
                @pl.when(s == at)
                def _():
                    steps(*pairs)

    NT1 = FW // 256
    NT2 = LW // 256
    T = 2 * NT1 + 4 * NT2

    def phase_a(s, _):
        tok_copy(s).wait()

        def ln(i, _):
            x = tok[blk(s, i), :].astype(F32) * mask_rows(s, i)
            hat, _r = norm_stats(x)
            a_r[blk(s, i), :] = (hat * vec_ref[0:1, :] + vec_ref[1:2, :]).astype(BF16)
            return 0

        chunks(ln)

        @pl.when(s == 0)
        def _():
            ins[0].wait()

            def tok_start(i, _):
                tok_copy(i).start()
                return 0

            lax.fori_loop(1, S, tok_start, 0)

        rs = seq_rows(s)
        av = a_r[rs, :]
        for c in range(3):
            cs = slice(c * LW, (c + 1) * LW)
            qkv_r[rs, cs] = (mm(av, wqkv[c], NN) + vec_ref[7:8, cs]).astype(BF16)

        def pair(hp, _):
            q = qkv_r[rs, pair_cols(0, hp)]
            k = qkv_r[rs, pair_cols(1, hp)]
            v = qkv_r[rs, pair_cols(2, hp)]
            o = None
            for hh in range(2):
                pr = probs_of(q * head_mask(hh, SCALE), k, s).astype(BF16)
                oh = mm(pr, v * head_mask(hh), NN)
                o = oh if o is None else o + oh
            heads_r[rs, pair_cols(0, hp)] = o.astype(BF16)
            return 0

        lax.fori_loop(0, npair, pair, 0)
        hv = heads_r[rs, :]

        @pl.when(s == 0)
        def _():
            ins[1].wait()
            pl.semaphore_wait(bar, 2 + NBITS)

        ps_start(0, s, lambda h: mm(hv, wproj[:, half_cols(h)], NN))

        @pl.when(s == 0)
        def _():
            for c in ins[2:]:
                c.start()

        return 0

    lax.fori_loop(0, S, phase_a, 0)

    ps_forward(0, 0)

    vec_rows(2, 7)
    count = lax.fori_loop(
        0, kept_ref.shape[0], lambda i, acc: acc + (kept_ref[i] + BUFFER).astype(F32), jnp.float32(0.0)
    )

    ins[2].wait()
    ins[3].wait()

    def phase_b(s, _):
        ps_finish(0, s)

        def ln(i, _):
            x = tok[blk(s, i), :].astype(F32) * mask_rows(s, i)
            h1 = x + ps_total(0, s, i) + vec_ref[2:3, :]
            h1_r[blk(s, i), :] = h1
            hat, _r = norm_stats(h1)
            c_r[blk(s, i), :] = (hat * vec_ref[3:4, :] + vec_ref[4:5, :]).astype(BF16)
            return 0

        chunks(ln)
        rs = seq_rows(s)
        cv = c_r[rs, :]

        def fc1(j, _):
            cs = pl.ds(pl.multiple_of(j * 256, 256), 256)
            pre = mm(cv, wfc1[:, cs], NN) + vec_ref[5:6, cs]
            phi = 0.5 * (1.0 + lax.erf(pre * INV_SQRT2))
            act_r[rs, cs] = (pre * phi).astype(BF16)
            gp_r[rs, cs] = phi + pre * (INV_SQRT_2PI * jnp.exp(-0.5 * pre * pre))
            return 0

        lax.fori_loop(0, FW // 256, fc1, 0)
        @pl.when(s + 1 < S)
        def _():
            ps_forward(0, s + 1)

        @pl.when(s + 1 == S)
        def _():
            ps_forward(1, 0)

        ps_start(1, s, lambda h: mm(act_r[rs, :], wfc2[:, half_cols(h)], NN))
        return 0

    lax.fori_loop(0, S, phase_b, 0)

    ins[4].wait()
    ins[5].wait()
    loss_scale = kept_ref.shape[0] / (2.0 * count * D)
    seed_scale = kept_ref.shape[0] * SLOTS * 1.0 / count

    loss_r[...] = jnp.zeros_like(loss_r)

    def phase_c(s, _):
        lacc[...] = jnp.zeros_like(lacc)

        def fin(h):
            hc = half_cols(h)

            def one(i, _):
                m = mask_rows(s, i)
                mlp = tot[1, s, h, 0, loc(i), :].astype(F32) + tot[1, s, h, 1, loc(i), :].astype(F32)
                final = (h1_r[blk(s, i), hc] + mlp + vec_ref[6:7, hc]) * m
                diff = (final - tea[blk(s, i), hc].astype(F32)) * m
                seed = (og[blk(s, i), hc].astype(F32) + diff * seed_scale) * m
                tea[blk(s, i), hc] = final.astype(BF16)
                seed_r[blk(s, i), hc] = seed
                sl_r[blk(s, i), hc] = seed.astype(BF16)
                lacc[...] += fold8(diff * diff)
                vacc[6, :, hc] += fold8(seed)
                return 0

            chunks(one)

        fin(lo)
        ps_finish(1, s)
        fin(1 - lo)
        here = (lax.broadcasted_iota(jnp.int32, (1, D), 1) == s).astype(F32)
        loss_r[...] += here * (jnp.sum(lacc[...]) * loss_scale)
        rs = seq_rows(s)
        sv = sl_r[rs, :]

        @pl.when(s == S - 1)
        def _():
            grad_tiles(0, 2, sl_r, act_r)


        def dact(j, _):
            cs = pl.ds(pl.multiple_of(j * 256, 256), 256)
            d = mm(sv, wfc2[cs, :], NT) * gp_r[rs, cs]
            dl = d.astype(BF16)
            dpre_r[rs, cs] = dl
            vacc[5, :, cs] += fold8(dl.astype(F32))
            return 0

        lax.fori_loop(0, FW // 256, dact, 0)
        ps_start(0, s, lambda h: mm(dpre_r[rs, :], wfc1[half_cols(h), :], NT))

        @pl.when(s + 1 < S)
        def _():
            ps_forward(1, s + 1)

        return 0

    lax.fori_loop(0, S, phase_c, 0)

    grad_tiles(2, 4, sl_r, act_r)
    grad_tiles(4, 5, c_r, dpre_r, 4)
    ps_forward(0, 0)

    def phase_d(s, _):
        ps_finish(0, s)

        def lnb(i, _):
            hat, r = norm_stats(h1_r[blk(s, i), :])
            dy = ps_total(0, s, i)
            vacc[3] += fold8(dy * hat)
            vacc[4] += fold8(dy)
            dg = dy * vec_ref[3:4, :]
            m1 = jnp.mean(dg, axis=-1, keepdims=True)
            m2 = jnp.mean(dg * hat, axis=-1, keepdims=True)
            dh1 = seed_r[blk(s, i), :] + r * (dg - m1 - hat * m2)
            seed_r[blk(s, i), :] = dh1
            vacc[2] += fold8(dh1)
            sl_r[blk(s, i), :] = dh1.astype(BF16)
            return 0

        chunks(lnb)
        rs = seq_rows(s)

        def pair(hp, _):
            wc = pl.ds(pl.multiple_of(hp * 2 * HEAD, 2 * HEAD), 2 * HEAD)
            dh = mm(sl_r[rs, :], wproj[wc, :], NT).astype(BF16)
            q = qkv_r[rs, pair_cols(0, hp)]
            k = qkv_r[rs, pair_cols(1, hp)]
            v = qkv_r[rs, pair_cols(2, hp)]
            dq = dk = dv = None
            for hh in range(2):
                hm = head_mask(hh)
                qm, km, dm = q * head_mask(hh, SCALE), k * hm, dh * hm
                pr = probs_of(qm, k, s)
                dpr = mm(dm, v, NT)
                ds = (pr * (dpr - jnp.sum(pr * dpr, axis=-1, keepdims=True))).astype(BF16)
                q1, k1, v1 = mm(ds, km, NN), mm(ds, qm, TN), mm(pr.astype(BF16), dm, TN)
                if dq is None:
                    dq, dk, dv = q1, k1, v1
                else:
                    dq, dk, dv = dq + q1, dk + k1, dv + v1
            dql = (dq * SCALE).astype(BF16)
            dvl = dv.astype(BF16)
            dqkv_r[rs, pair_cols(0, hp)] = dql
            dqkv_r[rs, pair_cols(1, hp)] = dk.astype(BF16)
            dqkv_r[rs, pair_cols(2, hp)] = dvl
            vacc[7, :, pair_cols(0, hp)] += fold8(dql.astype(F32))
            vacc[7, :, pair_cols(1, hp)] += fold8(dvl.astype(F32))
            return 0

        steps_at(
            s,
            [(0, 0)],
            [(0, 1), (4, 0)],
            [(5, 0), (4, 1)],
        )
        lax.fori_loop(0, npair, pair, 0, unroll=True)
        steps_at(
            s,
            [(2, 0)],
            [(3, 0), (2, 1)],
            [(6, 0), (5, 1)],
        )
        @pl.when(s + 1 < S)
        def _():
            ps_forward(0, s + 1)

        @pl.when(s + 1 == S)
        def _():
            ps_forward(1, 0)

        ps_start(1, s, lambda h: sum(
            mm(dqkv_r[rs, c * LW:(c + 1) * LW], wqkv[c, half_cols(h), :], NT) for c in range(3)
        ))

        @pl.when(s == 0)
        def _():
            grad_tiles(5, 8, c_r, dpre_r, 4)

        return 0

    lax.fori_loop(0, S, phase_d, 0)
    grad_tile(8, sl_r, heads_r[...])

    def attn_tile(k, _):
        grad_tile(k, a_r, dqkv_r[:, pl.ds(pl.multiple_of((k - 9) * 256, 256), 256)])

        @pl.when(k == 9)
        def _():
            steps((7, 0))

        return 0

    lax.fori_loop(9, 12, attn_tile, 0)
    steps((1, 0), (6, 1))

    def phase_e(s, _):
        ps_finish(1, s)

        def lnb(i, _):
            m = mask_rows(s, i)
            hat, r = norm_stats(tok[blk(s, i), :].astype(F32) * m)
            dy = ps_total(1, s, i)
            vacc[0] += fold8(dy * hat)
            vacc[1] += fold8(dy)
            dg = dy * vec_ref[0:1, :]
            m1 = jnp.mean(dg, axis=-1, keepdims=True)
            m2 = jnp.mean(dg * hat, axis=-1, keepdims=True)
            seed_r[blk(s, i), :] = (seed_r[blk(s, i), :] + r * (dg - m1 - hat * m2)) * m
            return 0

        chunks(lnb)

        @pl.when(s + 1 < S)
        def _():
            ps_forward(1, s + 1)

        steps_at(
            s,
            [(0, 2), (3, 1)],
            [(2, 2), (7, 1)],
            [],
        )
        return 0

    lax.fori_loop(0, S, phase_e, 0)

    for j in range(8):
        vst[0, j:j + 1, :] = jnp.sum(vacc[j], axis=0, keepdims=True)

    def cp_v(j):
        return pltpu.make_async_remote_copy(
            src_ref=vst.at[j], dst_ref=vrc.at[j], send_sem=v_s.at[j], recv_sem=v_r.at[j],
            device_id=flip((j + 1) % NBITS), device_id_type=MESH,
        )

    def step_v(j):
        cp_v(j).wait()
        total = vst[j] + vrc[j]
        if j + 1 < NBITS:
            vst[j + 1] = total
            cp_v(j + 1).start()
        else:
            vout_ref[0:8, :] = total
            vout_ref[8:9, :] = loss_r[...]

    cp_v(0).start()
    steps((8, 0), (4, 2), (5, 2), (9, 0), (8, 1))
    step_v(0)
    steps((6, 2), (10, 0), (9, 1), (3, 2), (7, 2), (11, 0), (10, 1), (12, 0))
    for j in range(1, NBITS - 1):
        step_v(j)
    steps((11, 1), (8, 2), (1, 1), (12, 1))
    step_v(NBITS - 1)
    steps((9, 2), (10, 2), (11, 2), (1, 2), (12, 2))

    def drain(tile, _):
        cp_g(tile, NBITS - 1).wait_send()
        return 0

    lax.fori_loop(0, T - 1, drain, 0)
    drain(T - 1, 0)
    drain(T, 0)


def finish(v_in, *refs):
    ins, refs = refs[:6], refs[6:]
    loss_o, ln1g_o, ln1b_o, bqv_o, bproj_o, ln2g_o, ln2b_o, bfc1_o, bfc2_o = refs[:9]
    outs, sem, mids = refs[9:15], refs[15], refs[16:]
    moves = [pltpu.make_async_copy(src, dst, sem.at[i]) for i, (src, dst) in enumerate(zip(ins, outs))]
    for c in moves:
        c.start()
    loss_s, bqv_s, mids = mids[0], mids[1], mids[2:]
    for i in range(loss_o.shape[0]):
        loss_s[i] = v_in[8, i]
    for j, (mid, ref) in enumerate(zip(mids, [ln1g_o, ln1b_o, bproj_o, ln2g_o, ln2b_o, bfc1_o, bfc2_o])):
        mid[...] = v_in[j]
        moves.append(pltpu.make_async_copy(mid, ref, sem.at[6 + j]))
        moves[-1].start()
    lw = bqv_o.shape[1]
    bqv_s[0:1, :] = v_in[7:8, 0:lw]
    bqv_s[1:2, :] = v_in[7:8, lw:2 * lw]
    for j, (mid, ref) in enumerate(((loss_s, loss_o), (bqv_s, bqv_o))):
        moves.append(pltpu.make_async_copy(mid, ref, sem.at[13 + j]))
        moves[-1].start()
    for c in moves:
        c.wait()


def body(
    n_dp,
    tokens, kept, teacher, out_grad, ln1_gain, ln1_bias, w_qkv, bias_qv, w_proj, bias_proj,
    ln2_gain, ln2_bias, w_fc1, bias_fc1, w_fc2, bias_fc2,
):
    rows = tokens.shape[0]
    S = rows // SLOTS
    LW = w_qkv.shape[2]
    FW = w_fc1.shape[1]
    CH = D // n_dp
    NBITS = n_dp.bit_length() - 1
    T = (2 * FW + 4 * LW) // 256
    cfg = (S, n_dp, NBITS, CH, FW)
    any_spec = pl.BlockSpec(memory_space=pl.ANY)
    vm = pl.BlockSpec(memory_space=pltpu.VMEM)
    sm = pl.BlockSpec(memory_space=pltpu.SMEM)
    sds = jax.ShapeDtypeStruct
    DMA = pltpu.SemaphoreType.DMA
    V = pltpu.VMEM
    big = [
        ((rows, D), BF16), ((rows, D), F32), ((FW, CH), F32), ((CH, FW), F32), ((LW, CH), F32), ((3, CH, LW), F32),
    ]
    out, tg, vout, *grads = pl.pallas_call(
        functools.partial(kernel, cfg),
        out_shape=[V(*big[0]), V(*big[1]), V((16, D), F32)] + [V(*b) for b in big[2:]],
        in_specs=[any_spec] * 16,
        out_specs=[vm] * 7,
        scratch_shapes=[
            V((3, D, LW), BF16), V((LW, D), BF16), V((D, FW), BF16), V((FW, D), BF16),
            V((rows, D), BF16), V((rows, D), BF16),
            V((rows, D), BF16), V((rows, 3 * LW), BF16), V((rows, LW), BF16), V((rows, D), BF16),
            V((rows, D), F32), V((rows, FW), BF16), V((rows, FW), F32),
            V((rows, D), BF16), V((rows, FW), BF16), V((rows, 3 * LW), BF16),
            V((S, SLOTS, HALF), BF16), V((S, SLOTS, HALF), BF16), V((2, S, 2, 2, SLOTS, HALF), BF16),
            V((T, n_dp, CH, 256), BF16), V((T, n_dp - 1, CH, 256), BF16),
            V((8, D), F32), V((8, HALF), F32), V((1, D), F32), V((8, 8, D), F32), V((NBITS, 8, D), F32), V((NBITS, 8, D), F32),
            V((D,), BF16), V((D,), BF16), V((D,), BF16), V((D,), BF16), V((D,), BF16), V((FW,), BF16), V((D,), BF16),
            V((2, LW), BF16), pltpu.SMEM((kept.shape[0],), jnp.int32), DMA((15 + S,)), DMA((S, 4)), DMA((S, 3)), DMA((2, S)), DMA((T + 1,)), DMA((T + 1, NBITS)),
            DMA((NBITS,)), DMA((NBITS,)),
        ],
        compiler_params=pltpu.CompilerParams(
            collective_id=0, has_side_effects=True, vmem_limit_bytes=56 * 2**20
        ),
        name="layer",
    )(
        kept, ln1_gain, ln1_bias, bias_proj, ln2_gain, ln2_bias, bias_fc1, bias_fc2, bias_qv,
        tokens, teacher, out_grad, w_qkv.transpose(1, 0, 2), w_proj, w_fc1, w_fc2,
    )
    vd = sds((D,), F32)
    loss, g_ln1g, g_ln1b, g_bqv, g_bproj, g_ln2g, g_ln2b, g_bfc1, g_bfc2, out, token_grad, g_wfc2, g_wfc1, g_wproj, g_wqkv = (
        pl.pallas_call(
            finish,
            out_shape=[sds((S,), F32), vd, vd, sds((2, LW), F32), vd, vd, vd, sds((FW,), F32), vd]
            + [sds(*b) for b in big],
            in_specs=[vm] * 7,
            out_specs=[any_spec] * 15,
            scratch_shapes=[DMA((15,)), pltpu.SMEM((S,), F32), V((2, LW), F32)] + [V((D,), F32)] * 5 + [V((FW,), F32), V((D,), F32)],
            compiler_params=pltpu.CompilerParams(vmem_limit_bytes=16 * 2**20),
            name="finish",
        )(vout, out, tg, *grads)
    )
    return (
        out, loss, token_grad, g_ln1g, g_ln1b, g_wqkv.transpose(1, 0, 2), g_bqv, g_wproj, g_bproj, g_ln2g, g_ln2b,
        g_wfc1, g_bfc1, g_wfc2, g_bfc2,
    )


def solution(mesh):
    tp = P("tensor")
    in_specs = (
        P("dp", None), P(), P("dp", None), P("dp", None), P(), P(), P(None, None, "tensor"),
        P(None, "tensor"), P("tensor", None), P(), P(), P(), P(None, "tensor"), tp, P("tensor", None), P(),
    )
    out_specs = (
        P("dp", None), P("dp"), P("dp", None), P(), P(), P("dp", None, "tensor"), P(None, "tensor"),
        P("tensor", "dp"), P(), P(), P(), P("dp", "tensor"), tp, P("tensor", "dp"), P(),
    )
    return jax.shard_map(
        functools.partial(body, mesh.shape["dp"]), mesh=mesh, in_specs=in_specs, out_specs=out_specs,
        check_vma=False,
    )
```
